32 devices in a mesh: dp: 8 (over y, x, core), seq: 4 (over z).
Axes of the slice: x: 2, y: 2, z: 4, core: 2. Of those that a mesh axis runs over, the one named last changes fastest.
Arguments:
- hidden_in: bfloat16 [8, 1024, 2048], P('dp', 'seq'), may hold values from -6 to 6
- q_weight: bfloat16 [2048, 2048], P(('dp', 'seq')), may hold values from -0.125 to 0.125
- k_weight: bfloat16 [2048, 2048], P(('dp', 'seq')), may hold values from -0.125 to 0.125
- v_weight: bfloat16 [2048, 2048], P(('dp', 'seq')), may hold values from -0.125 to 0.125
- o_weight: bfloat16 [2048, 2048], P(('dp', 'seq')), may hold values from -0.125 to 0.125
- q_gain: bfloat16 [2048], P(('dp', 'seq')), may hold values from 0.099609375 to 1.8984375
- k_gain: bfloat16 [2048], P(('dp', 'seq')), may hold values from 0.099609375 to 1.8984375
- attn_gain: bfloat16 [2048], P(('dp', 'seq')), may hold values from 0.099609375 to 1.8984375
- gate_weight: bfloat16 [2048, 8192], P(('dp', 'seq')), may hold values from -0.125 to 0.125
- up_weight: bfloat16 [2048, 8192], P(('dp', 'seq')), may hold values from -0.125 to 0.125
- down_weight: bfloat16 [8192, 2048], P(('dp', 'seq')), may hold values from -0.0625 to 0.0625
- mlp_gain: bfloat16 [2048], P(('dp', 'seq')), may hold values from 0.099609375 to 1.8984375
- out_grad: bfloat16 [8, 1024, 2048], P('dp', 'seq'), may hold values from -6 to 6
Outputs:
- layer_out: bfloat16 [8, 1024, 2048], P('dp', 'seq')
- in_grad: bfloat16 [8, 1024, 2048], P('dp', 'seq')
- q_weight_grad: float32 [2048, 2048], P(('dp', 'seq'))
- k_weight_grad: float32 [2048, 2048], P(('dp', 'seq'))
- v_weight_grad: float32 [2048, 2048], P(('dp', 'seq'))
- o_weight_grad: float32 [2048, 2048], P(('dp', 'seq'))
- gate_weight_grad: float32 [2048, 8192], P(('dp', 'seq'))
- up_weight_grad: float32 [2048, 8192], P(('dp', 'seq'))
- down_weight_grad: float32 [8192, 2048], P(('dp', 'seq'))
- q_gain_grad: float32 [2048], P(('dp', 'seq'))
- k_gain_grad: float32 [2048], P(('dp', 'seq'))
- attn_gain_grad: float32 [2048], P(('dp', 'seq'))
- mlp_gain_grad: float32 [2048], P(('dp', 'seq'))
The draws below stay inside these ranges and needn't reach their ends.
All inputs are finite; a program needn't handle non-finite values.
Results may differ from the reference program's by a relative error of at most 0.02.
Values may be sent and summed in bfloat16 or wider, within the bound.
No kernel may reach another device: no remote copies, remote signals or barrier semaphores. Data moves between devices by JAX's collectives and lax.ppermute only.
A program may use at most 512 MiB of HBM per device.

```python
import math
import jax
import jax.numpy as jnp
from jax import lax

D = 2048
HEADS = 16
FF = 8192
SEQ_LEN = 1024
SEQS = 8


def levels(key, extent, shards, least, high):
    gain = 1.0
    for dim, parts in shards:
        draws = jax.random.uniform(jax.random.fold_in(jax.random.fold_in(key, 6), dim), (parts,), jnp.float32, least / len(shards), high / len(shards))
        gain = gain * jnp.repeat(jnp.exp(draws), extent[dim] // parts).reshape((-1,) + (1,) * (len(extent) - 1 - dim))
    return gain


def centred(own_key, shape, spread, most, shards=(), kind=jnp.bfloat16):
    values = spread * jax.random.normal(own_key, shape, jnp.float32)
    if shards:
        values = values * levels(own_key, shape, shards, -0.22, 0.18)
    return jnp.clip(values, -most, most).astype(kind)


def setup_inputs(seed: int = 0) -> dict:
    key_list = jax.random.split(jax.random.key(seed), 14)
    return {
        "hidden_in": centred(key_list[0], (SEQS, SEQ_LEN, D), 1.0, 6.0, ((0, 8), (1, 4))),
        "q_weight": centred(key_list[1], (D, D), D ** -0.5, 0.125, ((0, 32),)),
        "k_weight": centred(key_list[2], (D, D), D ** -0.5, 0.125, ((0, 32),)),
        "v_weight": centred(key_list[3], (D, D), D ** -0.5, 0.125, ((0, 32),)),
        "o_weight": centred(key_list[4], (D, D), D ** -0.5, 0.125, ((0, 32),)),
        "q_gain": jnp.clip(1.0 + 0.18 * jax.random.normal(key_list[5], (D,), jnp.float32), 0.099609375, 1.8984375).astype(jnp.bfloat16),
        "k_gain": jnp.clip(1.0 + 0.18 * jax.random.normal(key_list[6], (D,), jnp.float32), 0.099609375, 1.8984375).astype(jnp.bfloat16),
        "attn_gain": jnp.clip(1.0 + 0.18 * jax.random.normal(key_list[7], (D,), jnp.float32), 0.099609375, 1.8984375).astype(jnp.bfloat16),
        "gate_weight": centred(key_list[8], (D, FF), D ** -0.5, 0.125, ((0, 32),)),
        "up_weight": centred(key_list[9], (D, FF), D ** -0.5, 0.125, ((0, 32),)),
        "down_weight": centred(key_list[10], (FF, D), FF ** -0.5, 0.0625, ((0, 32),)),
        "mlp_gain": jnp.clip(1.0 + 0.18 * jax.random.normal(key_list[11], (D,), jnp.float32), 0.099609375, 1.8984375).astype(jnp.bfloat16),
        "out_grad": centred(key_list[12], (SEQS, SEQ_LEN, D), 1.0, 6.0, ((0, 8), (1, 4))),
    }


EPSILON = 1e-06
ROPE_THETA = 500000.0

@jax.custom_vjp
def low(v):
    return lax.optimization_barrier(v.astype(jnp.bfloat16)).astype(jnp.float32)

@jax.custom_vjp
def low_back(v):
    return v

def low_keep(v):
    return (low(v), None)

def low_pass(kept, grad):
    return (grad,)

def back_keep(v):
    return (v, None)

def back_low(kept, grad):
    return (low(grad),)
low.defvjp(low_keep, low_pass)
low_back.defvjp(back_keep, back_low)

def dense_dot(left_side, right_side):
    return jnp.einsum('...k,kn->...n', left_side, right_side, precision=lax.Precision.HIGHEST)

def rms_scale(tensor, gain_vec):
    return tensor * lax.rsqrt(lax.optimization_barrier(jnp.mean(tensor * tensor, axis=-1, keepdims=True)) + EPSILON) * gain_vec

def rope_tables(offset, length, head_dim):
    half_dim = head_dim // 2
    inverse = jnp.power(jnp.float32(ROPE_THETA), -(jnp.arange(half_dim, dtype=jnp.float32) * 2.0 / head_dim))
    places = (offset + jnp.arange(length, dtype=jnp.int32)).astype(jnp.float32)
    angles = places[:, None] * inverse[None, :]
    angles = jnp.concatenate([angles, angles], axis=-1)[:, None, :]
    return (jnp.cos(angles), jnp.sin(angles))

def rotate(tensor, cosine_table, sine_table):
    first, second = jnp.split(tensor, 2, axis=-1)
    turned = jnp.concatenate([-second, first], axis=-1)
    return tensor * cosine_table + turned * sine_table

def layer_block(params, block_in):
    q_full, k_full, v_full, o_full, q_gain_full, k_gain_full, attn_gain_full, gate_full, up_full, down_full, mlp_gain_full = params
    groups, length, model_width = block_in.shape
    head_dim = model_width // HEADS
    head_shape = (groups, length, HEADS, head_dim)
    cosine_table, sine_table = rope_tables(0, length, head_dim)
    q_raw = low_back(dense_dot(block_in, q_full))
    k_raw = low_back(dense_dot(block_in, k_full))
    v_raw = low_back(dense_dot(block_in, v_full))
    queries = low(rotate(rms_scale(q_raw, q_gain_full).reshape(head_shape), cosine_table, sine_table))
    keys_all = low(rotate(rms_scale(k_raw, k_gain_full).reshape(head_shape), cosine_table, sine_table))
    values_all = low(v_raw).reshape(head_shape)
    score_raw = low_back(jnp.einsum('sqhd,skhd->shqk', queries, keys_all, precision=lax.Precision.HIGHEST)) * (1.0 / math.sqrt(head_dim))
    places = jnp.arange(length, dtype=jnp.int32)
    allowed = places[None, :] <= places[:, None]
    masked = jnp.where(allowed, score_raw, -1e+30)
    row_max = lax.optimization_barrier(jnp.max(masked, axis=-1, keepdims=True))
    weights = jnp.exp(masked - row_max)
    probabilities = low(weights / lax.optimization_barrier(jnp.sum(weights, axis=-1, keepdims=True)))
    mixed_heads = low(low_back(jnp.einsum('shqk,skhd->sqhd', probabilities, values_all, precision=lax.Precision.HIGHEST)))
    attn_out = low_back(dense_dot(mixed_heads.reshape(groups, length, model_width), o_full))
    residual = block_in + rms_scale(attn_out, attn_gain_full)
    residual_low = low(residual)
    gate_raw = low_back(dense_dot(residual_low, gate_full))
    up_raw = low_back(dense_dot(residual_low, up_full))
    hidden = low(gate_raw * lax.logistic(gate_raw) * up_raw)
    branch = low_back(dense_dot(hidden, down_full))
    return residual + rms_scale(branch, mlp_gain_full)

def reference(hidden_in, q_weight, k_weight, v_weight, o_weight, q_gain, k_gain, attn_gain, gate_weight, up_weight, down_weight, mlp_gain, out_grad):
    params = tuple((item.astype(jnp.float32) for item in (q_weight, k_weight, v_weight, o_weight, q_gain, k_gain, attn_gain, gate_weight, up_weight, down_weight, mlp_gain)))
    inputs = hidden_in.astype(jnp.float32)
    seq_total = hidden_in.shape[0]
    group_size = 2 if seq_total % 2 == 0 else 1

    def forward(params, inputs):
        blocks = inputs.reshape(seq_total // group_size, group_size, inputs.shape[1], inputs.shape[2])

        def one_block(block_in):
            return layer_block(params, block_in)
        result = lax.map(jax.checkpoint(one_block), blocks)
        return result.reshape(inputs.shape)
    result, pullback = jax.vjp(forward, params, inputs)
    param_grads, input_grad = pullback(out_grad.astype(jnp.float32))
    return (result.astype(jnp.bfloat16), input_grad.astype(jnp.bfloat16), param_grads[0], param_grads[1], param_grads[2], param_grads[3], param_grads[7], param_grads[8], param_grads[9], param_grads[4], param_grads[5], param_grads[6], param_grads[10])
```

```python
import math

import jax
import jax.numpy as jnp
from jax import lax
from jax.sharding import Mesh
from jax.sharding import PartitionSpec as P

HEADS = 16
EPSILON = 1e-06
ROPE_THETA = 500000.0
LOW = jnp.bfloat16
FULL = jnp.float32

AXES = ("g", "e", "x", "c", "h", "l")
SWAP = [(0, 1), (1, 0)]


def matmul(left_side, right_side):
    return lax.dot_general(
        left_side, right_side, (((1,), (0,)), ((), ())), preferred_element_type=FULL
    )


def matmul_back(left_side, right_side):
    return lax.dot_general(
        left_side, right_side, (((1,), (1,)), ((), ())), preferred_element_type=FULL
    )


def outer(left_side, right_side):
    return lax.dot_general(
        left_side, right_side, (((0,), (0,)), ((), ())), preferred_element_type=FULL
    )


def swap(value, axis):
    return lax.ppermute(value, axis, SWAP)


def swap_both(value, first, second):
    return lax.ppermute(value, (first, second), [(i, 3 - i) for i in range(4)])


def transpose_axes(value, first, second):
    return lax.ppermute(value, (first, second), [(0, 0), (1, 2), (2, 1), (3, 3)])


def after(value, *others):
    return lax.optimization_barrier((value,) + others)[0]


def pick(value, places):
    starts = [0] * value.ndim
    sizes = list(value.shape)
    for dim, place in places.items():
        starts[dim] = place
        sizes[dim] = 1
    taken = lax.dynamic_slice(value, starts, sizes)
    return taken.reshape([s for d, s in enumerate(value.shape) if d not in places])


def lay(shape, parts):
    out = jnp.zeros(shape, parts[0][0].dtype)
    for value, starts in parts:
        out = lax.dynamic_update_slice(out, value, starts)
    return out


class Place:
    def __init__(self):
        self.g, self.e, self.x, self.c, self.h, self.l = (lax.axis_index(a) for a in AXES)
        self.groups = lax.axis_size("g")


def tokens_in(at, rows):
    count, width = rows.shape
    halves = rows.reshape(2, count // 2, width)
    other = swap(pick(halves, {0: 1 - at.x}), "x")
    mine = pick(halves, {0: at.x})
    same = at.x == at.h
    kept = jnp.where(same, mine, other)
    got = swap(jnp.where(same, other, mine), "h")
    low_first = at.h == 0
    return jnp.stack([jnp.where(low_first, kept, got), jnp.where(low_first, got, kept)])


def tokens_out(at, blocks):
    kept = pick(blocks, {0: at.h})
    got = swap(pick(blocks, {0: 1 - at.h}), "h")
    same = at.x == at.h
    mine = jnp.where(same, kept, got)
    other = swap(jnp.where(same, got, kept), "x")
    low_first = at.x == 0
    return jnp.concatenate(
        [jnp.where(low_first, mine, other), jnp.where(low_first, other, mine)], axis=0
    )


def gather_tokens(at, blocks):
    two, count, width = blocks.shape
    from_x = swap(blocks, "x")
    from_l = swap(blocks, "l")
    far_0 = swap(from_l[0], "x")
    far_1 = swap(from_x[1], "l")
    cut = (2, 1, 1, count, width)
    one = (1, 1, 1, count, width)
    out = lay(
        (2, 2, 2, count, width),
        [
            (blocks.reshape(cut), (0, at.l, at.x, 0, 0)),
            (from_x.reshape(cut), (0, at.l, 1 - at.x, 0, 0)),
            (from_l.reshape(cut), (0, 1 - at.l, at.x, 0, 0)),
            (far_0.reshape(one), (0, 1 - at.l, 1 - at.x, 0, 0)),
            (far_1.reshape(one), (1, 1 - at.l, 1 - at.x, 0, 0)),
        ],
    )
    return out.reshape(8 * count, width)


def scatter_tokens(at, rows):
    total, width = rows.shape
    parts = rows.reshape(2, 2, 2, total // 8, width)
    far = pick(parts, {1: 1 - at.l, 2: 1 - at.x})
    for_l_0 = swap(far[0], "x")
    for_x_1 = swap(far[1], "l")
    for_l = pick(parts, {1: 1 - at.l, 2: at.x})
    for_x = pick(parts, {1: at.l, 2: 1 - at.x})
    wide = lambda v: v.astype(FULL)
    for_l = jnp.stack([(wide(for_l[0]) + wide(for_l_0)).astype(LOW), for_l[1]])
    for_x = jnp.stack([for_x[0], (wide(for_x[1]) + wide(for_x_1)).astype(LOW)])
    from_l = swap(for_l, "l")
    from_x = swap(for_x, "x")
    return wide(pick(parts, {1: at.l, 2: at.x})) + wide(from_l) + wide(from_x)


def sum_chips(value):
    return value + swap(value, "x") + swap(value, "l") + swap_both(value, "x", "l")


def spread(at, parts):
    mine = pick(parts, {0: at.x, 1: at.l})
    from_x = swap(pick(parts, {0: 1 - at.x, 1: at.l}), "x")
    from_l = swap(pick(parts, {0: at.x, 1: 1 - at.l}), "l")
    far = swap_both(pick(parts, {0: 1 - at.x, 1: 1 - at.l}), "x", "l")
    tail = (0,) * mine.ndim
    one = (1, 1) + mine.shape
    return lay(
        parts.shape,
        [
            (mine.reshape(one), (at.x, at.l) + tail),
            (from_x.reshape(one), (1 - at.x, at.l) + tail),
            (from_l.reshape(one), (at.x, 1 - at.l) + tail),
            (far.reshape(one), (1 - at.x, 1 - at.l) + tail),
        ],
    )


def gather_pieces(at, piece):
    from_h = swap(piece, "h")
    near = [(piece, at.e, at.h), (from_h, at.e, 1 - at.h)]
    near += [(swap(piece, "e"), 1 - at.e, at.h), (swap(from_h, "e"), 1 - at.e, 1 - at.h)]
    pieces = [(v, at.g, e, at.c, h) for v, e, h in near]
    groups = at.groups
    ring = [(i, (i + 1) % groups) for i in range(groups)]
    for v, e, h in near:
        for step in range(1, groups):
            v = lax.ppermute(v, "g", ring)
            pieces.append((v, lax.rem(at.g - step + groups, groups), e, at.c, h))
    pieces += [(swap(v, "c"), g, e, 1 - at.c, h) for v, g, e, _, h in pieces]
    return [(v, (g, e, c, h)) for v, g, e, c, h in pieces]


def scatter_groups(at, value):
    groups = at.groups
    if groups == 1:
        return value[0]
    ring = [(i, (i + 1) % groups) for i in range(groups)]
    total = pick(value, {0: lax.rem(at.g + groups - 1, groups)})
    for step in range(2, groups + 1):
        total = lax.ppermute(total, "g", ring)
        part = pick(value, {0: lax.rem(at.g + 2 * groups - step, groups)})
        total = (total.astype(FULL) + part.astype(FULL)).astype(total.dtype)
    return total


def halve(value, axis, dim, place):
    other = swap(pick(value, {dim: 1 - place}), axis)
    mine = pick(value, {dim: place})
    return (mine.astype(FULL) + other.astype(FULL)).astype(value.dtype)


class Columns:
    def __init__(self, at, split, join):
        self.at, self.split, self.join = at, split, join

    def fetch(self, weight):
        at = self.at
        rows = weight.shape[0]
        mine = spread(at, self.split(weight))
        columns = mine.shape[-1]
        pieces = gather_pieces(at, mine)
        shape = (at.groups, 2, 2, 2, 2, 2, rows, columns)
        out = lay(
            shape,
            [
                (v.reshape(1, 1, 2, 1, 1, 2, rows, columns), (g, e, 0, c, h, 0, 0, 0))
                for v, (g, e, c, h) in pieces
            ],
        )
        return out.reshape(-1, columns)

    def reduce(self, grad):
        at = self.at
        columns = grad.shape[1]
        value = grad.reshape(at.groups, 2, 2, 2, 2, 2, -1, columns)
        value = halve(value, "c", 3, at.c)
        value = halve(value, "e", 1, at.e)
        value = halve(value, "h", 2, at.h)
        value = scatter_groups(at, value)
        return self.join(spread(at, value))


class Rows:
    def __init__(self, at, order):
        self.at, self.order = at, order

    def fetch(self, piece):
        at = self.at
        rows, columns = piece.shape
        sizes = {"g": at.groups, "e": 2, "c": 2, "h": 2}
        shape = tuple(sizes[a] for a in self.order) + (rows, columns)
        parts = []
        for v, place in gather_pieces(at, piece):
            place = dict(zip("gech", place))
            starts = tuple(place[a] for a in self.order) + (0, 0)
            parts.append((v.reshape((1,) * 4 + (rows, columns)), starts))
        return lay(shape, parts).reshape(-1, columns)

    def reduce(self, grad):
        at = self.at
        sizes = {"g": at.groups, "e": 2, "c": 2, "h": 2}
        columns = grad.shape[1]
        value = grad.reshape(tuple(sizes[a] for a in self.order) + (-1, columns))
        left = list(self.order)
        for axis in "ceh":
            dim = left.index(axis)
            value = halve(value, axis, dim, getattr(at, axis))
            left.pop(dim)
        return scatter_groups(at, value)


def gather_gains(at, gains):
    count = gains.shape[0]
    value = gains.reshape(count, 1, -1)
    for axis in ("l", "h", "c", "x", "e"):
        other = swap(value, axis)
        low_first = getattr(at, axis) == 0
        value = jnp.where(
            low_first,
            jnp.concatenate([value, other], axis=1),
            jnp.concatenate([other, value], axis=1),
        )
    if at.groups > 1:
        value = lax.all_gather(value, "g", axis=1, tiled=True)
    return value.reshape(count, -1)


def scatter_gains(at, grads):
    count = grads.shape[0]
    value = grads.reshape(count, at.groups, 2, 2, 2, 2, 2, -1)
    if at.groups > 1:
        value = lax.psum_scatter(value, "g", scatter_dimension=1, tiled=True)
    value = value.reshape(value.shape[:1] + value.shape[2:])
    for axis in ("e", "x", "c", "h", "l"):
        value = halve(value, axis, 1, getattr(at, axis))
    return value


def rope_tables(length, head_dim):
    half_dim = head_dim // 2
    inverse = jnp.power(
        jnp.float32(ROPE_THETA), -(jnp.arange(half_dim, dtype=FULL) * 2.0 / head_dim)
    )
    places = jnp.arange(length, dtype=jnp.int32).astype(FULL)
    angles = places[:, None] * inverse[None, :]
    angles = jnp.concatenate([angles, angles], axis=-1)[:, None, :]
    return (jnp.cos(angles), jnp.sin(angles))


def rotate(tensor, cosine_table, sine_table):
    first, second = jnp.split(tensor, 2, axis=-1)
    turned = jnp.concatenate([-second, first], axis=-1)
    return tensor * cosine_table + turned * sine_table


def rotate_back(grad_in, cosine_table, sine_table):
    shifted = grad_in * sine_table
    first, second = jnp.split(shifted, 2, axis=-1)
    return grad_in * cosine_table + jnp.concatenate([second, -first], axis=-1)


def norm_forward(tensor, gain_vec):
    inverse = lax.rsqrt(jnp.mean(tensor * tensor, axis=-1, keepdims=True) + EPSILON)
    unit = tensor * inverse
    return unit * gain_vec, unit, inverse


def norm_backward(grad_in, unit, inverse, gain_vec):
    axes = tuple(range(grad_in.ndim - 1))
    gain_grad = jnp.sum(grad_in * unit, axis=axes)
    unit_grad = grad_in * gain_vec
    inner = jnp.mean(unit_grad * unit, axis=-1, keepdims=True)
    return inverse * (unit_grad - unit * inner), gain_grad


def on_device(
    hidden_in,
    q_weight,
    k_weight,
    v_weight,
    o_weight,
    q_gain,
    k_gain,
    attn_gain,
    gate_weight,
    up_weight,
    down_weight,
    mlp_gain,
    out_grad,
):
    at = Place()
    batch, rows_here, width = hidden_in.shape
    head_dim = width // HEADS
    length = batch * rows_here * 4
    rows_owned = q_weight.shape[0]
    groups = at.groups
    ff_block = down_weight.shape[0]
    factor = 1.0 / math.sqrt(head_dim)

    trade = "c" if 2 * rows_owned == head_dim else "e"
    if trade == "c":
        feature_shape = (groups * 2, 2, 2, 4 * rows_owned)
        feature_dims = (1, 2)
        o_order = "gehc"
    else:
        feature_shape = (groups, 2, 2, 8 * rows_owned)
        feature_dims = (2, 1)
        o_order = "gche"

    def features_of(vector):
        value = vector.reshape(feature_shape + vector.shape[1:])
        x_dim, l_dim = feature_dims
        rest = [d for d in range(value.ndim) if d not in feature_dims]
        value = value.transpose([x_dim, l_dim] + rest)
        return value.reshape((2, 2, -1) + vector.shape[1:])

    def features_back(value):
        tail = value.shape[3:]
        kept = [n for d, n in enumerate(feature_shape) if d not in feature_dims]
        value = value.reshape([2, 2] + kept + list(tail))
        x_dim, l_dim = feature_dims
        rest = [d for d in range(len(feature_shape) + len(tail)) if d not in feature_dims]
        order = [x_dim, l_dim] + rest
        inverse = [order.index(d) for d in range(len(order))]
        return value.transpose(inverse).reshape((-1,) + tail)

    def split_features(weight):
        return features_of(weight.T).swapaxes(2, 3)

    def join_features(value):
        return features_back(value.swapaxes(2, 3)).T

    ff_shape = (groups * 2, 2, 4, 2, ff_block)

    def split_units(weight):
        value = weight.reshape((-1,) + ff_shape).transpose(2, 4, 0, 1, 3, 5)
        return value.reshape(2, 2, weight.shape[0], -1)

    def join_units(value):
        value = value.reshape(2, 2, value.shape[2], groups * 2, 4, ff_block)
        return value.transpose(2, 3, 0, 4, 1, 5).reshape(value.shape[2], -1)

    def split_three(weight):
        three = [split_features(w) for w in jnp.split(weight, 3, axis=1)]
        return jnp.concatenate(three, axis=-1)

    def join_three(value):
        return [join_features(v) for v in jnp.split(value, 3, axis=-1)]

    qkv = Columns(at, split_three, join_three)
    units = Columns(at, split_units, join_units)
    o_rows = Rows(at, o_order)
    down_rows = Rows(at, "gech")

    gains = gather_gains(at, jnp.stack([q_gain, k_gain, attn_gain, mlp_gain]).astype(FULL))
    here = lambda v: pick(features_of(v), {0: at.x, 1: at.l})
    q_gain_here, k_gain_here = here(gains[0]), here(gains[1])
    attn_gain_all, mlp_gain_all = gains[2], gains[3]

    own_in = tokens_in(at, hidden_in.reshape(-1, width))
    all_in = gather_tokens(at, own_in)
    qkv_all = qkv.fetch(jnp.concatenate([q_weight, k_weight, v_weight], axis=1))
    o_all = o_rows.fetch(transpose_axes(o_weight, trade, "l"))
    gate_all = units.fetch(gate_weight)
    up_all = units.fetch(up_weight)
    down_all = down_rows.fetch(down_weight)
    own_top = tokens_in(at, out_grad.reshape(-1, width)).astype(FULL)

    cosine_table, sine_table = rope_tables(length, head_dim)
    raw = matmul(all_in, qkv_all)
    q_raw, k_raw, v_raw = jnp.split(raw, 3, axis=1)
    squares = sum_chips(jnp.stack([jnp.sum(q_raw * q_raw, -1), jnp.sum(k_raw * k_raw, -1)]))
    inverses = lax.rsqrt(squares / width + EPSILON)
    q_inverse, k_inverse = inverses[0][:, None], inverses[1][:, None]
    q_unit = q_raw * q_inverse
    k_unit = k_raw * k_inverse
    head_shape = (length, -1, head_dim)
    queries = rotate((q_unit * q_gain_here).reshape(head_shape), cosine_table, sine_table)
    keys = rotate((k_unit * k_gain_here).reshape(head_shape), cosine_table, sine_table)
    queries, keys = queries.astype(LOW), keys.astype(LOW)
    values = v_raw.reshape(head_shape).astype(LOW)

    order = jnp.arange(length, dtype=jnp.int32)
    allowed = (order[None, :] <= order[:, None])[None]

    def masked_scores():
        score_raw = jnp.einsum("qhd,khd->hqk", queries, keys, preferred_element_type=FULL)
        return jnp.where(allowed, score_raw * factor, -1e30)

    masked = masked_scores()
    row_max = jnp.max(masked, axis=-1, keepdims=True)
    exponent_terms = jnp.exp(masked - row_max)
    row_total = jnp.sum(exponent_terms, axis=-1, keepdims=True)
    probabilities = (exponent_terms / row_total).astype(LOW)
    log_total = row_max + jnp.log(row_total)
    mixed = jnp.einsum("hqk,khd->qhd", probabilities, values, preferred_element_type=FULL)
    mixed = mixed.astype(LOW).reshape(length, -1)
    attn_out = scatter_tokens(at, matmul(mixed, o_all).astype(LOW))
    attn_normed, attn_unit, attn_inverse = norm_forward(attn_out, attn_gain_all)
    residual = own_in.astype(FULL) + attn_normed
    mlp_in = gather_tokens(at, residual.astype(LOW))
    gate_raw = matmul(mlp_in, gate_all)
    up_raw = matmul(mlp_in, up_all)
    sigmoid_gate = lax.logistic(gate_raw)
    hidden = (gate_raw * sigmoid_gate * up_raw).astype(LOW)
    branch = scatter_tokens(at, matmul(hidden, down_all).astype(LOW))
    branch_normed, branch_unit, branch_inverse = norm_forward(branch, mlp_gain_all)
    layer_out = tokens_out(at, (residual + branch_normed).astype(LOW))

    branch_grad, mlp_gain_grad = norm_backward(own_top, branch_unit, branch_inverse, mlp_gain_all)
    branch_rows = gather_tokens(at, branch_grad.astype(LOW))
    hidden_grad = matmul_back(branch_rows, down_all)
    gate_grad = (
        hidden_grad * up_raw * (sigmoid_gate * (1.0 + gate_raw * (1.0 - sigmoid_gate)))
    ).astype(LOW)
    up_grad = (hidden_grad * gate_raw * sigmoid_gate).astype(LOW)
    input_part = matmul_back(gate_grad, gate_all) + matmul_back(up_grad, up_all)
    residual_grad = own_top + scatter_tokens(at, input_part.astype(LOW))
    down_own = down_rows.reduce(outer(hidden, branch_rows).astype(LOW))
    gate_own = units.reduce(outer(mlp_in, gate_grad).astype(LOW))
    up_own = units.reduce(outer(mlp_in, up_grad).astype(LOW))

    attn_grad, attn_gain_grad = norm_backward(
        residual_grad, attn_unit, attn_inverse, attn_gain_all
    )
    attn_low = gather_tokens(at, attn_grad.astype(LOW))
    o_own = transpose_axes(
        o_rows.reduce(outer(mixed, attn_low).astype(LOW)), trade, "l"
    )
    mixed_grad = matmul_back(attn_low, o_all).astype(LOW).reshape(head_shape)
    probs_again = jnp.exp(masked_scores() - log_total)
    prob_grad = jnp.einsum("qhd,khd->hqk", mixed_grad, values, preferred_element_type=FULL)
    row_dot = jnp.sum(probs_again * prob_grad, axis=-1, keepdims=True)
    score_grad = (probs_again * (prob_grad - row_dot) * factor).astype(LOW)
    query_grad = jnp.einsum("hqk,khd->qhd", score_grad, keys, preferred_element_type=FULL)
    key_grad = jnp.einsum("hqk,qhd->khd", score_grad, queries, preferred_element_type=FULL)
    value_grad = jnp.einsum(
        "hqk,qhd->khd", probs_again.astype(LOW), mixed_grad, preferred_element_type=FULL
    )
    q_pre = rotate_back(query_grad, cosine_table, sine_table).reshape(length, -1)
    k_pre = rotate_back(key_grad, cosine_table, sine_table).reshape(length, -1)
    q_gain_grad = jnp.sum(q_pre * q_unit, axis=0)
    k_gain_grad = jnp.sum(k_pre * k_unit, axis=0)
    q_unit_grad = q_pre * q_gain_here
    k_unit_grad = k_pre * k_gain_here
    inner = sum_chips(
        jnp.stack([jnp.sum(q_unit_grad * q_unit, -1), jnp.sum(k_unit_grad * k_unit, -1)])
    ) / width
    q_low = (q_inverse * (q_unit_grad - q_unit * inner[0][:, None])).astype(LOW)
    k_low = (k_inverse * (k_unit_grad - k_unit * inner[1][:, None])).astype(LOW)
    v_low = value_grad.reshape(length, -1).astype(LOW)
    raw_grad = jnp.concatenate([q_low, k_low, v_low], axis=1)
    own_three = qkv.reduce(outer(all_in, raw_grad).astype(LOW))
    in_part = scatter_tokens(at, matmul_back(raw_grad, qkv_all).astype(LOW))
    in_grad = tokens_out(at, (residual_grad + in_part).astype(LOW))

    def whole(vector):
        out = jnp.zeros((2, 2) + vector.shape, FULL)
        out = lax.dynamic_update_slice(out, vector[None, None], (at.x, at.l, 0))
        return features_back(out)

    gain_grads = scatter_gains(
        at,
        jnp.stack([whole(q_gain_grad), whole(k_gain_grad), attn_gain_grad, mlp_gain_grad]),
    )
    grads = [v.astype(FULL) for v in own_three + [o_own, gate_own, up_own, down_own]]
    shape = hidden_in.shape
    return (
        (layer_out.reshape(shape), in_grad.reshape(shape)) + tuple(grads) + tuple(gain_grads)
    )


def solution(mesh):
    dp, seq = mesh.shape["dp"], mesh.shape["seq"]
    split = Mesh(mesh.devices.reshape(dp // 8, 2, 2, 2, seq // 2, 2), AXES)
    dp_axes, seq_axes = AXES[:4], AXES[4:]
    tokens = P(dp_axes, seq_axes, None)
    matrix, vector = P(AXES, None), P(AXES)
    return jax.shard_map(
        on_device,
        mesh=split,
        in_specs=(tokens,)
        + (matrix,) * 4
        + (vector,) * 3
        + (matrix,) * 3
        + (vector, tokens),
        out_specs=(tokens,) * 2 + (matrix,) * 7 + (vector,) * 4,
        check_vma=False,
    )
```

```python
import math

import jax
import jax.numpy as jnp
from jax import lax
from jax.experimental import pallas as pl
from jax.experimental.pallas import tpu as pltpu
from jax.sharding import Mesh
from jax.sharding import PartitionSpec as P

HEADS = 16
EPSILON = 1e-06
ROPE_THETA = 500000.0
LOW = jnp.bfloat16
FULL = jnp.float32

AXES = ("g", "e", "x", "c", "h", "l")
SWAP = [(0, 1), (1, 0)]
BOTH = [(i, 3 - i) for i in range(4)]
VMEM_LIMIT = 48 * 1024 * 1024


BLOCK = 256

def dot_nt(a, b):
    return lax.dot_general(a, b, (((1,), (1,)), ((), ())), preferred_element_type=FULL)

def dot_nn(a, b):
    return lax.dot_general(a, b, (((1,), (0,)), ((), ())), preferred_element_type=FULL)

def dot_tn(a, b):
    return lax.dot_general(a, b, (((0,), (0,)), ((), ())), preferred_element_type=FULL)

def turn(tensor):
    return pltpu.roll(tensor, tensor.shape[1] // 2, 1)


def attend_kernel(q_raw, k_raw, v_raw, inverse, q_gain, k_gain, cosine, sine,
                  q_out, k_out, v_out, mixed):
    length, head_dim = q_raw.shape
    factor = 1.0 / math.sqrt(head_dim)
    block = min(BLOCK, length)

    def rope(raw, column, gain):
        normed = raw[...] * inverse[:, column : column + 1] * gain[...]
        return (normed * cosine[...] + turn(normed) * sine[...]).astype(LOW)

    q_out[...] = rope(q_raw, 0, q_gain)
    k_out[...] = rope(k_raw, 1, k_gain)
    v_out[...] = v_raw[...].astype(LOW)
    shape = (block, block)
    allowed = lax.broadcasted_iota(jnp.int32, shape, 1) <= lax.broadcasted_iota(jnp.int32, shape, 0)
    for start in range(0, length, block):
        here = slice(start, start + block)
        queries = q_out[here, :]
        near = jnp.where(allowed, dot_nt(queries, k_out[here, :]) * factor, -1e30)
        top = jnp.max(near, axis=1, keepdims=True)
        if start:
            far = dot_nt(queries, k_out[:start, :]) * factor
            top = jnp.maximum(top, jnp.max(far, axis=1, keepdims=True))
            far = jnp.exp(far - top)
        near = jnp.exp(near - top)
        total = jnp.sum(near, axis=1, keepdims=True)
        if start:
            total += jnp.sum(far, axis=1, keepdims=True)
        scale = 1.0 / total
        out = dot_nn((near * scale).astype(LOW), v_out[here, :])
        if start:
            out += dot_nn((far * scale).astype(LOW), v_out[:start, :])
        mixed[here, :] = out.astype(LOW)


def attend(raw, inverse, q_gain, k_gain, cosine, sine):
    length, wide = raw.shape
    head_dim = cosine.shape[1]
    width = wide // 3
    heads = width // head_dim
    column = lambda shift: pl.BlockSpec((length, head_dim), lambda i: (0, i + shift * heads))
    whole = lambda v: pl.BlockSpec(v.shape, lambda i: (0, 0))
    gain = pl.BlockSpec((1, head_dim), lambda i: (0, i))
    out = jax.ShapeDtypeStruct((length, width), LOW)
    return pl.pallas_call(
        attend_kernel,
        grid=(heads,),
        in_specs=[column(0), column(1), column(2), whole(inverse), gain, gain, whole(cosine), whole(sine)],
        out_specs=[column(0)] * 4,
        out_shape=[out] * 4,
        compiler_params=pltpu.CompilerParams(vmem_limit_bytes=VMEM_LIMIT),
        cost_estimate=pl.CostEstimate(flops=3 * length * length * width, bytes_accessed=20 * length * width, transcendentals=heads * length * length // 2),
    )(raw, raw, raw, inverse, q_gain, k_gain, cosine, sine)


def attend_back_kernel(queries, keys, values, mixed_grad, q_raw, k_raw, inverse, q_gain, k_gain, cosine, sine,
                       q_grad, k_grad, v_grad, sums, q_gain_grad, k_gain_grad, k_total, v_total):
    length, head_dim = queries.shape
    factor = 1.0 / math.sqrt(head_dim)
    block = min(BLOCK, length)
    shape = (block, block)
    allowed = lax.broadcasted_iota(jnp.int32, shape, 0) <= lax.broadcasted_iota(jnp.int32, shape, 1)
    first = pl.program_id(0) == 0

    def unrope(grad, raw, column, gain, rows):
        pre = grad * cosine[rows, :] - turn(grad) * sine[rows, :]
        unit = raw[rows, :] * inverse[rows, column : column + 1]
        scaled = pre * gain[...]
        return scaled, jnp.sum(scaled * unit, axis=1, keepdims=True), jnp.sum(pre * unit, axis=0, keepdims=True)

    q_gain_total = jnp.zeros((1, head_dim), FULL)
    for start in range(0, length, block):
        here = slice(start, start + block)
        query, out_grad = queries[here, :], mixed_grad[here, :]
        near = jnp.where(allowed, dot_nt(keys[here, :], query) * factor, -1e30)
        top = jnp.max(near, axis=0, keepdims=True)
        if start:
            far = dot_nt(keys[:start, :], query) * factor
            top = jnp.maximum(top, jnp.max(far, axis=0, keepdims=True))
            far = jnp.exp(far - top)
        near = jnp.exp(near - top)
        total = jnp.sum(near, axis=0, keepdims=True)
        if start:
            total += jnp.sum(far, axis=0, keepdims=True)
        scale = 1.0 / total
        near = near * scale
        near_grad = dot_nt(values[here, :], out_grad)
        inner = jnp.sum(near * near_grad, axis=0, keepdims=True)
        if start:
            far = far * scale
            far_grad = dot_nt(values[:start, :], out_grad)
            inner += jnp.sum(far * far_grad, axis=0, keepdims=True)
        near_score = (near * (near_grad - inner) * factor).astype(LOW)
        grad = dot_tn(near_score, keys[here, :])
        k_total[here, :] = dot_nn(near_score, query)
        v_total[here, :] = dot_nn(near.astype(LOW), out_grad)
        if start:
            far_score = (far * (far_grad - inner) * factor).astype(LOW)
            grad += dot_tn(far_score, keys[:start, :])
            k_total[:start, :] += dot_nn(far_score, query)
            v_total[:start, :] += dot_nn(far.astype(LOW), out_grad)
        scaled, row_sum, gain_part = unrope(grad, q_raw, 0, q_gain, here)
        q_grad[here, :] = scaled
        q_gain_total += gain_part
        sums[here, 0:1] = jnp.where(first, row_sum, sums[here, 0:1] + row_sum)
    q_gain_grad[...] = q_gain_total
    scaled, row_sum, gain_part = unrope(k_total[...], k_raw, 1, k_gain, slice(None))
    k_grad[...] = scaled
    k_gain_grad[...] = gain_part
    sums[:, 1:2] = jnp.where(first, row_sum, sums[:, 1:2] + row_sum)
    v_grad[...] = v_total[...].astype(LOW)


def attend_back(queries, keys, values, mixed_grad, raw, inverse, q_gain, k_gain, cosine, sine):
    length, width = queries.shape
    head_dim = cosine.shape[1]
    heads = width // head_dim
    column = lambda shift: pl.BlockSpec((length, head_dim), lambda i: (0, i + shift * heads))
    whole = lambda v: pl.BlockSpec(v.shape, lambda i: (0, 0))
    gain = pl.BlockSpec((1, head_dim), lambda i: (0, i))
    wide = jax.ShapeDtypeStruct((length, width), FULL)
    vector = jax.ShapeDtypeStruct((1, width), FULL)
    return pl.pallas_call(
        attend_back_kernel,
        grid=(heads,),
        in_specs=[column(0)] * 4 + [column(0), column(1), whole(inverse), gain, gain, whole(cosine), whole(sine)],
        out_specs=[column(0)] * 3 + [pl.BlockSpec((length, 2), lambda i: (0, 0)), gain, gain],
        out_shape=[wide, wide, jax.ShapeDtypeStruct((length, width), LOW), jax.ShapeDtypeStruct((length, 2), FULL), vector, vector],
        scratch_shapes=[pltpu.VMEM((length, head_dim), FULL)] * 2,
        compiler_params=pltpu.CompilerParams(vmem_limit_bytes=VMEM_LIMIT),
        cost_estimate=pl.CostEstimate(flops=6 * length * length * width, bytes_accessed=30 * length * width, transcendentals=heads * length * length // 2),
    )(queries, keys, values, mixed_grad, raw, raw, inverse, q_gain, k_gain, cosine, sine)


def matmul(left_side, right_side):
    return dot_nn(left_side, right_side)


def matmul_back(left_side, right_side):
    return dot_nt(left_side, right_side)


def outer(left_side, right_side):
    return dot_tn(left_side, right_side)


def wide(value):
    return value.astype(FULL)


def tie(values, others):
    if not others:
        return tuple(values)
    return lax.optimization_barrier(tuple(values) + tuple(others))[: len(values)]


class Steps:
    def __init__(self):
        self.last = ()

    def __call__(self, step, *inputs):
        flat, tree = jax.tree.flatten(inputs)
        out = step(*tree.unflatten(tie(flat, self.last)))
        self.last = tuple(jax.tree.leaves(out))
        return out


class Links:
    def __init__(self):
        self.sent = {}

    def send(self, value, axes, pairs):
        last = {id(v): v for v in (self.sent.get(a) for a in axes) if v is not None}
        (value,) = tie((value,), last.values())
        got = lax.ppermute(value, axes if len(axes) > 1 else axes[0], pairs)
        for axis in axes:
            self.sent[axis] = got
        return got

    def swap(self, value, axis):
        return self.send(value, (axis,), SWAP)

    def swap_both(self, value, first, second):
        return self.send(value, (first, second), BOTH)


def swap(value, axis):
    return lax.ppermute(value, axis, SWAP)


def pick(value, places):
    starts = [0] * value.ndim
    sizes = list(value.shape)
    for dim, place in places.items():
        starts[dim] = place
        sizes[dim] = 1
    taken = lax.dynamic_slice(value, starts, sizes)
    return taken.reshape([s for d, s in enumerate(value.shape) if d not in places])


def put(out, parts):
    for value, starts in parts:
        out = lax.dynamic_update_slice(out, value, starts)
    return out


class Place:
    def __init__(self):
        self.g, self.e, self.x, self.c, self.h, self.l = (lax.axis_index(a) for a in AXES)
        self.groups = lax.axis_size("g")
        self.links = Links()
        self.steps = Steps()


class TokensIn:
    def __init__(self, at, rows):
        self.at = at
        count, width = rows.shape

        def start(rows):
            halves = rows.reshape(2, count // 2, width)
            return pick(halves, {0: at.x}), pick(halves, {0: 1 - at.x})

        self.mine, other = at.steps(start, rows)
        self.other = at.links.swap(other, "x")

    def second(self):
        at = self.at
        same = at.x == at.h

        def turn_over(mine, other):
            return jnp.where(same, mine, other), jnp.where(same, other, mine)

        self.kept, other = at.steps(turn_over, self.mine, self.other)
        self.got = at.links.swap(other, "h")

    def third(self):
        low_first = self.at.h == 0

        def join(kept, got):
            return jnp.stack(
                [jnp.where(low_first, kept, got), jnp.where(low_first, got, kept)]
            )

        return self.at.steps(join, self.kept, self.got)


class TokensOut:
    def __init__(self, at, blocks):
        self.at = at
        start = lambda v: (pick(v, {0: at.h}), pick(v, {0: 1 - at.h}))
        self.kept, other = at.steps(start, blocks)
        self.got = at.links.swap(other, "h")

    def second(self):
        at = self.at
        same = at.x == at.h

        def turn_over(kept, got):
            return jnp.where(same, kept, got), jnp.where(same, got, kept)

        self.mine, other = at.steps(turn_over, self.kept, self.got)
        self.other = at.links.swap(other, "x")

    def third(self):
        low_first = self.at.x == 0

        def join(mine, other):
            return jnp.concatenate(
                [jnp.where(low_first, mine, other), jnp.where(low_first, other, mine)], axis=0
            )

        return self.at.steps(join, self.mine, self.other)


class GatherTokens:
    def __init__(self, at, blocks):
        self.at, self.blocks = at, blocks
        self.from_l = at.links.swap(blocks, "l")
        self.from_x = at.links.swap(blocks, "x")

    def second(self):
        at = self.at
        half_l, half_x = at.steps(lambda a, b: (a[0], b[1]), self.from_l, self.from_x)
        self.far_0 = at.links.swap(half_l, "x")
        self.far_1 = at.links.swap(half_x, "l")
        two, count, width = self.blocks.shape
        cut = (2, 1, 1, count, width)

        def near(blocks, from_x, from_l):
            out = jnp.zeros((2, 2, 2, count, width), blocks.dtype)
            parts = [
                (blocks.reshape(cut), (0, at.l, at.x, 0, 0)),
                (from_x.reshape(cut), (0, at.l, 1 - at.x, 0, 0)),
                (from_l.reshape(cut), (0, 1 - at.l, at.x, 0, 0)),
            ]
            return put(out, parts)

        self.out = at.steps(near, self.blocks, self.from_x, self.from_l)

    def third(self):
        at = self.at
        two, count, width = self.blocks.shape
        one = (1, 1, 1, count, width)

        def far(out, far_0, far_1):
            parts = [
                (far_0.reshape(one), (0, 1 - at.l, 1 - at.x, 0, 0)),
                (far_1.reshape(one), (1, 1 - at.l, 1 - at.x, 0, 0)),
            ]
            return put(out, parts).reshape(8 * count, width)

        return at.steps(far, self.out, self.far_0, self.far_1)


class ScatterTokens:
    def __init__(self, at, rows):
        self.at = at
        total, width = rows.shape
        self.parts = rows.reshape(2, 2, 2, total // 8, width)

        def start(parts):
            far = pick(parts, {1: 1 - at.l, 2: 1 - at.x})
            return far[0], far[1]

        far_0, far_1 = at.steps(start, self.parts)
        self.for_l_0 = at.links.swap(far_0, "x")
        self.for_x_1 = at.links.swap(far_1, "l")

    def second(self):
        at = self.at

        def add(parts, for_l_0, for_x_1):
            for_l = pick(parts, {1: 1 - at.l, 2: at.x})
            for_x = pick(parts, {1: at.l, 2: 1 - at.x})
            for_l = jnp.stack([(wide(for_l[0]) + wide(for_l_0)).astype(LOW), for_l[1]])
            for_x = jnp.stack([for_x[0], (wide(for_x[1]) + wide(for_x_1)).astype(LOW)])
            return for_l, for_x

        for_l, for_x = at.steps(add, self.parts, self.for_l_0, self.for_x_1)
        self.from_l = at.links.swap(for_l, "l")
        self.from_x = at.links.swap(for_x, "x")

    def third(self, step, *inputs):
        at = self.at

        def add(parts, from_l, from_x, *inputs):
            mine = pick(parts, {1: at.l, 2: at.x})
            return step(wide(mine) + wide(from_l) + wide(from_x), *inputs)

        return at.steps(add, self.parts, self.from_l, self.from_x, *inputs)


def sum_chips(value):
    far = lax.ppermute(value, ("x", "l"), BOTH)
    return value + swap(value, "x") + swap(value, "l") + far


class Spread:
    def __init__(self, at, parts):
        self.at = at

        def start(parts):
            return tuple(
                pick(parts, {0: x, 1: l}) for x in (at.x, 1 - at.x) for l in (at.l, 1 - at.l)
            )

        self.mine, for_l, for_x, far = at.steps(start, parts)
        self.from_x = at.links.swap(for_x, "x")
        self.from_l = at.links.swap(for_l, "l")
        self.far = at.links.swap_both(far, "x", "l")

    def second(self, last=lambda v: v):
        at = self.at
        shape = self.mine.shape
        tail = (0,) * len(shape)

        def join(mine, from_x, from_l, far):
            one = (1, 1) + shape
            out = jnp.zeros((2, 2) + shape, mine.dtype)
            parts = [
                (mine.reshape(one), (at.x, at.l) + tail),
                (from_x.reshape(one), (1 - at.x, at.l) + tail),
                (from_l.reshape(one), (at.x, 1 - at.l) + tail),
                (far.reshape(one), (1 - at.x, 1 - at.l) + tail),
            ]
            return last(put(out, parts))

        return at.steps(join, self.mine, self.from_x, self.from_l, self.far)


class Fetch:
    def __init__(self, at, piece):
        self.at, self.piece = at, piece
        self.from_h = at.links.swap(piece, "h")
        self.from_e = at.links.swap(piece, "e")
        self.from_both = at.links.swap(self.from_h, "e")
        near = [
            (piece, at.e, at.h),
            (self.from_e, 1 - at.e, at.h),
            (self.from_h, at.e, 1 - at.h),
            (self.from_both, 1 - at.e, 1 - at.h),
        ]
        groups = at.groups
        ring = [(i, (i + 1) % groups) for i in range(groups)]
        self.pieces = []
        for value, e, h in near:
            for step in range(groups):
                if step:
                    value = lax.ppermute(value, "g", ring)
                g = lax.rem(at.g - step + groups, groups)
                self.pieces.append((value, (g, e, at.c, h)))
                self.pieces.append((swap(value, "c"), (g, e, 1 - at.c, h)))

    def lay(self, out, shape, starts_of, count):
        now, self.pieces = self.pieces[:count], self.pieces[count:]
        values = [v for v, _ in now]

        def step(out, values):
            return put(
                out,
                [(v.reshape(shape), starts_of(p)) for v, (_, p) in zip(values, now)],
            )

        return self.at.steps(step, out, values)


class FetchColumns(Fetch):
    def __init__(self, at, mine):
        super().__init__(at, mine)
        rows, columns = mine.shape[2:]
        self.shape = (1, 1, 2, 1, 1, 2, rows, columns)
        self.out = jnp.zeros((at.groups, 2, 2, 2, 2, 2, rows, columns), mine.dtype)

    def more(self, share):
        starts_of = lambda p: (p[0], p[1], 0, p[2], p[3], 0, 0, 0)
        count = share * self.at.groups
        self.out = self.lay(self.out, self.shape, starts_of, count)
        return self.out.reshape(-1, self.out.shape[-1])


class FetchRows(Fetch):
    def __init__(self, at, piece, order):
        super().__init__(at, piece)
        self.order = order
        sizes = {"g": at.groups, "e": 2, "c": 2, "h": 2}
        self.shape = (1,) * 4 + piece.shape
        self.out = jnp.zeros(tuple(sizes[a] for a in order) + piece.shape, piece.dtype)

    def more(self, share):
        starts_of = lambda p: tuple(dict(zip("gech", p))[a] for a in self.order) + (0, 0)
        count = share * self.at.groups
        self.out = self.lay(self.out, self.shape, starts_of, count)
        return self.out.reshape(-1, self.out.shape[-1])


class Reduce:
    def __init__(self, at, value, dims):
        self.at = at
        self.value, self.dims = value, list(dims)
        place = self.dims.index("c")
        send = at.steps(lambda v: pick(v, {place: 1 - at.c}), value)
        self.got = at.links.swap(send, "c")

    def second(self):
        at = self.at
        c_dim = self.dims.index("c")
        self.dims.pop(c_dim)
        dim = self.dims.index("e")

        def add(value, got):
            mine = pick(value, {c_dim: at.c})
            part = lambda e: (wide(pick(mine, {dim: e})) + wide(pick(got, {dim: e}))).astype(LOW)
            return part(at.e), part(1 - at.e)

        self.kept, send = at.steps(add, self.value, self.got)
        self.dims.pop(dim)
        self.got = at.links.swap(send, "e")

    def third(self):
        at = self.at
        dim = self.dims.index("h")

        def add(kept, got):
            part = lambda h: (wide(pick(kept, {dim: h})) + wide(pick(got, {dim: h}))).astype(LOW)
            return part(at.h), part(1 - at.h)

        self.kept, send = at.steps(add, self.kept, self.got)
        self.dims.pop(dim)
        self.got = at.links.swap(send, "h")

    def fourth(self, kind=LOW):
        at = self.at
        groups = at.groups
        add = lambda kept, got: (wide(kept) + wide(got)).astype(kind if groups == 1 else LOW)
        value = at.steps(add, self.kept, self.got)
        dim = self.dims.index("g")
        if groups == 1:
            return value.reshape([s for d, s in enumerate(value.shape) if d != dim])
        ring = [(i, (i + 1) % groups) for i in range(groups)]
        total = pick(value, {dim: lax.rem(at.g + groups - 1, groups)})
        for step in range(2, groups + 1):
            total = lax.ppermute(total, "g", ring)
            part = pick(value, {dim: lax.rem(at.g + 2 * groups - step, groups)})
            total = wide(total) + wide(part)
            total = total.astype(kind if step == groups else LOW)
        return total


def gather_gains(at, gains):
    count = gains.shape[0]
    value = gains.reshape(count, 1, -1)
    for axis in ("l", "h", "c", "x", "e"):
        other = swap(value, axis)
        low_first = getattr(at, axis) == 0
        value = jnp.where(
            low_first,
            jnp.concatenate([value, other], axis=1),
            jnp.concatenate([other, value], axis=1),
        )
    if at.groups > 1:
        value = lax.all_gather(value, "g", axis=1, tiled=True)
    return value.reshape(count, -1)


def scatter_gains(at, grads):
    count = grads.shape[0]
    value = grads.reshape(count, at.groups, 2, 2, 2, 2, 2, -1)
    if at.groups > 1:
        value = lax.psum_scatter(value, "g", scatter_dimension=1, tiled=True)
    value = value.reshape(value.shape[:1] + value.shape[2:])
    for axis in ("e", "x", "c", "h", "l"):
        place = getattr(at, axis)
        value = pick(value, {1: place}) + swap(pick(value, {1: 1 - place}), axis)
    return value


def rope_tables(length, head_dim):
    half_dim = head_dim // 2
    inverse = jnp.power(
        jnp.float32(ROPE_THETA), -(jnp.arange(half_dim, dtype=FULL) * 2.0 / head_dim)
    )
    places = jnp.arange(length, dtype=jnp.int32).astype(FULL)
    angles = places[:, None] * inverse[None, :]
    sine = jnp.sin(angles)
    cosine = jnp.cos(angles)
    return (
        jnp.concatenate([cosine, cosine], axis=-1),
        jnp.concatenate([-sine, sine], axis=-1),
    )


def norm_forward(tensor, gain_vec):
    inverse = lax.rsqrt(jnp.mean(tensor * tensor, axis=-1, keepdims=True) + EPSILON)
    unit = tensor * inverse
    return unit * gain_vec, unit, inverse


def norm_backward(grad_in, unit, inverse, gain_vec):
    axes = tuple(range(grad_in.ndim - 1))
    gain_grad = jnp.sum(grad_in * unit, axis=axes)
    unit_grad = grad_in * gain_vec
    inner = jnp.mean(unit_grad * unit, axis=-1, keepdims=True)
    return inverse * (unit_grad - unit * inner), gain_grad


def on_device(
    hidden_in,
    q_weight,
    k_weight,
    v_weight,
    o_weight,
    q_gain,
    k_gain,
    attn_gain,
    gate_weight,
    up_weight,
    down_weight,
    mlp_gain,
    out_grad,
):
    at = Place()
    steps = at.steps
    batch, rows_here, width = hidden_in.shape
    head_dim = width // HEADS
    length = batch * rows_here * 4
    rows_owned = q_weight.shape[0]
    groups = at.groups
    ff_block = down_weight.shape[0]

    trade = "c" if 2 * rows_owned == head_dim else "e"
    if trade == "c":
        feature_shape = (groups * 2, 2, 2, 4 * rows_owned)
        feature_dims = (1, 2)
        o_order = "gehc"
    else:
        feature_shape = (groups, 2, 2, 8 * rows_owned)
        feature_dims = (2, 1)
        o_order = "gche"

    def features_of(vector):
        value = vector.reshape(feature_shape + vector.shape[1:])
        x_dim, l_dim = feature_dims
        rest = [d for d in range(value.ndim) if d not in feature_dims]
        value = value.transpose([x_dim, l_dim] + rest)
        return value.reshape((2, 2, -1) + vector.shape[1:])

    def features_back(value):
        tail = value.shape[3:]
        kept = [n for d, n in enumerate(feature_shape) if d not in feature_dims]
        value = value.reshape([2, 2] + kept + list(tail))
        x_dim, l_dim = feature_dims
        rest = [d for d in range(len(feature_shape) + len(tail)) if d not in feature_dims]
        order = [x_dim, l_dim] + rest
        inverse = [order.index(d) for d in range(len(order))]
        return value.transpose(inverse).reshape((-1,) + tail)

    ff_shape = (groups * 2, 2, 4, 2, ff_block)

    def split_units(weight):
        value = weight.reshape((-1,) + ff_shape).transpose(2, 4, 0, 1, 3, 5)
        return value.reshape(2, 2, weight.shape[0], -1)

    def join_units(value):
        value = wide(value).reshape(2, 2, value.shape[2], groups * 2, 4, ff_block)
        return value.transpose(2, 3, 0, 4, 1, 5).reshape(value.shape[2], -1)

    def split_three(*weights):
        return jnp.concatenate([features_of(w.T).swapaxes(2, 3) for w in weights], axis=-1)

    def join_three(value):
        parts = jnp.split(wide(value), 3, axis=-1)
        return [features_back(v.swapaxes(2, 3)).T for v in parts]

    def as_columns(grad):
        return grad.reshape(groups, 2, 2, 2, 2, 2, -1, grad.shape[1])

    def as_rows(grad, order):
        sizes = {"g": groups, "e": 2, "c": 2, "h": 2}
        return grad.reshape(tuple(sizes[a] for a in order) + (-1, grad.shape[1]))

    own = TokensIn(at, hidden_in.reshape(-1, width))
    qkv_spread = Spread(at, steps(split_three, q_weight, k_weight, v_weight))
    gate_spread = Spread(at, steps(split_units, gate_weight))
    own.second()
    qkv_fetch = FetchColumns(at, qkv_spread.second())
    o_mine = lax.ppermute(o_weight, (trade, "l"), [(0, 0), (1, 2), (2, 1), (3, 3)])
    o_fetch = FetchRows(at, o_mine, o_order)
    up_spread = Spread(at, steps(split_units, up_weight))
    gate_fetch = FetchColumns(at, gate_spread.second())
    cosine, sine = steps(lambda: rope_tables(length, head_dim))
    own_in = own.third()
    all_in = GatherTokens(at, own_in)
    up_fetch = FetchColumns(at, up_spread.second())
    down_fetch = FetchRows(at, down_weight, "gech")
    gains = gather_gains(at, wide(jnp.stack([q_gain, k_gain, attn_gain, mlp_gain])))
    here = lambda v: pick(features_of(v), {0: at.x, 1: at.l})[None]
    q_gain_here, k_gain_here = here(gains[0]), here(gains[1])
    attn_gain_all, mlp_gain_all = gains[2], gains[3]
    qkv_fetch.more(4)
    all_in.second()
    top = TokensIn(at, out_grad.reshape(-1, width))
    qkv_fetch.more(2)
    all_in = all_in.third()
    qkv_all = qkv_fetch.more(2)

    def project(all_in, qkv_all):
        raw = matmul(all_in, qkv_all)
        q_raw, k_raw, _ = jnp.split(raw, 3, axis=1)
        return raw, jnp.stack([jnp.sum(q_raw * q_raw, -1), jnp.sum(k_raw * k_raw, -1)])

    raw, squares = steps(project, all_in, qkv_all)
    squares = sum_chips(squares)
    o_fetch.more(6)
    inverse = steps(lambda s: lax.rsqrt(s / width + EPSILON).T, squares)
    queries, keys, values, mixed = steps(
        attend, raw, inverse, q_gain_here, k_gain_here, cosine, sine
    )
    o_all = o_fetch.more(2)
    attn_part = steps(lambda a, b: matmul(a, b).astype(LOW), mixed, o_all)
    scatter = ScatterTokens(at, attn_part)
    gate_fetch.more(4)
    scatter.second()
    gate_fetch.more(2)
    gate_all = gate_fetch.more(2)

    def after_attention(attn_out, own_in, gain):
        normed, unit, inverse = norm_forward(attn_out, gain)
        residual = wide(own_in) + normed
        return residual.astype(LOW), residual, unit, inverse

    residual_low, residual, attn_unit, attn_inverse = scatter.third(
        after_attention, own_in, attn_gain_all
    )

    mlp_in = GatherTokens(at, residual_low)
    up_fetch.more(4)
    top.second()
    mlp_in.second()
    up_fetch.more(2)
    up_all = up_fetch.more(2)
    mlp_in = mlp_in.third()

    gate_raw = steps(matmul, mlp_in, gate_all)

    def gated(mlp_in, up_all, gate_raw):
        up_raw = matmul(mlp_in, up_all)
        return (gate_raw * lax.logistic(gate_raw) * up_raw).astype(LOW), up_raw

    hidden, up_raw = steps(gated, mlp_in, up_all, gate_raw)
    down_fetch.more(6)
    down_all = down_fetch.more(2)
    branch_part = steps(lambda a, b: matmul(a, b).astype(LOW), hidden, down_all)
    scatter = ScatterTokens(at, branch_part)
    own_top = top.third()
    scatter.second()

    def after_mlp(branch, residual, own_top, gain):
        normed, unit, inverse = norm_forward(branch, gain)
        grad, gain_grad = norm_backward(wide(own_top), unit, inverse, gain)
        return grad.astype(LOW), (residual + normed).astype(LOW), gain_grad

    branch_low, own_out, mlp_gain_grad = scatter.third(
        after_mlp, residual, own_top, mlp_gain_all
    )

    branch_rows = GatherTokens(at, branch_low)
    layer_out = TokensOut(at, own_out)
    branch_rows.second()
    branch_rows = branch_rows.third()
    grad = steps(lambda a, b: outer(a, b).astype(LOW), hidden, branch_rows)
    down_reduce = Reduce(at, as_rows(grad, "gech"), "gech__")

    def gated_back(branch_rows, down_all, gate_raw, up_raw):
        hidden_grad = matmul_back(branch_rows, down_all)
        sigmoid_gate = lax.logistic(gate_raw)
        gate_grad = hidden_grad * up_raw * (sigmoid_gate * (1.0 + gate_raw * (1.0 - sigmoid_gate)))
        up_grad = hidden_grad * gate_raw * sigmoid_gate
        return gate_grad.astype(LOW), up_grad.astype(LOW)

    gate_grad, up_grad = steps(gated_back, branch_rows, down_all, gate_raw, up_raw)
    down_reduce.second()
    layer_out.second()

    def input_back(gate_grad, gate_all, up_grad, up_all):
        return (matmul_back(gate_grad, gate_all) + matmul_back(up_grad, up_all)).astype(LOW)

    input_part = steps(input_back, gate_grad, gate_all, up_grad, up_all)
    scatter = ScatterTokens(at, input_part)
    grad = steps(lambda a, b: outer(a, b).astype(LOW), mlp_in, gate_grad)
    gate_reduce = Reduce(at, as_columns(grad), "ge_ch___")
    scatter.second()
    grad = steps(lambda a, b: outer(a, b).astype(LOW), mlp_in, up_grad)
    up_reduce = Reduce(at, as_columns(grad), "ge_ch___")
    gate_reduce.second()
    down_reduce.third()

    def before_attention(input_grad, own_top, unit, inverse, gain):
        residual_grad = wide(own_top) + input_grad
        grad, gain_grad = norm_backward(residual_grad, unit, inverse, gain)
        return grad.astype(LOW), residual_grad, gain_grad

    attn_grad, residual_grad, attn_gain_grad = scatter.third(
        before_attention, own_top, attn_unit, attn_inverse, attn_gain_all
    )

    attn_low = GatherTokens(at, attn_grad)
    up_reduce.second()
    attn_low.second()
    attn_low = attn_low.third()
    mixed_grad = steps(lambda a, b: matmul_back(a, b).astype(LOW), attn_low, o_all)
    grad = steps(lambda a, b: outer(a, b).astype(LOW), mixed, attn_low)
    o_reduce = Reduce(at, as_rows(grad, o_order), o_order + "__")
    layer_out = layer_out.third()
    gate_reduce.third()
    q_scaled, k_scaled, v_low, inner, q_gain_grad, k_gain_grad = steps(
        attend_back, queries, keys, values, mixed_grad, raw, inverse,
        q_gain_here, k_gain_here, cosine, sine,
    )
    inner = sum_chips(steps(lambda v: v.T / width, inner))
    o_reduce.second()
    down_own = down_reduce.fourth(FULL)

    def before_project(raw, inverse, q_scaled, k_scaled, inner):
        q_raw, k_raw, _ = jnp.split(raw, 3, axis=1)
        inner = inner.T
        grads = []
        for i, (part, scaled) in enumerate([(q_raw, q_scaled), (k_raw, k_scaled)]):
            each = inverse[:, i : i + 1]
            grads.append((each * (scaled - part * each * inner[:, i : i + 1])).astype(LOW))
        return grads

    q_low, k_low = steps(before_project, raw, inverse, q_scaled, k_scaled, inner)
    raw_grad = steps(lambda *v: jnp.concatenate(v, axis=1), q_low, k_low, v_low)
    grad = steps(lambda a, b: outer(a, b).astype(LOW), all_in, raw_grad)
    qkv_reduce = Reduce(at, as_columns(grad), "ge_ch___")
    in_part = steps(lambda a, b: matmul_back(a, b).astype(LOW), raw_grad, qkv_all)
    scatter = ScatterTokens(at, in_part)
    up_reduce.third()
    qkv_reduce.second()
    scatter.second()
    gate_spread = Spread(at, gate_reduce.fourth())
    o_reduce.third()
    in_grad = TokensOut(
        at, scatter.third(lambda a, b: (a + b).astype(LOW), residual_grad)
    )
    up_spread = Spread(at, up_reduce.fourth())
    qkv_reduce.third()
    gate_own = gate_spread.second(join_units)
    o_own = o_reduce.fourth()
    o_own = lax.ppermute(o_own, (trade, "l"), [(0, 0), (1, 2), (2, 1), (3, 3)])
    in_grad.second()

    def whole(vector):
        out = jnp.zeros((2, 2) + vector.shape, FULL)
        out = lax.dynamic_update_slice(out, vector[None, None], (at.x, at.l, 0))
        return features_back(out)

    gain_grads = scatter_gains(
        at,
        jnp.stack([whole(q_gain_grad[0]), whole(k_gain_grad[0]), attn_gain_grad, mlp_gain_grad]),
    )
    up_own = up_spread.second(join_units)
    qkv_spread = Spread(at, qkv_reduce.fourth())
    in_grad = in_grad.third()
    own_three = qkv_spread.second(join_three)
    shape = hidden_in.shape
    grads = own_three + [wide(o_own), gate_own, up_own, down_own]
    return (
        (layer_out.reshape(shape), in_grad.reshape(shape)) + tuple(grads) + tuple(gain_grads)
    )


def solution(mesh):
    dp, seq = mesh.shape["dp"], mesh.shape["seq"]
    split = Mesh(mesh.devices.reshape(dp // 8, 2, 2, 2, seq // 2, 2), AXES)
    dp_axes, seq_axes = AXES[:4], AXES[4:]
    tokens = P(dp_axes, seq_axes, None)
    matrix, vector = P(AXES, None), P(AXES)
    return jax.shard_map(
        on_device,
        mesh=split,
        in_specs=(tokens,)
        + (matrix,) * 4
        + (vector,) * 3
        + (matrix,) * 3
        + (vector, tokens),
        out_specs=(tokens,) * 2 + (matrix,) * 7 + (vector,) * 4,
        check_vma=False,
    )
```

```python
import math

import jax
import jax.numpy as jnp
from jax import lax
from jax.experimental import pallas as pl
from jax.experimental.pallas import tpu as pltpu
from jax.sharding import Mesh
from jax.sharding import PartitionSpec as P

HEADS = 16
EPSILON = 1e-06
ROPE_THETA = 500000.0
LOW = jnp.bfloat16
FULL = jnp.float32

AXES = ("g", "e", "x", "c", "h", "l")
SWAP = [(0, 1), (1, 0)]
BOTH = [(i, 3 - i) for i in range(4)]
VMEM_LIMIT = 56 * 1024 * 1024


BLOCK = 256

def dot_nt(a, b):
    return lax.dot_general(a, b, (((1,), (1,)), ((), ())), preferred_element_type=FULL)

def dot_nn(a, b):
    return lax.dot_general(a, b, (((1,), (0,)), ((), ())), preferred_element_type=FULL)

def dot_tn(a, b):
    return lax.dot_general(a, b, (((0,), (0,)), ((), ())), preferred_element_type=FULL)

def turn(tensor):
    return pltpu.roll(tensor, tensor.shape[1] // 2, 1)


def attend_kernel(q_raw, k_raw, v_raw, inverse, q_gain, k_gain, cosine, sine,
                  q_out, k_out, v_out, mixed):
    length, head_dim = q_raw.shape
    factor = 1.0 / math.sqrt(head_dim)
    block = min(BLOCK, length)

    def rope(raw, column, gain):
        normed = raw[...] * inverse[:, column : column + 1] * gain[...]
        return (normed * cosine[...] + turn(normed) * sine[...]).astype(LOW)

    q_out[...] = rope(q_raw, 0, q_gain)
    k_out[...] = rope(k_raw, 1, k_gain)
    v_out[...] = v_raw[...].astype(LOW)
    shape = (block, block)
    allowed = lax.broadcasted_iota(jnp.int32, shape, 1) <= lax.broadcasted_iota(jnp.int32, shape, 0)
    for start in range(0, length, block):
        here = slice(start, start + block)
        queries = q_out[here, :]
        near = jnp.where(allowed, dot_nt(queries, k_out[here, :]) * factor, -1e30)
        top = jnp.max(near, axis=1, keepdims=True)
        if start:
            far = dot_nt(queries, k_out[:start, :]) * factor
            top = jnp.maximum(top, jnp.max(far, axis=1, keepdims=True))
            far = jnp.exp(far - top)
        near = jnp.exp(near - top)
        total = jnp.sum(near, axis=1, keepdims=True)
        if start:
            total += jnp.sum(far, axis=1, keepdims=True)
        scale = 1.0 / total
        out = dot_nn((near * scale).astype(LOW), v_out[here, :])
        if start:
            out += dot_nn((far * scale).astype(LOW), v_out[:start, :])
        mixed[here, :] = out.astype(LOW)


def attend(raw, inverse, q_gain, k_gain, cosine, sine):
    length = raw.shape[0]
    head_dim = cosine.shape[1]
    width = q_gain.shape[1]
    heads = width // head_dim
    column = lambda shift: pl.BlockSpec((length, head_dim), lambda i: (0, i + shift * heads))
    whole = lambda v: pl.BlockSpec(v.shape, lambda i: (0, 0))
    gain = pl.BlockSpec((1, head_dim), lambda i: (0, i))
    out = jax.ShapeDtypeStruct((length, width), LOW)
    return pl.pallas_call(
        attend_kernel,
        grid=(heads,),
        in_specs=[column(0), column(1), column(2), whole(inverse), gain, gain, whole(cosine), whole(sine)],
        out_specs=[column(0)] * 4,
        out_shape=[out] * 4,
        compiler_params=pltpu.CompilerParams(vmem_limit_bytes=VMEM_LIMIT),
        cost_estimate=pl.CostEstimate(flops=0, bytes_accessed=0, transcendentals=0),
    )(raw, raw, raw, inverse, q_gain, k_gain, cosine, sine)


def attend_back_kernel(queries, keys, values, mixed_grad, q_raw, k_raw, inverse, q_gain, k_gain, cosine, sine,
                       q_grad, k_grad, v_grad, sums, q_gain_grad, k_gain_grad, k_total, v_total):
    length, head_dim = queries.shape
    factor = 1.0 / math.sqrt(head_dim)
    block = min(BLOCK, length)
    shape = (block, block)
    allowed = lax.broadcasted_iota(jnp.int32, shape, 0) <= lax.broadcasted_iota(jnp.int32, shape, 1)
    first = pl.program_id(0) == 0

    def unrope(grad, raw, column, gain, rows):
        pre = grad * cosine[rows, :] - turn(grad) * sine[rows, :]
        unit = raw[rows, :] * inverse[rows, column : column + 1]
        scaled = pre * gain[...]
        return scaled, jnp.sum(scaled * unit, axis=1, keepdims=True), jnp.sum(pre * unit, axis=0, keepdims=True)

    q_gain_total = jnp.zeros((1, head_dim), FULL)
    for start in range(0, length, block):
        here = slice(start, start + block)
        query, out_grad = queries[here, :], mixed_grad[here, :]
        near = jnp.where(allowed, dot_nt(keys[here, :], query) * factor, -1e30)
        top = jnp.max(near, axis=0, keepdims=True)
        if start:
            far = dot_nt(keys[:start, :], query) * factor
            top = jnp.maximum(top, jnp.max(far, axis=0, keepdims=True))
            far = jnp.exp(far - top)
        near = jnp.exp(near - top)
        total = jnp.sum(near, axis=0, keepdims=True)
        if start:
            total += jnp.sum(far, axis=0, keepdims=True)
        scale = 1.0 / total
        near = near * scale
        near_grad = dot_nt(values[here, :], out_grad)
        inner = jnp.sum(near * near_grad, axis=0, keepdims=True)
        if start:
            far = far * scale
            far_grad = dot_nt(values[:start, :], out_grad)
            inner += jnp.sum(far * far_grad, axis=0, keepdims=True)
        near_score = (near * (near_grad - inner) * factor).astype(LOW)
        grad = dot_tn(near_score, keys[here, :])
        k_total[here, :] = dot_nn(near_score, query)
        v_total[here, :] = dot_nn(near.astype(LOW), out_grad)
        if start:
            far_score = (far * (far_grad - inner) * factor).astype(LOW)
            grad += dot_tn(far_score, keys[:start, :])
            k_total[:start, :] += dot_nn(far_score, query)
            v_total[:start, :] += dot_nn(far.astype(LOW), out_grad)
        scaled, row_sum, gain_part = unrope(grad, q_raw, 0, q_gain, here)
        q_grad[here, :] = scaled
        q_gain_total += gain_part
        sums[here, 0:1] = jnp.where(first, row_sum, sums[here, 0:1] + row_sum)
    q_gain_grad[...] = q_gain_total
    scaled, row_sum, gain_part = unrope(k_total[...], k_raw, 1, k_gain, slice(None))
    k_grad[...] = scaled
    k_gain_grad[...] = gain_part
    sums[:, 1:2] = jnp.where(first, row_sum, sums[:, 1:2] + row_sum)
    v_grad[...] = v_total[...].astype(LOW)


def attend_back(queries, keys, values, mixed_grad, raw, inverse, q_gain, k_gain, cosine, sine):
    length, width = queries.shape
    head_dim = cosine.shape[1]
    heads = width // head_dim
    column = lambda shift: pl.BlockSpec((length, head_dim), lambda i: (0, i + shift * heads))
    whole = lambda v: pl.BlockSpec(v.shape, lambda i: (0, 0))
    gain = pl.BlockSpec((1, head_dim), lambda i: (0, i))
    wide = jax.ShapeDtypeStruct((length, width), FULL)
    vector = jax.ShapeDtypeStruct((1, width), FULL)
    return pl.pallas_call(
        attend_back_kernel,
        grid=(heads,),
        in_specs=[column(0)] * 4 + [column(0), column(1), whole(inverse), gain, gain, whole(cosine), whole(sine)],
        out_specs=[column(0)] * 3 + [pl.BlockSpec((length, 2), lambda i: (0, 0)), gain, gain],
        out_shape=[wide, wide, jax.ShapeDtypeStruct((length, width), LOW), jax.ShapeDtypeStruct((length, 2), FULL), vector, vector],
        scratch_shapes=[pltpu.VMEM((length, head_dim), FULL)] * 2,
        compiler_params=pltpu.CompilerParams(vmem_limit_bytes=VMEM_LIMIT),
        cost_estimate=pl.CostEstimate(flops=0, bytes_accessed=0, transcendentals=0),
    )(queries, keys, values, mixed_grad, raw, raw, inverse, q_gain, k_gain, cosine, sine)

def call(kernel, grid, inputs, outputs):
    out = pl.pallas_call(
        kernel,
        grid=grid,
        in_specs=[pl.BlockSpec(block, index) for _, block, index in inputs],
        out_specs=[pl.BlockSpec(block, index) for _, _, block, index in outputs],
        out_shape=[jax.ShapeDtypeStruct(shape, kind) for shape, kind, _, _ in outputs],
        compiler_params=pltpu.CompilerParams(vmem_limit_bytes=VMEM_LIMIT),
        cost_estimate=pl.CostEstimate(flops=0, bytes_accessed=0, transcendentals=0),
    )(*(v for v, _, _ in inputs))
    return out[0] if len(outputs) == 1 else out


def stay(array):
    return array, array.shape, lambda *i: (0,) * array.ndim


ATTN_TILE = 512


def feature_blocks(groups, rows):
    size = 8 * rows
    for g in range(groups):
        for k in range(4):
            start = (g * 4 + k) * size
            yield slice(start, start + size), slice(g * 8, g * 8 + 8), k


def project(all_in, weights):
    length = all_in.shape[0]
    eight, four, rows, _ = weights.shape
    tile = ATTN_TILE

    def kernel(a, w, out):
        total = jnp.zeros(out.shape, FULL)
        for columns, pieces, k in feature_blocks(eight // 8, rows):
            total += dot_nn(a[:, columns], w[pieces, k].reshape(8 * rows, tile))
        out[...] = total

    return call(
        kernel,
        (3,),
        [stay(all_in), (weights, (eight, four, rows, tile), lambda j: (0, 0, 0, j + 1))],
        [((length, 3 * tile), FULL, (length, tile), lambda j: (0, j))],
    )


def project_back(raw_grad, weights):
    length = raw_grad.shape[0]
    eight, four, rows, columns = weights.shape
    tile = ATTN_TILE
    size = 8 * rows

    def kernel(a, w, out):
        right = w[:, 0, :, tile : 4 * tile].reshape(size, 3 * tile)
        out[...] = dot_nt(a[...], right).astype(LOW)

    return call(
        kernel,
        (eight // 8 * 4,),
        [
            stay(raw_grad),
            (weights, (8, 1, rows, columns), lambda j: (j // 4, j % 4, 0, 0)),
        ],
        [((length, eight // 8 * 4 * size), LOW, (length, size), lambda j: (0, j))],
    )


def mix_out(mixed, weights):
    length, features = mixed.shape
    eight, four, rows, _ = weights.shape
    tile = ATTN_TILE

    def kernel(a, w, out):
        out[...] = dot_nn(a[...], w[:, 0].reshape(features, tile)).astype(LOW)

    return call(
        kernel,
        (four,),
        [stay(mixed), (weights, (eight, 1, rows, tile), lambda j: (0, j, 0, 0))],
        [((length, four * tile), LOW, (length, tile), lambda j: (0, j))],
    )


def mix_out_back(attn_grad, weights):
    length, width = attn_grad.shape
    eight, four, rows, _ = weights.shape
    tile = ATTN_TILE
    features = eight * rows
    part = min(length, 256)

    def kernel(a, w, out):
        total = jnp.zeros(out.shape, FULL)
        for k in range(four):
            right = w[:, k].reshape(features, tile)
            total += dot_nt(a[:, k * tile : (k + 1) * tile], right)
        out[...] = total.astype(LOW)

    return call(
        kernel,
        (length // part,),
        [
            (attn_grad, (part, width), lambda j: (j, 0)),
            (weights, (eight, four, rows, tile), lambda j: (0, 0, 0, 0)),
        ],
        [((length, features), LOW, (part, features), lambda j: (j, 0))],
    )


def gated(mlp_in, weights):
    length = mlp_in.shape[0]
    eight, _, four, rows, count = weights.shape
    tile = min(count, 512)

    def kernel(a, gate_w, up_w, hidden, gate, up):
        both = []
        for w in (gate_w, up_w):
            total = jnp.zeros(gate.shape, FULL)
            for columns, pieces, k in feature_blocks(eight // 8, rows):
                total += dot_nn(a[:, columns], w[pieces, 0, k].reshape(8 * rows, tile))
            both.append(total)
        gate[...], up[...] = both
        hidden[...] = (both[0] * jax.nn.sigmoid(both[0]) * both[1]).astype(LOW)

    weight = lambda i: (
        weights, (eight, 1, four, rows, tile), lambda j: (0, i, 0, 0, j),
    )
    cut = ((length, tile), lambda j: (0, j))
    shape = (length, count)
    return call(
        kernel,
        (count // tile,),
        [stay(mlp_in), weight(0), weight(1)],
        [(shape, LOW) + cut, (shape, FULL) + cut, (shape, FULL) + cut],
    )


def branch_out(hidden, weights):
    length, units = hidden.shape
    eight, _, four, rows, width = weights.shape
    tile = min(width, 512)

    def kernel(a, w, out):
        out[...] = dot_nn(a[...], w[:, 0].reshape(units, tile)).astype(LOW)

    return call(
        kernel,
        (width // tile,),
        [
            stay(hidden),
            (weights, (eight, 1, four, rows, tile), lambda j: (0, 2, 0, 0, j)),
        ],
        [((length, width), LOW, (length, tile), lambda j: (0, j))],
    )


def gated_back(branch_rows, weights, gate_raw, up_raw):
    length, units = gate_raw.shape
    eight, _, four, rows, width = weights.shape
    tile = min(units, 512)
    pieces = tile // (four * rows)

    def kernel(a, w, gate, up, out):
        hidden_grad = dot_nt(a[...], w[:, 0].reshape(tile, width))
        raw = gate[...]
        sigmoid = jax.nn.sigmoid(raw)
        slope = sigmoid * (1.0 + raw * (1.0 - sigmoid))
        out[0] = (hidden_grad * up[...] * slope).astype(LOW)
        out[1] = (hidden_grad * raw * sigmoid).astype(LOW)

    cut = ((length, tile), lambda j: (0, j))
    return call(
        kernel,
        (units // tile,),
        [
            stay(branch_rows),
            (weights, (pieces, 1, four, rows, width), lambda j: (j, 2, 0, 0, 0)),
            (gate_raw,) + cut,
            (up_raw,) + cut,
        ],
        [((2, length, units), LOW, (2, length, tile), lambda j: (0, 0, j))],
    )


def input_back(grads, weights):
    _, length, units = grads.shape
    eight, _, four, rows, _ = weights.shape
    size = 8 * rows

    def kernel(a, gate_w, up_w, out):
        gate = dot_nt(a[0], gate_w[:, 0, 0].reshape(size, units))
        up = dot_nt(a[1], up_w[:, 0, 0].reshape(size, units))
        out[...] = (gate + up).astype(LOW)

    weight = lambda i: (
        weights, (8, 1, 1, rows, units), lambda j: (j // 4, i, j % 4, 0, 0),
    )
    return call(
        kernel,
        (eight // 8 * four,),
        [stay(grads), weight(0), weight(1)],
        [((length, eight // 8 * four * size), LOW, (length, size), lambda j: (0, j))],
    )


def down_grad(hidden, branch_rows, groups, rows):
    length, units = hidden[0].shape
    width = branch_rows[0].shape[1]
    run = 4 * rows
    many = 1 if run % 128 == 0 else 4
    shape = (4, groups, run, width)

    def kernel(a, b, c, d, out):
        total = dot_tn(a[...], b[...]) + dot_tn(c[...], d[...])
        out[...] = total.astype(LOW).reshape(out.shape)

    cut = ((length, many * run), lambda g, j: (0, g * (4 // many) + j))
    return call(
        kernel,
        (groups, 4 // many),
        [
            (hidden[0],) + cut,
            stay(branch_rows[0]),
            (hidden[1],) + cut,
            stay(branch_rows[1]),
        ],
        [(shape, LOW, (many, 1, run, width), lambda g, j: (j, g, 0, 0))],
    )


def lay_features(total, out, many, rows):
    for i in range(many):
        for j in range(4):
            start = (i * 4 + j) * rows
            yield (j, i), total[start : start + rows]


def units_grad(mlp_in, grads, groups, rows):
    length = mlp_in[0].shape[0]
    units = grads[0].shape[2]
    run = 4 * rows
    many = 1 if run % 128 == 0 else 4
    shape = (4, 2, groups, 4, rows, units)

    def kernel(a, b, c, d, out):
        total = (dot_tn(a[...], b[0]) + dot_tn(c[...], d[0])).astype(LOW)
        for (j, i), part in lay_features(total, out, many, rows):
            out[j, 0, 0, i] = part

    cut = ((length, many * run), lambda i, g, j: (0, g * (4 // many) + j))
    right = ((1, length, units), lambda i, g, j: (i, 0, 0))
    return call(
        kernel,
        (2, groups, 4 // many),
        [
            (mlp_in[0],) + cut,
            (grads[0],) + right,
            (mlp_in[1],) + cut,
            (grads[1],) + right,
        ],
        [
            (
                shape,
                LOW,
                (4, 1, 1, many, rows, units),
                lambda i, g, j: (0, i, g, j, 0, 0),
            )
        ],
    )


def attention_grad(all_in, raw_grad, mixed, attn_grad, groups, rows):
    length = all_in[0].shape[0]
    tile = ATTN_TILE
    run = 4 * rows
    many = 1 if run % 128 == 0 else 4
    shape = (4, groups, 4, rows, 4 * tile)

    def kernel(a, b, c, d, e, f, p, q, out):
        total = (dot_tn(a[...], b[...]) + dot_tn(c[...], d[...])).astype(LOW)
        for (j, i), part in lay_features(total, out, many, rows):
            out[j, 0, i, :, tile:] = part
        total = (dot_tn(e[0], f[...]) + dot_tn(p[0], q[...])).astype(LOW)
        for i in range(many):
            for j in range(4):
                part = total[j * rows : (j + 1) * rows, i * tile : (i + 1) * tile]
                out[j, 0, i, :, :tile] = part

    cut = ((length, many * run), lambda g, j: (0, g * (4 // many) + j))
    left = ((1, length, run), lambda g, j: (g, 0, 0))
    right = ((length, many * tile), lambda g, j: (0, j))
    return call(
        kernel,
        (groups, 4 // many),
        [
            (all_in[0],) + cut,
            stay(raw_grad[0]),
            (all_in[1],) + cut,
            stay(raw_grad[1]),
            (mixed[0],) + left,
            (attn_grad[0],) + right,
            (mixed[1],) + left,
            (attn_grad[1],) + right,
        ],
        [(shape, LOW, (4, 1, many, rows, 4 * tile), lambda g, j: (0, g, j, 0, 0))],
    )


def wide(value):
    return value.astype(FULL)


def tie(values, others):
    if not others:
        return tuple(values)
    return lax.optimization_barrier(tuple(values) + tuple(others))[: len(values)]


def hold(value, *others):
    def kernel(*refs):
        pass

    anywhere = pl.BlockSpec(memory_space=pl.ANY)
    return pl.pallas_call(
        kernel,
        in_specs=[anywhere] * (1 + len(others)),
        out_specs=anywhere,
        out_shape=jax.ShapeDtypeStruct(value.shape, value.dtype),
        input_output_aliases={0: 0},
        cost_estimate=pl.CostEstimate(flops=0, bytes_accessed=0, transcendentals=0),
    )(value, *others)


class Steps:
    def __init__(self):
        self.last = ()

    def wait(self, *values):
        self.last += tuple(jax.tree.leaves(values))

    def __call__(self, step, *inputs):
        flat, tree = jax.tree.flatten(inputs)
        out = step(*tree.unflatten(tie(flat, self.last)))
        self.last = tuple(jax.tree.leaves(out))
        return out


class Links:
    def __init__(self, steps):
        self.steps = steps

    def send(self, value, axes, pairs):
        (value,) = tie((value,), self.steps.last)
        return lax.ppermute(value, axes, pairs)

    def swap(self, value, axis):
        return self.send(value, axis, SWAP)

    def swap_both(self, value, first, second):
        return self.send(value, (first, second), BOTH)


def swap(value, axis):
    return lax.ppermute(value, axis, SWAP)


def pick(value, places):
    starts = [0] * value.ndim
    sizes = list(value.shape)
    for dim, place in places.items():
        starts[dim] = place
        sizes[dim] = 1
    taken = lax.dynamic_slice(value, starts, sizes)
    return taken.reshape([s for d, s in enumerate(value.shape) if d not in places])


def put(out, parts):
    for value, starts in parts:
        out = lax.dynamic_update_slice(out, value, starts)
    return out


class Place:
    def __init__(self):
        self.g, self.e, self.x, self.c, self.h, self.l = (lax.axis_index(a) for a in AXES)
        self.groups = lax.axis_size("g")
        self.steps = Steps()
        self.links = Links(self.steps)


class Spread:
    def __init__(self, at, part, inputs, first="e", second="x"):
        self.at, self.places = at, (getattr(at, first), getattr(at, second))
        a, b = self.places

        def start(*inputs):
            return tuple(part(i, j, *inputs) for i in (a, 1 - a) for j in (b, 1 - b))

        self.mine, for_b, for_a, far = at.steps(start, *inputs)
        self.from_a = at.links.swap(for_a, first)
        self.from_b = at.links.swap(for_b, second)
        self.far = at.links.swap_both(far, first, second)

    def second(self, lay):
        a, b = self.places

        def join(mine, from_a, from_b, far):
            return lay(
                [(mine, a, b), (from_a, 1 - a, b), (from_b, a, 1 - b), (far, 1 - a, 1 - b)]
            )

        return self.at.steps(join, self.mine, self.from_a, self.from_b, self.far)


def one_of(i, j, parts):
    return pick(parts, {0: i, 1: j})


def lay_all(parts):
    shape = parts[0][0].shape
    out = jnp.zeros((2, 2) + shape, parts[0][0].dtype)
    tail = (0,) * len(shape)
    return put(out, [(v.reshape((1, 1) + shape), (i, j) + tail) for v, i, j in parts])


class TokensIn:
    def __init__(self, at, rows):
        self.at = at
        self.spread = Spread(at, one_of, [rows.reshape(2, 2, -1, rows.shape[1])])

    def second(self):
        self.spread = Spread(self.at, one_of, [self.spread.second(lay_all)], "h", "l")

    def third(self):
        def lay(parts):
            out = lay_all(parts)
            return out.reshape((4,) + out.shape[2:])

        return self.spread.second(lay)


class TokensOut:
    def __init__(self, at, blocks):
        self.at = at
        blocks = blocks.reshape((2, 2) + blocks.shape[1:])
        self.spread = Spread(at, one_of, [blocks], "h", "l")

    def second(self):
        self.spread = Spread(self.at, one_of, [self.spread.second(lay_all)])

    def third(self):
        def lay(parts):
            out = lay_all(parts)
            return out.reshape(-1, out.shape[-1])

        return self.spread.second(lay)


class GatherTokens:
    def __init__(self, at, blocks):
        self.at, self.blocks = at, blocks
        self.from_e = at.links.swap(blocks, "e")
        self.from_x = at.links.swap(blocks, "x")

    def second(self):
        at = self.at
        half_e, half_x = at.steps(lambda a, b: (a[:2], b[2:]), self.from_e, self.from_x)
        self.far_0 = at.links.swap(half_e, "x")
        self.far_1 = at.links.swap(half_x, "e")
        four, count, width = self.blocks.shape
        cut = (four, 1, 1, count, width)

        def near(blocks, from_x, from_e):
            out = jnp.zeros((four, 2, 2, count, width), blocks.dtype)
            parts = [
                (blocks.reshape(cut), (0, at.e, at.x, 0, 0)),
                (from_x.reshape(cut), (0, at.e, 1 - at.x, 0, 0)),
                (from_e.reshape(cut), (0, 1 - at.e, at.x, 0, 0)),
            ]
            return put(out, parts)

        self.out = at.steps(near, self.blocks, self.from_x, self.from_e)

    def third(self):
        at = self.at
        four, count, width = self.blocks.shape
        cut = (2, 1, 1, count, width)

        def far(out, far_0, far_1):
            parts = [
                (far_0.reshape(cut), (0, 1 - at.e, 1 - at.x, 0, 0)),
                (far_1.reshape(cut), (2, 1 - at.e, 1 - at.x, 0, 0)),
            ]
            return put(out, parts).reshape(-1, width)

        return at.steps(far, self.out, self.far_0, self.far_1)


class ScatterTokens:
    def __init__(self, at, rows):
        self.at = at
        total, width = rows.shape
        self.parts = rows.reshape(4, 2, 2, total // 16, width)

        def start(parts):
            far = pick(parts, {1: 1 - at.e, 2: 1 - at.x})
            return far[:2], far[2:]

        far_0, far_1 = at.steps(start, self.parts)
        self.for_e_0 = at.links.swap(far_0, "x")
        self.for_x_1 = at.links.swap(far_1, "e")

    def second(self):
        at = self.at

        def add(parts, for_e_0, for_x_1):
            for_e = pick(parts, {1: 1 - at.e, 2: at.x})
            for_x = pick(parts, {1: at.e, 2: 1 - at.x})
            for_e_0 = (wide(for_e[:2]) + wide(for_e_0)).astype(LOW)
            for_x_1 = (wide(for_x[2:]) + wide(for_x_1)).astype(LOW)
            return jnp.concatenate([for_e_0, for_e[2:]]), jnp.concatenate([for_x[:2], for_x_1])

        for_e, for_x = at.steps(add, self.parts, self.for_e_0, self.for_x_1)
        self.from_e = at.links.swap(for_e, "e")
        self.from_x = at.links.swap(for_x, "x")

    def third(self, step, *inputs):
        at = self.at

        def add(parts, from_e, from_x, *inputs):
            mine = pick(parts, {1: at.e, 2: at.x})
            return step(wide(mine) + wide(from_e) + wide(from_x), *inputs)

        return at.steps(add, self.parts, self.from_e, self.from_x, *inputs)


def sum_chips(value):
    far = lax.ppermute(value, ("e", "x"), BOTH)
    return value + swap(value, "x") + swap(value, "e") + far


def gather(at, piece, *others):
    (piece,) = tie((piece,), at.steps.last + others)
    return lax.all_gather(piece, ("g", "c", "h", "l"), axis=0)


def scatter(at, value, *others):
    (value,) = tie((value,), at.steps.last + others)
    value = lax.psum_scatter(value, ("h", "l"), scatter_dimension=0)
    return value


def scatter_groups(at, value, dim):
    if at.groups == 1:
        return value.reshape([n for d, n in enumerate(value.shape) if d != dim])
    return lax.psum_scatter(value, "g", scatter_dimension=dim)


def halves(value, core, runs):
    rows, count = value.shape
    each = count // (2 * runs)

    def of(place):
        parts = [
            lax.dynamic_slice(value, (0, (2 * k + place) * each), (rows, each))
            for k in range(runs)
        ]
        return jnp.concatenate(parts, axis=1)

    return of(core), of(1 - core)


class ScatterGains:
    def __init__(self, at, grads):
        self.at = at
        value = grads.reshape(grads.shape[0], at.groups, 2, 2, 2, 2, 2, -1)
        if at.groups > 1:
            value = lax.psum_scatter(value, "g", scatter_dimension=1, tiled=True)
        self.value = value.reshape(value.shape[:1] + value.shape[2:])
        self.axes = ["e", "x", "c", "h", "l"]
        self.start()

    def start(self):
        place = getattr(self.at, self.axes[0])
        self.kept, send = self.at.steps(
            lambda v: (pick(v, {1: place}), pick(v, {1: 1 - place})), self.value
        )
        self.got = self.at.links.swap(send, self.axes.pop(0))

    def more(self):
        self.value = self.at.steps(lambda a, b: a + b, self.kept, self.got)
        if self.axes:
            self.start()
        return self.value


def rope_tables(places, head_dim):
    half_dim = head_dim // 2
    inverse = jnp.power(
        jnp.float32(ROPE_THETA), -(jnp.arange(half_dim, dtype=FULL) * 2.0 / head_dim)
    )
    angles = places.astype(FULL)[:, None] * inverse[None, :]
    sine = jnp.sin(angles)
    cosine = jnp.cos(angles)
    return (
        jnp.concatenate([cosine, cosine], axis=-1),
        jnp.concatenate([-sine, sine], axis=-1),
    )


def norm_forward(tensor, gain_vec):
    inverse = lax.rsqrt(jnp.mean(tensor * tensor, axis=-1, keepdims=True) + EPSILON)
    unit = tensor * inverse
    return unit * gain_vec, unit, inverse


def norm_backward(grad_in, unit, inverse, gain_vec):
    axes = tuple(range(grad_in.ndim - 1))
    gain_grad = jnp.sum(grad_in * unit, axis=axes)
    unit_grad = grad_in * gain_vec
    inner = jnp.mean(unit_grad * unit, axis=-1, keepdims=True)
    return inverse * (unit_grad - unit * inner), gain_grad


def on_device(
    hidden_in,
    q_weight,
    k_weight,
    v_weight,
    o_weight,
    q_gain,
    k_gain,
    attn_gain,
    gate_weight,
    up_weight,
    down_weight,
    mlp_gain,
    out_grad,
):
    at = Place()
    steps = at.steps
    batch, rows_here, width = hidden_in.shape
    head_dim = width // HEADS
    length = batch * rows_here * 4
    rows_owned = q_weight.shape[0]
    groups = at.groups
    ff_block = down_weight.shape[0]

    assert head_dim % (8 * rows_owned) == 0 or (8 * rows_owned) % head_dim == 0
    assert ff_block == 4 * rows_owned

    def columns_of(e, x, weight):
        rows, count = weight.shape
        part = count // (4 * groups)
        each = [
            lax.dynamic_slice(weight, (0, ((g * 2 + e) * 2 + x) * part), (rows, part))
            for g in range(groups)
        ]
        return jnp.concatenate(each, axis=1)

    def lay_columns(parts):
        rows, count = parts[0][0].shape
        part = count // groups
        out = jnp.zeros((rows, 4 * count), FULL)
        for value, e, x in parts:
            for g in range(groups):
                piece = wide(value[:, g * part : (g + 1) * part])
                out = lax.dynamic_update_slice(out, piece, (0, ((g * 2 + e) * 2 + x) * part))
        return out

    quarter = width // 4

    def columns_of_attention(e, x, q, k, v, o, gains):
        three = [columns_of(e, x, w) for w in (q, k, v)]
        return jnp.concatenate(three + [gains], axis=1)

    def lay_attention(parts):
        tail = lay_all(parts)
        tail = tail.reshape((4,) + tail.shape[2:])
        runs = jnp.stack([o_weight[:, k * quarter : (k + 1) * quarter] for k in range(4)])
        return jnp.concatenate([runs, tail], axis=2)

    def lay_four(parts):
        out = lay_all(parts)
        return out.reshape((4,) + out.shape[2:])

    def lay_three(parts):
        return tuple(
            lay_columns([(v[:, i * quarter : (i + 1) * quarter], e, x) for v, e, x in parts])
            for i in range(3)
        )

    def here(vector):
        return pick(vector.reshape(groups, 2, 2, -1), {1: at.e, 2: at.x}).reshape(1, -1)

    def whole(vector):
        out = jnp.zeros((groups, 2, 2, vector.size // groups), FULL)
        part = vector.reshape(groups, 1, 1, -1)
        return lax.dynamic_update_slice(out, part, (0, at.e, at.x, 0)).reshape(-1)

    def pair(halved, core_sent):
        return halved, at.links.swap(core_sent, "c")

    gains = jnp.stack([q_gain, k_gain, attn_gain, mlp_gain], axis=1)
    gains = jnp.pad(gains, ((0, 0), (0, 124)))
    attn_spread = Spread(
        at, columns_of_attention, [q_weight, k_weight, v_weight, o_weight, gains]
    )
    own = TokensIn(at, hidden_in.reshape(-1, width))
    gate_spread = Spread(at, columns_of, [gate_weight])
    up_spread = Spread(at, columns_of, [up_weight])
    attn_all = gather(at, attn_spread.second(lay_attention))
    own.second()
    cosine, sine = steps(lambda n: rope_tables(n, head_dim), jnp.arange(length))
    gate_mine = gate_spread.second(lay_four)
    up_mine = up_spread.second(lay_four)
    mlp_mine = steps(
        lambda *v: jnp.stack(v), gate_mine, up_mine, down_weight.reshape((4, -1, width))
    )
    mlp_all = gather(at, mlp_mine)
    own_in = own.third()
    all_in = GatherTokens(at, own_in)
    all_in.second()
    all_in = all_in.third()
    all_in_half = pair(*steps(lambda v: halves(v, at.c, 4 * groups), all_in))
    steps.wait(all_in_half)

    def gains_of(weights):
        value = wide(weights[..., -128:-124]).reshape(groups, 8, 4, rows_owned, 4)
        return value.transpose(4, 0, 2, 1, 3).reshape(4, -1)

    gains = steps(gains_of, attn_all)
    q_gain_here, k_gain_here = here(gains[0]), here(gains[1])
    attn_gain_all, mlp_gain_all = gains[2], gains[3]

    def squares_of(raw):
        q_raw, k_raw = jnp.split(raw[:, : 2 * quarter], 2, axis=1)
        return jnp.stack([jnp.sum(q_raw * q_raw, -1), jnp.sum(k_raw * k_raw, -1)])

    raw = steps(project, all_in, attn_all)
    squares = sum_chips(steps(squares_of, raw))
    inverse = steps(lambda s: lax.rsqrt(s / width + EPSILON).T, squares)
    queries, keys, values, mixed = steps(
        attend, raw, inverse, q_gain_here, k_gain_here, cosine, sine
    )
    attn_part = steps(mix_out, mixed, attn_all)
    attn_out = ScatterTokens(at, attn_part)

    def halve_mixed(mixed):
        return [
            v.reshape(length, groups, -1).swapaxes(0, 1) for v in halves(mixed, at.c, groups)
        ]

    mixed_half = pair(*steps(halve_mixed, mixed))
    steps.wait(mixed_half)
    attn_out.second()

    def after_attention(attn_out, own_in, gain):
        normed, unit, inverse = norm_forward(attn_out, gain)
        residual = wide(own_in) + normed
        return residual.astype(LOW), residual, unit, inverse

    residual_low, residual, attn_unit, attn_inverse = attn_out.third(
        after_attention, own_in, attn_gain_all
    )

    mlp_in = GatherTokens(at, residual_low)
    mlp_in.second()
    mlp_in = mlp_in.third()
    mlp_in_half = pair(*steps(lambda v: halves(v, at.c, 4 * groups), mlp_in))
    steps.wait(mlp_in_half)
    hidden, gate_raw, up_raw = steps(gated, mlp_in, mlp_all)
    branch_part = steps(branch_out, hidden, mlp_all)
    branch = ScatterTokens(at, branch_part)
    top = TokensIn(at, out_grad.reshape(-1, width))
    hidden_half = pair(*steps(lambda v: halves(v, at.c, groups), hidden))
    steps.wait(hidden_half)
    branch.second()
    top.second()
    own_top = top.third()

    def after_mlp(branch, residual, own_top, gain):
        normed, unit, inverse = norm_forward(branch, gain)
        grad, gain_grad = norm_backward(wide(own_top), unit, inverse, gain)
        return grad.astype(LOW), (residual + normed).astype(LOW), gain_grad

    branch_low, own_out, mlp_gain_grad = branch.third(
        after_mlp, residual, own_top, mlp_gain_all
    )

    branch_rows = GatherTokens(at, branch_low)
    layer_out = TokensOut(at, own_out)
    branch_rows.second()
    branch_rows = branch_rows.third()
    branch_rows = (branch_rows, at.links.swap(branch_rows, "c"))
    grad = steps(lambda a, b: down_grad(a, b, groups, rows_owned), hidden_half, branch_rows)
    down_own = scatter(at, grad)
    unit_grads = steps(gated_back, branch_rows[0], mlp_all, gate_raw, up_raw)
    unit_grads = (unit_grads, at.links.swap(unit_grads, "c"))
    input_part = steps(input_back, unit_grads[0], mlp_all)
    input_part = ScatterTokens(at, input_part)
    grad = steps(lambda a, b: units_grad(a, b, groups, rows_owned), mlp_in_half, unit_grads)
    units_own = scatter(at, grad)
    input_part.second()
    layer_out.second()

    def before_attention(input_grad, own_top, unit, inverse, gain):
        residual_grad = wide(own_top) + input_grad
        grad, gain_grad = norm_backward(residual_grad, unit, inverse, gain)
        return grad.astype(LOW), residual_grad, gain_grad

    attn_grad, residual_grad, attn_gain_grad = input_part.third(
        before_attention, own_top, attn_unit, attn_inverse, attn_gain_all
    )

    attn_low = GatherTokens(at, attn_grad)
    layer_out = layer_out.third()
    attn_low.second()
    attn_low = attn_low.third()
    attn_low = (attn_low, swap(attn_low, "c"))
    mixed_grad = steps(mix_out_back, attn_low[0], attn_all)
    q_scaled, k_scaled, v_low, inner, q_gain_grad, k_gain_grad = steps(
        attend_back, queries, keys, values, mixed_grad, raw, inverse,
        q_gain_here, k_gain_here, cosine, sine,
    )
    inner = sum_chips(steps(lambda v: v.T / width, inner))

    def before_project(raw, inverse, q_scaled, k_scaled, v_low, inner):
        q_raw, k_raw = jnp.split(raw[:, : 2 * quarter], 2, axis=1)
        inner = inner.T
        grads = []
        for i, (part, scaled) in enumerate([(q_raw, q_scaled), (k_raw, k_scaled)]):
            each = inverse[:, i : i + 1]
            grads.append((each * (scaled - part * each * inner[:, i : i + 1])).astype(LOW))
        return jnp.concatenate(grads + [v_low], axis=1)

    raw_grad = steps(before_project, raw, inverse, q_scaled, k_scaled, v_low, inner)
    raw_grad = (raw_grad, swap(raw_grad, "c"))
    in_part = steps(project_back, raw_grad[0], attn_all)
    in_part = ScatterTokens(at, in_part)
    attn_grad_part = steps(
        lambda *v: attention_grad(*v, groups, rows_owned),
        all_in_half, raw_grad, mixed_half, attn_low,
    )
    in_part.second()
    gains = ScatterGains(
        at,
        jnp.stack([whole(q_gain_grad), whole(k_gain_grad), attn_gain_grad, mlp_gain_grad]),
    )
    in_grad = in_part.third(lambda a, b: (a + b).astype(LOW), residual_grad)
    in_grad = TokensOut(at, in_grad)
    gains.more()
    gains.more()
    attn_own = scatter(at, hold(attn_grad_part, units_own))
    units_own = scatter_groups(at, units_own, 1)
    gate_spread = Spread(at, one_of, [units_own[0].reshape(2, 2, rows_owned, -1)])
    up_spread = Spread(at, one_of, [units_own[1].reshape(2, 2, rows_owned, -1)])
    gains.more()
    gate_own = gate_spread.second(lay_columns)
    up_own = up_spread.second(lay_columns)
    in_grad.second()
    gains.more()
    gains = gains.more()
    attn_own = scatter_groups(at, attn_own, 0)
    attn_spread = Spread(
        at, one_of, [attn_own[..., quarter:].reshape(2, 2, rows_owned, -1)]
    )
    o_own = wide(jnp.concatenate([attn_own[k, :, :quarter] for k in range(4)], axis=1))
    in_grad = in_grad.third()
    own_three = list(attn_spread.second(lay_three))
    down_own = wide(scatter_groups(at, down_own, 0))
    shape = hidden_in.shape
    grads = own_three + [o_own, gate_own, up_own, down_own]
    return (layer_out.reshape(shape), in_grad.reshape(shape)) + tuple(grads) + tuple(gains)


def solution(mesh):
    dp, seq = mesh.shape["dp"], mesh.shape["seq"]
    split = Mesh(mesh.devices.reshape(dp // 8, 2, 2, 2, seq // 2, 2), AXES)
    dp_axes, seq_axes = AXES[:4], AXES[4:]
    tokens = P(dp_axes, seq_axes, None)
    matrix, vector = P(AXES, None), P(AXES)
    return jax.shard_map(
        on_device,
        mesh=split,
        in_specs=(tokens,)
        + (matrix,) * 4
        + (vector,) * 3
        + (matrix,) * 3
        + (vector, tokens),
        out_specs=(tokens,) * 2 + (matrix,) * 7 + (vector,) * 4,
        check_vma=False,
    )
```

```python
import math

import jax
import jax.numpy as jnp
from jax import lax
from jax.experimental import pallas as pl
from jax.experimental.pallas import tpu as pltpu
from jax.sharding import Mesh
from jax.sharding import PartitionSpec as P

HEADS = 16
EPSILON = 1e-06
ROPE_THETA = 500000.0
LOW = jnp.bfloat16
FULL = jnp.float32

AXES = ("g", "e", "x", "c", "h", "l")
SWAP = [(0, 1), (1, 0)]
BOTH = [(i, 3 - i) for i in range(4)]
VMEM_LIMIT = 56 * 1024 * 1024


BLOCK = 256

def dot_nt(a, b):
    return lax.dot_general(a, b, (((1,), (1,)), ((), ())), preferred_element_type=FULL)

def dot_nn(a, b):
    return lax.dot_general(a, b, (((1,), (0,)), ((), ())), preferred_element_type=FULL)

def dot_tn(a, b):
    return lax.dot_general(a, b, (((0,), (0,)), ((), ())), preferred_element_type=FULL)

def turn(tensor):
    return pltpu.roll(tensor, tensor.shape[1] // 2, 1)


def attend_kernel(q_raw, k_raw, v_raw, inverse, q_gain, k_gain, cosine, sine,
                  q_out, k_out, v_out, mixed):
    length, head_dim = q_raw.shape
    factor = 1.0 / math.sqrt(head_dim)
    block = min(BLOCK, length)

    def rope(raw, column, gain):
        normed = raw[...] * inverse[:, column : column + 1] * gain[...]
        return (normed * cosine[...] + turn(normed) * sine[...]).astype(LOW)

    q_out[...] = rope(q_raw, 0, q_gain)
    k_out[...] = rope(k_raw, 1, k_gain)
    v_out[...] = v_raw[...].astype(LOW)
    shape = (block, block)
    allowed = lax.broadcasted_iota(jnp.int32, shape, 1) <= lax.broadcasted_iota(jnp.int32, shape, 0)
    for start in range(0, length, block):
        here = slice(start, start + block)
        queries = q_out[here, :]
        near = jnp.where(allowed, dot_nt(queries, k_out[here, :]) * factor, -1e30)
        top = jnp.max(near, axis=1, keepdims=True)
        if start:
            far = dot_nt(queries, k_out[:start, :]) * factor
            top = jnp.maximum(top, jnp.max(far, axis=1, keepdims=True))
            far = jnp.exp(far - top)
        near = jnp.exp(near - top)
        total = jnp.sum(near, axis=1, keepdims=True)
        if start:
            total += jnp.sum(far, axis=1, keepdims=True)
        scale = 1.0 / total
        out = dot_nn((near * scale).astype(LOW), v_out[here, :])
        if start:
            out += dot_nn((far * scale).astype(LOW), v_out[:start, :])
        mixed[here, :] = out.astype(LOW)


def attend(raw, inverse, q_gain, k_gain, cosine, sine):
    length = raw.shape[0]
    head_dim = cosine.shape[1]
    width = q_gain.shape[1]
    heads = width // head_dim
    column = lambda shift: pl.BlockSpec((length, head_dim), lambda i: (0, i + shift * heads))
    whole = lambda v: pl.BlockSpec(v.shape, lambda i: (0, 0))
    gain = pl.BlockSpec((1, head_dim), lambda i: (0, i))
    out = jax.ShapeDtypeStruct((length, width), LOW)
    return pl.pallas_call(
        attend_kernel,
        grid=(heads,),
        in_specs=[column(0), column(1), column(2), whole(inverse), gain, gain, whole(cosine), whole(sine)],
        out_specs=[column(0)] * 4,
        out_shape=[out] * 4,
        compiler_params=pltpu.CompilerParams(vmem_limit_bytes=VMEM_LIMIT),
        cost_estimate=pl.CostEstimate(flops=0, bytes_accessed=0, transcendentals=0),
    )(raw, raw, raw, inverse, q_gain, k_gain, cosine, sine)


def attend_back_kernel(queries, keys, values, mixed_grad, q_raw, k_raw, inverse, q_gain, k_gain, cosine, sine,
                       q_grad, k_grad, v_grad, sums, q_gain_grad, k_gain_grad, k_total, v_total):
    length, head_dim = queries.shape
    factor = 1.0 / math.sqrt(head_dim)
    block = min(BLOCK, length)
    shape = (block, block)
    allowed = lax.broadcasted_iota(jnp.int32, shape, 0) <= lax.broadcasted_iota(jnp.int32, shape, 1)
    first = pl.program_id(0) == 0

    def unrope(grad, raw, column, gain, rows):
        pre = grad * cosine[rows, :] - turn(grad) * sine[rows, :]
        unit = raw[rows, :] * inverse[rows, column : column + 1]
        scaled = pre * gain[...]
        return scaled, jnp.sum(scaled * unit, axis=1, keepdims=True), jnp.sum(pre * unit, axis=0, keepdims=True)

    q_gain_total = jnp.zeros((1, head_dim), FULL)
    for start in range(0, length, block):
        here = slice(start, start + block)
        query, out_grad = queries[here, :], mixed_grad[here, :]
        near = jnp.where(allowed, dot_nt(keys[here, :], query) * factor, -1e30)
        top = jnp.max(near, axis=0, keepdims=True)
        if start:
            far = dot_nt(keys[:start, :], query) * factor
            top = jnp.maximum(top, jnp.max(far, axis=0, keepdims=True))
            far = jnp.exp(far - top)
        near = jnp.exp(near - top)
        total = jnp.sum(near, axis=0, keepdims=True)
        if start:
            total += jnp.sum(far, axis=0, keepdims=True)
        scale = 1.0 / total
        near = near * scale
        near_grad = dot_nt(values[here, :], out_grad)
        inner = jnp.sum(near * near_grad, axis=0, keepdims=True)
        if start:
            far = far * scale
            far_grad = dot_nt(values[:start, :], out_grad)
            inner += jnp.sum(far * far_grad, axis=0, keepdims=True)
        near_score = (near * (near_grad - inner) * factor).astype(LOW)
        grad = dot_tn(near_score, keys[here, :])
        k_total[here, :] = dot_nn(near_score, query)
        v_total[here, :] = dot_nn(near.astype(LOW), out_grad)
        if start:
            far_score = (far * (far_grad - inner) * factor).astype(LOW)
            grad += dot_tn(far_score, keys[:start, :])
            k_total[:start, :] += dot_nn(far_score, query)
            v_total[:start, :] += dot_nn(far.astype(LOW), out_grad)
        scaled, row_sum, gain_part = unrope(grad, q_raw, 0, q_gain, here)
        q_grad[here, :] = scaled
        q_gain_total += gain_part
        sums[here, 0:1] = jnp.where(first, row_sum, sums[here, 0:1] + row_sum)
    q_gain_grad[...] = q_gain_total
    scaled, row_sum, gain_part = unrope(k_total[...], k_raw, 1, k_gain, slice(None))
    k_grad[...] = scaled
    k_gain_grad[...] = gain_part
    sums[:, 1:2] = jnp.where(first, row_sum, sums[:, 1:2] + row_sum)
    v_grad[...] = v_total[...].astype(LOW)


def attend_back(
    queries, keys, values, mixed_grad, raw, inverse, q_gain, k_gain, cosine, sine, waits
):
    length, width = queries.shape
    head_dim = cosine.shape[1]
    heads = width // head_dim
    column = lambda shift: pl.BlockSpec((length, head_dim), lambda i: (0, i + shift * heads))
    whole = lambda v: pl.BlockSpec(v.shape, lambda i: (0, 0))
    gain = pl.BlockSpec((1, head_dim), lambda i: (0, i))
    wide = jax.ShapeDtypeStruct((length, width), FULL)
    vector = jax.ShapeDtypeStruct((1, width), FULL)
    def body(*refs):
        attend_back_kernel(*refs[:11], *refs[11 + len(waits) :])

    return pl.pallas_call(
        body,
        grid=(heads,),
        in_specs=[column(0)] * 4 + [column(0), column(1), whole(inverse), gain, gain, whole(cosine), whole(sine)]
        + [pl.BlockSpec(memory_space=pl.ANY)] * len(waits),
        out_specs=[column(0)] * 3 + [pl.BlockSpec((length, 2), lambda i: (0, 0)), gain, gain],
        out_shape=[wide, wide, jax.ShapeDtypeStruct((length, width), LOW), jax.ShapeDtypeStruct((length, 2), FULL), vector, vector],
        scratch_shapes=[pltpu.VMEM((length, head_dim), FULL)] * 2,
        compiler_params=pltpu.CompilerParams(vmem_limit_bytes=VMEM_LIMIT),
        cost_estimate=pl.CostEstimate(flops=0, bytes_accessed=0, transcendentals=0),
    )(queries, keys, values, mixed_grad, raw, raw, inverse, q_gain, k_gain, cosine, sine, *waits)

def call(kernel, grid, inputs, outputs, waits=(), scalars=(), work=2**33):
    count = len(scalars) + len(inputs)

    def body(*refs):
        kernel(*refs[:count], *refs[count + len(waits) :])

    out = pl.pallas_call(
        body,
        grid=grid,
        in_specs=[spec for _, spec in scalars]
        + [pl.BlockSpec(block, index) for _, block, index in inputs]
        + [pl.BlockSpec(memory_space=pl.ANY)] * len(waits),
        out_specs=[pl.BlockSpec(block, index) for _, _, block, index in outputs],
        out_shape=[jax.ShapeDtypeStruct(shape, kind) for shape, kind, _, _ in outputs],
        compiler_params=pltpu.CompilerParams(vmem_limit_bytes=VMEM_LIMIT),
        cost_estimate=pl.CostEstimate(flops=work, bytes_accessed=0, transcendentals=0),
    )(*(v for v, _ in scalars), *(v for v, _, _ in inputs), *waits)
    return out[0] if len(outputs) == 1 else out


def stay(array):
    return array, array.shape, lambda *i: (0,) * array.ndim


def chip_product(places, lefts, weights, product, width, tile):
    length = lefts[0][0].shape[-2]
    count = length // 16
    inputs = lefts + weights

    def rows_of(ref, chip):
        parts = []
        for z in range(4):
            start = pl.multiple_of((z * 4 + chip) * count, count)
            parts.append(ref[pl.ds(start, count), :])
        return jnp.concatenate(parts, axis=0)

    def part(place, refs, flip_e, flip_x):
        e = 1 - place[0] if flip_e else place[0]
        x = 1 - place[1] if flip_x else place[1]
        rows = [rows_of(ref, e * 2 + x) for ref in refs[: len(lefts)]]
        out = product(rows, *refs[len(lefts) : len(inputs)])
        return out.astype(LOW).reshape(4, count, tile)

    def far_kernel(place, *refs):
        out = part(place, refs, True, True)
        refs[-2][...] = out[:2]
        refs[-1][...] = out[2:]

    def near_kernel(place, *refs):
        refs[-3][...] = part(place, refs, True, False)
        refs[-2][...] = part(place, refs, False, True)
        refs[-1][...] = part(place, refs, False, False)

    smem = pl.BlockSpec(memory_space=pltpu.SMEM)

    def run(kernel, parts, outs, waits):
        out = ((parts, count, width), LOW, (parts, count, tile), lambda j: (0, 0, j))
        return call(kernel, (width // tile,), inputs, [out] * outs, waits, [(places, smem)])

    far = lambda: run(far_kernel, 2, 2, ())
    near = lambda *waits: run(near_kernel, 4, 3, waits)
    return far, near


ATTN_TILE = 512


def feature_blocks(groups, rows):
    size = 8 * rows
    for g in range(groups):
        for k in range(4):
            start = (g * 4 + k) * size
            yield slice(start, start + size), slice(g * 8, g * 8 + 8), k


def project(all_in, weights):
    length = all_in.shape[0]
    eight, four, rows, _ = weights.shape
    tile = ATTN_TILE

    def kernel(a, w, out):
        total = jnp.zeros(out.shape, FULL)
        for columns, pieces, k in feature_blocks(eight // 8, rows):
            total += dot_nn(a[:, columns], w[pieces, k].reshape(8 * rows, tile))
        out[...] = total

    return call(
        kernel,
        (3,),
        [stay(all_in), (weights, (eight, four, rows, tile), lambda j: (0, 0, 0, j + 1))],
        [((length, 3 * tile), FULL, (length, tile), lambda j: (0, j))],
    )


def project_back(places, raw_grad, weights):
    eight, four, rows, columns = weights.shape
    tile = ATTN_TILE
    size = 8 * rows

    def product(lefts, w):
        return dot_nt(lefts[0], w[:, 0, :, tile : 4 * tile].reshape(size, 3 * tile))

    weight = (weights, (8, 1, rows, columns), lambda j: (j // 4, j % 4, 0, 0))
    width = eight // 8 * 4 * size
    return chip_product(places, [stay(raw_grad)], [weight], product, width, size)


def mix_out(places, mixed, weights):
    eight, four, rows, _ = weights.shape
    features = mixed.shape[1]
    tile = ATTN_TILE

    def product(lefts, w):
        return dot_nn(lefts[0], w[:, 0].reshape(features, tile))

    weight = (weights, (eight, 1, rows, tile), lambda j: (0, j, 0, 0))
    return chip_product(places, [stay(mixed)], [weight], product, four * tile, tile)


def mix_out_back(attn_grad, weights):
    length, width = attn_grad.shape
    eight, four, rows, _ = weights.shape
    tile = ATTN_TILE
    features = eight * rows
    part = min(length, 256)

    def kernel(a, w, out):
        total = jnp.zeros(out.shape, FULL)
        for k in range(four):
            right = w[:, k].reshape(features, tile)
            total += dot_nt(a[:, k * tile : (k + 1) * tile], right)
        out[...] = total.astype(LOW)

    return call(
        kernel,
        (length // part,),
        [
            (attn_grad, (part, width), lambda j: (j, 0)),
            (weights, (eight, four, rows, tile), lambda j: (0, 0, 0, 0)),
        ],
        [((length, features), LOW, (part, features), lambda j: (j, 0))],
    )


def gated(mlp_in, weights, waits):
    length = mlp_in.shape[0]
    eight, _, four, rows, count = weights.shape
    tile = min(count, 512)

    def kernel(a, gate_w, up_w, hidden, gate, up):
        both = []
        for w in (gate_w, up_w):
            total = jnp.zeros(gate.shape, FULL)
            for columns, pieces, k in feature_blocks(eight // 8, rows):
                total += dot_nn(a[:, columns], w[pieces, 0, k].reshape(8 * rows, tile))
            both.append(total)
        gate[...], up[...] = both
        hidden[...] = (both[0] * jax.nn.sigmoid(both[0]) * both[1]).astype(LOW)

    weight = lambda i: (
        weights, (eight, 1, four, rows, tile), lambda j: (0, i, 0, 0, j),
    )
    cut = ((length, tile), lambda j: (0, j))
    shape = (length, count)
    return call(
        kernel,
        (count // tile,),
        [stay(mlp_in), weight(0), weight(1)],
        [(shape, LOW) + cut, (shape, FULL) + cut, (shape, FULL) + cut],
        waits,
    )


def branch_out(places, hidden, weights):
    units = hidden.shape[1]
    eight, _, four, rows, width = weights.shape
    tile = min(width, 512)

    def product(lefts, w):
        return dot_nn(lefts[0], w[:, 0].reshape(units, tile))

    weight = (weights, (eight, 1, four, rows, tile), lambda j: (0, 2, 0, 0, j))
    return chip_product(places, [stay(hidden)], [weight], product, width, tile)


def gated_back(branch_rows, weights, gate_raw, up_raw):
    length, units = gate_raw.shape
    eight, _, four, rows, width = weights.shape
    tile = min(units, 512)
    pieces = tile // (four * rows)

    def kernel(a, w, gate, up, out):
        hidden_grad = dot_nt(a[...], w[:, 0].reshape(tile, width))
        raw = gate[...]
        sigmoid = jax.nn.sigmoid(raw)
        slope = sigmoid * (1.0 + raw * (1.0 - sigmoid))
        out[0] = (hidden_grad * up[...] * slope).astype(LOW)
        out[1] = (hidden_grad * raw * sigmoid).astype(LOW)

    cut = ((length, tile), lambda j: (0, j))
    return call(
        kernel,
        (units // tile,),
        [
            stay(branch_rows),
            (weights, (pieces, 1, four, rows, width), lambda j: (j, 2, 0, 0, 0)),
            (gate_raw,) + cut,
            (up_raw,) + cut,
        ],
        [((2, length, units), LOW, (2, length, tile), lambda j: (0, 0, j))],
    )


def input_back(places, grads, weights):
    _, length, units = grads.shape
    eight, _, four, rows, _ = weights.shape
    size = 8 * rows

    def product(lefts, gate_w, up_w):
        gate = dot_nt(lefts[0], gate_w[:, 0, 0].reshape(size, units))
        return gate + dot_nt(lefts[1], up_w[:, 0, 0].reshape(size, units))

    left = lambda i: (grads, (None, length, units), lambda j: (i, 0, 0))
    weight = lambda i: (
        weights, (8, 1, 1, rows, units), lambda j: (j // 4, i, j % 4, 0, 0),
    )
    width = eight // 8 * four * size
    return chip_product(
        places, [left(0), left(1)], [weight(0), weight(1)], product, width, size
    )


def down_grad(hidden, branch_rows, groups, rows):
    length, units = hidden[0].shape
    width = branch_rows[0].shape[1]
    run = 4 * rows
    many = 1 if run % 128 == 0 else 4
    shape = (4, groups, run, width)

    def kernel(a, b, c, d, out):
        total = dot_tn(a[...], b[...]) + dot_tn(c[...], d[...])
        out[...] = total.astype(LOW).reshape(out.shape)

    cut = ((length, many * run), lambda g, j: (0, g * (4 // many) + j))
    return call(
        kernel,
        (groups, 4 // many),
        [
            (hidden[0],) + cut,
            stay(branch_rows[0]),
            (hidden[1],) + cut,
            stay(branch_rows[1]),
        ],
        [(shape, LOW, (many, 1, run, width), lambda g, j: (j, g, 0, 0))],
    )


def lay_features(total, out, many, rows):
    for i in range(many):
        for j in range(4):
            start = (i * 4 + j) * rows
            yield (j, i), total[start : start + rows]


def units_grad(mlp_in, grads, groups, rows):
    length = mlp_in[0].shape[0]
    units = grads[0].shape[2]
    run = 4 * rows
    many = 1 if run % 128 == 0 else 4
    shape = (4, 2, groups, 4, rows, units)

    def kernel(a, b, c, d, out):
        total = (dot_tn(a[...], b[0]) + dot_tn(c[...], d[0])).astype(LOW)
        for (j, i), part in lay_features(total, out, many, rows):
            out[j, 0, 0, i] = part

    cut = ((length, many * run), lambda i, g, j: (0, g * (4 // many) + j))
    right = ((1, length, units), lambda i, g, j: (i, 0, 0))
    return call(
        kernel,
        (2, groups, 4 // many),
        [
            (mlp_in[0],) + cut,
            (grads[0],) + right,
            (mlp_in[1],) + cut,
            (grads[1],) + right,
        ],
        [
            (
                shape,
                LOW,
                (4, 1, 1, many, rows, units),
                lambda i, g, j: (0, i, g, j, 0, 0),
            )
        ],
    )


def attention_grad(all_in, raw_grad, mixed, attn_grad, groups, rows, waits):
    length = all_in[0].shape[0]
    tile = ATTN_TILE
    run = 4 * rows
    many = 1 if run % 128 == 0 else 4
    shape = (4, groups, 4, rows, 4 * tile)

    def kernel(a, b, c, d, e, f, p, q, out):
        total = (dot_tn(a[...], b[...]) + dot_tn(c[...], d[...])).astype(LOW)
        for (j, i), part in lay_features(total, out, many, rows):
            out[j, 0, i, :, tile:] = part
        total = (dot_tn(e[0], f[...]) + dot_tn(p[0], q[...])).astype(LOW)
        for i in range(many):
            for j in range(4):
                part = total[j * rows : (j + 1) * rows, i * tile : (i + 1) * tile]
                out[j, 0, i, :, :tile] = part

    cut = ((length, many * run), lambda g, j: (0, g * (4 // many) + j))
    left = ((1, length, run), lambda g, j: (g, 0, 0))
    right = ((length, many * tile), lambda g, j: (0, j))
    return call(
        kernel,
        (groups, 4 // many),
        [
            (all_in[0],) + cut,
            stay(raw_grad[0]),
            (all_in[1],) + cut,
            stay(raw_grad[1]),
            (mixed[0],) + left,
            (attn_grad[0],) + right,
            (mixed[1],) + left,
            (attn_grad[1],) + right,
        ],
        [(shape, LOW, (4, 1, many, rows, 4 * tile), lambda g, j: (0, g, j, 0, 0))],
        waits,
    )


def wide(value):
    return value.astype(FULL)


def tie(values, others):
    if not others:
        return tuple(values)
    return lax.optimization_barrier(tuple(values) + tuple(others))[: len(values)]


def two_halves(first, second, waits):
    half = (first.shape[0] // 2,) + first.shape[1:]

    def kernel(a, b, a_out, b_out):
        a_out[...] = a[...]
        b_out[...] = b[...]

    out = (half, first.dtype, half, lambda i: (0, 0, 0))
    return call(
        kernel,
        (1,),
        [(first, half, lambda i: (0, 0, 0)), (second, half, lambda i: (1, 0, 0))],
        [out, out],
        waits,
        work=0,
    )


def hold(value, *others):
    def kernel(a, out):
        out[...] = a[...]

    shape = value.shape
    whole = (shape, lambda i: (0,) * len(shape))
    return call(kernel, (1,), [(value,) + whole], [(shape, value.dtype) + whole], others, work=0)


class Steps:
    def __init__(self):
        self.last = ()

    def wait(self, *values):
        self.last += tuple(jax.tree.leaves(values))

    def __call__(self, step, *inputs):
        flat, tree = jax.tree.flatten(inputs)
        out = step(*tree.unflatten(tie(flat, self.last)))
        self.last = tuple(jax.tree.leaves(out))
        return out


class Links:
    def __init__(self, steps):
        self.steps = steps

    def send(self, value, axes, pairs):
        (value,) = tie((value,), self.steps.last)
        return lax.ppermute(value, axes, pairs)

    def swap(self, value, axis):
        return self.send(value, axis, SWAP)

    def swap_both(self, value, first, second):
        return self.send(value, (first, second), BOTH)


def swap(value, axis):
    return lax.ppermute(value, axis, SWAP)


def pick(value, places):
    starts = [0] * value.ndim
    sizes = list(value.shape)
    for dim, place in places.items():
        starts[dim] = place
        sizes[dim] = 1
    taken = lax.dynamic_slice(value, starts, sizes)
    return taken.reshape([s for d, s in enumerate(value.shape) if d not in places])


def put(out, parts):
    for value, starts in parts:
        out = lax.dynamic_update_slice(out, value, starts)
    return out


class Place:
    def __init__(self):
        self.g, self.e, self.x, self.c, self.h, self.l = (lax.axis_index(a) for a in AXES)
        self.groups = lax.axis_size("g")
        self.steps = Steps()
        self.links = Links(self.steps)


class Spread:
    def __init__(self, at, part, inputs, first="e", second="x"):
        self.at, self.places = at, (getattr(at, first), getattr(at, second))
        a, b = self.places

        def start(*inputs):
            return tuple(part(i, j, *inputs) for i in (a, 1 - a) for j in (b, 1 - b))

        self.mine, for_b, for_a, far = at.steps(start, *inputs)
        self.from_a = at.links.swap(for_a, first)
        self.from_b = at.links.swap(for_b, second)
        self.far = at.links.swap_both(far, first, second)
        self.sent = (self.mine, for_b, for_a, far)
        self.came = (self.from_a, self.from_b, self.far)

    def second(self, lay):
        a, b = self.places

        def join(mine, from_a, from_b, far):
            return lay(
                [(mine, a, b), (from_a, 1 - a, b), (from_b, a, 1 - b), (far, 1 - a, 1 - b)]
            )

        return self.at.steps(join, self.mine, self.from_a, self.from_b, self.far)


def one_of(i, j, parts):
    return pick(parts, {0: i, 1: j})


def lay_all(parts):
    shape = parts[0][0].shape
    out = jnp.zeros((2, 2) + shape, parts[0][0].dtype)
    tail = (0,) * len(shape)
    return put(out, [(v.reshape((1, 1) + shape), (i, j) + tail) for v, i, j in parts])


class TokensIn:
    def __init__(self, at, rows):
        self.at = at
        self.spread = Spread(at, one_of, [rows.reshape(2, 2, -1, rows.shape[1])])

    def second(self):
        self.spread = Spread(self.at, one_of, [self.spread.second(lay_all)], "h", "l")

    def third(self):
        def lay(parts):
            out = lay_all(parts)
            return out.reshape((4,) + out.shape[2:])

        return self.spread.second(lay)


class TokensOut:
    def __init__(self, at, blocks):
        self.at = at
        blocks = blocks.reshape((2, 2) + blocks.shape[1:])
        self.spread = Spread(at, one_of, [blocks], "h", "l")

    def second(self):
        self.spread = Spread(self.at, one_of, [self.spread.second(lay_all)])

    def third(self):
        def lay(parts):
            out = lay_all(parts)
            return out.reshape(-1, out.shape[-1])

        return self.spread.second(lay)


class GatherTokens:
    def __init__(self, at, blocks):
        self.at, self.blocks = at, blocks
        self.from_e = at.links.swap(blocks, "e")
        self.from_x = at.links.swap(blocks, "x")

    def second(self, waits=()):
        at = self.at
        half_e, half_x = at.steps(two_halves, self.from_e, self.from_x, waits)
        self.far_0 = at.links.swap(half_e, "x")
        self.far_1 = at.links.swap(half_x, "e")
        four, count, width = self.blocks.shape
        cut = (four, 1, 1, count, width)

        def near(blocks, from_x, from_e):
            out = jnp.zeros((four, 2, 2, count, width), blocks.dtype)
            parts = [
                (blocks.reshape(cut), (0, at.e, at.x, 0, 0)),
                (from_x.reshape(cut), (0, at.e, 1 - at.x, 0, 0)),
                (from_e.reshape(cut), (0, 1 - at.e, at.x, 0, 0)),
            ]
            return put(out, parts)

        self.out = at.steps(near, self.blocks, self.from_x, self.from_e)

    def third(self):
        at = self.at
        four, count, width = self.blocks.shape
        cut = (2, 1, 1, count, width)

        def far(out, far_0, far_1):
            parts = [
                (far_0.reshape(cut), (0, 1 - at.e, 1 - at.x, 0, 0)),
                (far_1.reshape(cut), (2, 1 - at.e, 1 - at.x, 0, 0)),
            ]
            return put(out, parts).reshape(-1, width)

        return at.steps(far, self.out, self.far_0, self.far_1)


class ScatterTokens:
    def __init__(self, at, far, near):
        self.at = at
        far_0, far_1 = at.steps(far)
        self.for_e_0 = at.links.swap(far_0, "x")
        self.for_x_1 = at.links.swap(far_1, "e")
        self.for_e, self.for_x, self.mine = at.steps(near, far_0)

    def second(self):
        at = self.at

        def add(for_e, for_x, for_e_0, for_x_1):
            for_e_0 = (wide(for_e[:2]) + wide(for_e_0)).astype(LOW)
            for_x_1 = (wide(for_x[2:]) + wide(for_x_1)).astype(LOW)
            return jnp.concatenate([for_e_0, for_e[2:]]), jnp.concatenate([for_x[:2], for_x_1])

        for_e, for_x = at.steps(add, self.for_e, self.for_x, self.for_e_0, self.for_x_1)
        self.from_e = at.links.swap(for_e, "e")
        self.from_x = at.links.swap(for_x, "x")

    def third(self, step, *inputs):
        def add(mine, from_e, from_x, *inputs):
            return step(wide(mine) + wide(from_e) + wide(from_x), *inputs)

        return self.at.steps(add, self.mine, self.from_e, self.from_x, *inputs)


def sum_chips(value):
    far = lax.ppermute(value, ("e", "x"), BOTH)
    return value + swap(value, "x") + swap(value, "e") + far


def gather(at, piece, *others):
    (piece,) = tie((piece,), at.steps.last + others)
    return lax.all_gather(piece, ("g", "c", "h", "l"), axis=0)


def scatter(at, value, *others):
    (value,) = tie((value,), at.steps.last + others)
    value = lax.psum_scatter(value, ("h", "l"), scatter_dimension=0)
    return value


def scatter_groups(at, value, dim):
    if at.groups == 1:
        return value.reshape([n for d, n in enumerate(value.shape) if d != dim])
    return lax.psum_scatter(value, "g", scatter_dimension=dim)


def halves(value, core, runs):
    rows, count = value.shape
    each = count // (2 * runs)

    def of(place):
        parts = [
            lax.dynamic_slice(value, (0, (2 * k + place) * each), (rows, each))
            for k in range(runs)
        ]
        return jnp.concatenate(parts, axis=1)

    return of(core), of(1 - core)


class ScatterGains:
    def __init__(self, at, grads):
        self.at = at
        value = grads.reshape(grads.shape[0], at.groups, 2, 2, 2, 2, 2, -1)
        if at.groups > 1:
            value = lax.psum_scatter(value, "g", scatter_dimension=1, tiled=True)
        self.value = value.reshape(value.shape[:1] + value.shape[2:])
        self.axes = ["e", "x", "c", "h", "l"]
        self.start()

    def start(self):
        place = getattr(self.at, self.axes[0])
        self.kept, send = self.at.steps(
            lambda v: (pick(v, {1: place}), pick(v, {1: 1 - place})), self.value
        )
        self.got = self.at.links.swap(send, self.axes.pop(0))

    def more(self):
        self.value = self.at.steps(lambda a, b: a + b, self.kept, self.got)
        if self.axes:
            self.start()
        return self.value


def rope_tables(places, head_dim):
    half_dim = head_dim // 2
    inverse = jnp.power(
        jnp.float32(ROPE_THETA), -(jnp.arange(half_dim, dtype=FULL) * 2.0 / head_dim)
    )
    angles = places.astype(FULL)[:, None] * inverse[None, :]
    sine = jnp.sin(angles)
    cosine = jnp.cos(angles)
    return (
        jnp.concatenate([cosine, cosine], axis=-1),
        jnp.concatenate([-sine, sine], axis=-1),
    )


def norm_forward(tensor, gain_vec):
    inverse = lax.rsqrt(jnp.mean(tensor * tensor, axis=-1, keepdims=True) + EPSILON)
    unit = tensor * inverse
    return unit * gain_vec, unit, inverse


def norm_backward(grad_in, unit, inverse, gain_vec):
    axes = tuple(range(grad_in.ndim - 1))
    gain_grad = jnp.sum(grad_in * unit, axis=axes)
    unit_grad = grad_in * gain_vec
    inner = jnp.mean(unit_grad * unit, axis=-1, keepdims=True)
    return inverse * (unit_grad - unit * inner), gain_grad


def on_device(
    hidden_in,
    q_weight,
    k_weight,
    v_weight,
    o_weight,
    q_gain,
    k_gain,
    attn_gain,
    gate_weight,
    up_weight,
    down_weight,
    mlp_gain,
    out_grad,
):
    at = Place()
    steps = at.steps
    batch, rows_here, width = hidden_in.shape
    head_dim = width // HEADS
    length = batch * rows_here * 4
    rows_owned = q_weight.shape[0]
    groups = at.groups
    ff_block = down_weight.shape[0]

    assert head_dim % (8 * rows_owned) == 0 or (8 * rows_owned) % head_dim == 0
    assert ff_block == 4 * rows_owned

    def columns_of(e, x, weight):
        rows, count = weight.shape
        part = count // (4 * groups)
        each = [
            lax.dynamic_slice(weight, (0, ((g * 2 + e) * 2 + x) * part), (rows, part))
            for g in range(groups)
        ]
        return jnp.concatenate(each, axis=1)

    def lay_columns(parts):
        rows, count = parts[0][0].shape
        part = count // groups
        out = jnp.zeros((rows, 4 * count), FULL)
        for value, e, x in parts:
            for g in range(groups):
                piece = wide(value[:, g * part : (g + 1) * part])
                out = lax.dynamic_update_slice(out, piece, (0, ((g * 2 + e) * 2 + x) * part))
        return out

    quarter = width // 4

    def columns_of_attention(e, x, q, k, v, o, gains):
        three = [columns_of(e, x, w) for w in (q, k, v)]
        return jnp.concatenate(three + [gains], axis=1)

    def lay_attention(parts):
        tail = lay_all(parts)
        tail = tail.reshape((4,) + tail.shape[2:])
        runs = jnp.stack([o_weight[:, k * quarter : (k + 1) * quarter] for k in range(4)])
        return jnp.concatenate([runs, tail], axis=2)

    def lay_four(parts):
        out = lay_all(parts)
        return out.reshape((4,) + out.shape[2:])

    def lay_three(parts):
        return tuple(
            lay_columns([(v[:, i * quarter : (i + 1) * quarter], e, x) for v, e, x in parts])
            for i in range(3)
        )

    places = jnp.stack([at.e, at.x]).astype(jnp.int32)

    def here(vector):
        return pick(vector.reshape(groups, 2, 2, -1), {1: at.e, 2: at.x}).reshape(1, -1)

    def whole(vector):
        out = jnp.zeros((groups, 2, 2, vector.size // groups), FULL)
        part = vector.reshape(groups, 1, 1, -1)
        return lax.dynamic_update_slice(out, part, (0, at.e, at.x, 0)).reshape(-1)

    def pair(halved, core_sent):
        return halved, at.links.swap(core_sent, "c")

    gains = jnp.stack([q_gain, k_gain, attn_gain, mlp_gain], axis=1)
    gains = jnp.pad(gains, ((0, 0), (0, 124)))
    attn_spread = Spread(
        at, columns_of_attention, [q_weight, k_weight, v_weight, o_weight, gains]
    )
    own = TokensIn(at, hidden_in.reshape(-1, width))
    gate_spread = Spread(at, columns_of, [gate_weight])
    up_spread = Spread(at, columns_of, [up_weight])
    attn_all = gather(at, attn_spread.second(lay_attention))
    own.second()
    cosine, sine = steps(lambda n: rope_tables(n, head_dim), jnp.arange(length))
    gate_mine = gate_spread.second(lay_four)
    up_mine = up_spread.second(lay_four)
    mlp_mine = steps(
        lambda *v: jnp.stack(v), gate_mine, up_mine, down_weight.reshape((4, -1, width))
    )
    mlp_all = gather(at, mlp_mine)
    own_in = own.third()
    all_in = GatherTokens(at, own_in)
    all_in.second()
    all_in = all_in.third()
    all_in_half = pair(*steps(lambda v: halves(v, at.c, 4 * groups), all_in))
    top = TokensIn(at, out_grad.reshape(-1, width))
    steps.wait(all_in_half)

    def gains_of(weights):
        value = wide(weights[..., -128:-124]).reshape(groups, 8, 4, rows_owned, 4)
        return value.transpose(4, 0, 2, 1, 3).reshape(4, -1)

    gains = steps(gains_of, attn_all)
    q_gain_here, k_gain_here = here(gains[0]), here(gains[1])
    attn_gain_all, mlp_gain_all = gains[2], gains[3]

    def squares_of(raw):
        q_raw, k_raw = jnp.split(raw[:, : 2 * quarter], 2, axis=1)
        return jnp.stack([jnp.sum(q_raw * q_raw, -1), jnp.sum(k_raw * k_raw, -1)])

    raw = steps(project, all_in, attn_all)
    squares = sum_chips(steps(squares_of, raw))
    inverse = steps(lambda s: lax.rsqrt(s / width + EPSILON).T, squares)
    queries, keys, values, mixed = steps(
        attend, raw, inverse, q_gain_here, k_gain_here, cosine, sine
    )
    attn_out = ScatterTokens(at, *mix_out(places, mixed, attn_all))

    def halve_mixed(mixed):
        return [
            v.reshape(length, groups, -1).swapaxes(0, 1) for v in halves(mixed, at.c, groups)
        ]

    mixed_half = pair(*steps(halve_mixed, mixed))
    steps.wait(mixed_half)
    attn_out.second()

    def after_attention(attn_out, own_in, gain):
        normed, unit, inverse = norm_forward(attn_out, gain)
        residual = wide(own_in) + normed
        return residual.astype(LOW), residual, unit, inverse

    residual_low, residual, attn_unit, attn_inverse = attn_out.third(
        after_attention, own_in, attn_gain_all
    )

    mlp_in = GatherTokens(at, residual_low)
    mlp_in.second()
    mlp_in = mlp_in.third()
    mlp_in_half = pair(*steps(lambda v: halves(v, at.c, 4 * groups), mlp_in))
    steps.wait(mlp_in_half)
    hidden, gate_raw, up_raw = steps(gated, mlp_in, mlp_all, top.spread.came)
    top.second()
    branch = ScatterTokens(at, *branch_out(places, hidden, mlp_all))
    hidden_half = pair(*steps(lambda v: halves(v, at.c, groups), hidden))
    steps.wait(hidden_half)
    branch.second()
    own_top = top.third()

    def after_mlp(branch, residual, own_top, gain):
        normed, unit, inverse = norm_forward(branch, gain)
        grad, gain_grad = norm_backward(wide(own_top), unit, inverse, gain)
        return grad.astype(LOW), (residual + normed).astype(LOW), gain_grad

    branch_low, own_out, mlp_gain_grad = branch.third(
        after_mlp, residual, own_top, mlp_gain_all
    )

    branch_rows = GatherTokens(at, branch_low)
    layer_out = TokensOut(at, own_out)
    branch_rows.second(layer_out.spread.came)
    branch_rows = branch_rows.third()
    branch_rows = (branch_rows, at.links.swap(branch_rows, "c"))
    grad = steps(lambda a, b: down_grad(a, b, groups, rows_owned), hidden_half, branch_rows)
    down_own = scatter(at, grad)
    unit_grads = steps(gated_back, branch_rows[0], mlp_all, gate_raw, up_raw)
    unit_grads = (unit_grads, at.links.swap(unit_grads, "c"))
    input_part = ScatterTokens(at, *input_back(places, unit_grads[0], mlp_all))
    grad = steps(lambda a, b: units_grad(a, b, groups, rows_owned), mlp_in_half, unit_grads)
    units_own = scatter(at, grad)
    input_part.second()
    layer_out.second()
    layer_out_came = layer_out.spread.came

    def before_attention(input_grad, own_top, unit, inverse, gain):
        residual_grad = wide(own_top) + input_grad
        grad, gain_grad = norm_backward(residual_grad, unit, inverse, gain)
        return grad.astype(LOW), residual_grad, gain_grad

    attn_grad, residual_grad, attn_gain_grad = input_part.third(
        before_attention, own_top, attn_unit, attn_inverse, attn_gain_all
    )

    attn_low = GatherTokens(at, attn_grad)
    layer_out = layer_out.third()
    attn_low.second()
    attn_low = attn_low.third()
    attn_low = (attn_low, swap(attn_low, "c"))
    mixed_grad = steps(mix_out_back, attn_low[0], attn_all)
    q_scaled, k_scaled, v_low, inner, q_gain_grad, k_gain_grad = steps(
        attend_back, queries, keys, values, mixed_grad, raw, inverse,
        q_gain_here, k_gain_here, cosine, sine, (down_own,) + layer_out_came,
    )
    inner = sum_chips(steps(lambda v: v.T / width, inner))

    def before_project(raw, inverse, q_scaled, k_scaled, v_low, inner):
        q_raw, k_raw = jnp.split(raw[:, : 2 * quarter], 2, axis=1)
        inner = inner.T
        grads = []
        for i, (part, scaled) in enumerate([(q_raw, q_scaled), (k_raw, k_scaled)]):
            each = inverse[:, i : i + 1]
            grads.append((each * (scaled - part * each * inner[:, i : i + 1])).astype(LOW))
        return jnp.concatenate(grads + [v_low], axis=1)

    raw_grad = steps(before_project, raw, inverse, q_scaled, k_scaled, v_low, inner)
    raw_grad = (raw_grad, swap(raw_grad, "c"))
    in_part = ScatterTokens(at, *project_back(places, raw_grad[0], attn_all))
    attn_grad_part = steps(
        lambda *v: attention_grad(*v[:-1], groups, rows_owned, v[-1:]),
        all_in_half, raw_grad, mixed_half, attn_low, units_own,
    )
    attn_own = scatter(at, attn_grad_part)
    in_part.second()
    in_grad = in_part.third(lambda a, b: (a + b).astype(LOW), residual_grad)
    in_grad = TokensOut(at, in_grad)
    units_own = scatter_groups(at, units_own, 1)
    gate_spread = Spread(at, one_of, [units_own[0].reshape(2, 2, rows_owned, -1)])
    up_spread = Spread(at, one_of, [units_own[1].reshape(2, 2, rows_owned, -1)])
    gate_own = gate_spread.second(lay_columns)
    up_own = up_spread.second(lay_columns)
    in_grad.second()
    gains = jnp.stack([whole(q_gain_grad), whole(k_gain_grad), attn_gain_grad, mlp_gain_grad])
    gains = ScatterGains(at, hold(gains, attn_own))
    attn_own = scatter_groups(at, attn_own, 0)
    attn_spread = Spread(
        at, one_of, [attn_own[..., quarter:].reshape(2, 2, rows_owned, -1)]
    )
    in_grad = in_grad.third()
    gains.more()
    o_own = wide(jnp.concatenate([attn_own[k, :, :quarter] for k in range(4)], axis=1))
    gains.more()
    own_three = list(attn_spread.second(lay_three))
    gains.more()
    down_own = wide(scatter_groups(at, down_own, 0))
    gains.more()
    gains = gains.more()
    shape = hidden_in.shape
    grads = own_three + [o_own, gate_own, up_own, down_own]
    return (layer_out.reshape(shape), in_grad.reshape(shape)) + tuple(grads) + tuple(gains)


def solution(mesh):
    dp, seq = mesh.shape["dp"], mesh.shape["seq"]
    split = Mesh(mesh.devices.reshape(dp // 8, 2, 2, 2, seq // 2, 2), AXES)
    dp_axes, seq_axes = AXES[:4], AXES[4:]
    tokens = P(dp_axes, seq_axes, None)
    matrix, vector = P(AXES, None), P(AXES)
    return jax.shard_map(
        on_device,
        mesh=split,
        in_specs=(tokens,)
        + (matrix,) * 4
        + (vector,) * 3
        + (matrix,) * 3
        + (vector, tokens),
        out_specs=(tokens,) * 2 + (matrix,) * 7 + (vector,) * 4,
        check_vma=False,
    )
```

```python
import math

import jax
import jax.numpy as jnp
from jax import lax
from jax.experimental import pallas as pl
from jax.experimental.pallas import tpu as pltpu
from jax.sharding import Mesh
from jax.sharding import PartitionSpec as P

HEADS = 16
EPSILON = 1e-06
ROPE_THETA = 500000.0
LOW = jnp.bfloat16
FULL = jnp.float32

AXES = ("g", "e", "x", "c", "h", "l")
SWAP = [(0, 1), (1, 0)]
BOTH = [(i, 3 - i) for i in range(4)]
VMEM_LIMIT = 56 * 1024 * 1024


BLOCK = 256

def dot_nt(a, b):
    return lax.dot_general(a, b, (((1,), (1,)), ((), ())), preferred_element_type=FULL)

def dot_nn(a, b):
    return lax.dot_general(a, b, (((1,), (0,)), ((), ())), preferred_element_type=FULL)

def dot_tn(a, b):
    return lax.dot_general(a, b, (((0,), (0,)), ((), ())), preferred_element_type=FULL)

def turn(tensor):
    return pltpu.roll(tensor, tensor.shape[1] // 2, 1)


def attend_kernel(q_raw, k_raw, v_raw, inverse, q_gain, k_gain, cosine, sine,
                  q_out, k_out, v_out, mixed):
    length, head_dim = q_raw.shape
    factor = 1.0 / math.sqrt(head_dim)
    block = min(BLOCK, length)

    def rope(raw, column, gain):
        normed = raw[...] * inverse[:, column : column + 1] * gain[...]
        return (normed * cosine[...] + turn(normed) * sine[...]).astype(LOW)

    q_out[...] = rope(q_raw, 0, q_gain)
    k_out[...] = rope(k_raw, 1, k_gain)
    v_out[...] = v_raw[...].astype(LOW)
    shape = (block, block)
    allowed = lax.broadcasted_iota(jnp.int32, shape, 1) <= lax.broadcasted_iota(jnp.int32, shape, 0)
    for start in range(0, length, block):
        here = slice(start, start + block)
        queries = q_out[here, :]
        near = jnp.where(allowed, dot_nt(queries, k_out[here, :]) * factor, -1e30)
        top = jnp.max(near, axis=1, keepdims=True)
        if start:
            far = dot_nt(queries, k_out[:start, :]) * factor
            top = jnp.maximum(top, jnp.max(far, axis=1, keepdims=True))
            far = jnp.exp(far - top)
        near = jnp.exp(near - top)
        total = jnp.sum(near, axis=1, keepdims=True)
        if start:
            total += jnp.sum(far, axis=1, keepdims=True)
        scale = 1.0 / total
        out = dot_nn((near * scale).astype(LOW), v_out[here, :])
        if start:
            out += dot_nn((far * scale).astype(LOW), v_out[:start, :])
        mixed[here, :] = out.astype(LOW)


def attend(raw, inverse, q_gain, k_gain, cosine, sine):
    length = raw.shape[0]
    head_dim = cosine.shape[1]
    width = q_gain.shape[1]
    heads = width // head_dim
    column = lambda shift: pl.BlockSpec((length, head_dim), lambda i: (0, i + shift * heads))
    whole = lambda v: pl.BlockSpec(v.shape, lambda i: (0, 0))
    gain = pl.BlockSpec((1, head_dim), lambda i: (0, i))
    out = jax.ShapeDtypeStruct((length, width), LOW)
    return pl.pallas_call(
        attend_kernel,
        grid=(heads,),
        in_specs=[column(0), column(1), column(2), whole(inverse), gain, gain, whole(cosine), whole(sine)],
        out_specs=[column(0)] * 4,
        out_shape=[out] * 4,
        compiler_params=pltpu.CompilerParams(vmem_limit_bytes=VMEM_LIMIT),
        cost_estimate=pl.CostEstimate(flops=0, bytes_accessed=0, transcendentals=0),
    )(raw, raw, raw, inverse, q_gain, k_gain, cosine, sine)


def attend_back_kernel(queries, keys, values, mixed_grad, q_raw, k_raw, inverse, q_gain, k_gain, cosine, sine,
                       q_grad, k_grad, v_grad, sums, q_gain_grad, k_gain_grad, k_total, v_total):
    length, head_dim = queries.shape
    factor = 1.0 / math.sqrt(head_dim)
    block = min(BLOCK, length)
    shape = (block, block)
    allowed = lax.broadcasted_iota(jnp.int32, shape, 0) <= lax.broadcasted_iota(jnp.int32, shape, 1)
    first = pl.program_id(0) == 0

    def unrope(grad, raw, column, gain, rows):
        pre = grad * cosine[rows, :] - turn(grad) * sine[rows, :]
        unit = raw[rows, :] * inverse[rows, column : column + 1]
        scaled = pre * gain[...]
        return scaled, jnp.sum(scaled * unit, axis=1, keepdims=True), jnp.sum(pre * unit, axis=0, keepdims=True)

    q_gain_total = jnp.zeros((1, head_dim), FULL)
    for start in range(0, length, block):
        here = slice(start, start + block)
        query, out_grad = queries[here, :], mixed_grad[here, :]
        near = jnp.where(allowed, dot_nt(keys[here, :], query) * factor, -1e30)
        top = jnp.max(near, axis=0, keepdims=True)
        if start:
            far = dot_nt(keys[:start, :], query) * factor
            top = jnp.maximum(top, jnp.max(far, axis=0, keepdims=True))
            far = jnp.exp(far - top)
        near = jnp.exp(near - top)
        total = jnp.sum(near, axis=0, keepdims=True)
        if start:
            total += jnp.sum(far, axis=0, keepdims=True)
        scale = 1.0 / total
        near = near * scale
        near_grad = dot_nt(values[here, :], out_grad)
        inner = jnp.sum(near * near_grad, axis=0, keepdims=True)
        if start:
            far = far * scale
            far_grad = dot_nt(values[:start, :], out_grad)
            inner += jnp.sum(far * far_grad, axis=0, keepdims=True)
        near_score = (near * (near_grad - inner) * factor).astype(LOW)
        grad = dot_tn(near_score, keys[here, :])
        k_total[here, :] = dot_nn(near_score, query)
        v_total[here, :] = dot_nn(near.astype(LOW), out_grad)
        if start:
            far_score = (far * (far_grad - inner) * factor).astype(LOW)
            grad += dot_tn(far_score, keys[:start, :])
            k_total[:start, :] += dot_nn(far_score, query)
            v_total[:start, :] += dot_nn(far.astype(LOW), out_grad)
        scaled, row_sum, gain_part = unrope(grad, q_raw, 0, q_gain, here)
        q_grad[here, :] = scaled
        q_gain_total += gain_part
        sums[here, 0:1] = jnp.where(first, row_sum, sums[here, 0:1] + row_sum)
    q_gain_grad[...] = q_gain_total
    scaled, row_sum, gain_part = unrope(k_total[...], k_raw, 1, k_gain, slice(None))
    k_grad[...] = scaled
    k_gain_grad[...] = gain_part
    sums[:, 1:2] = jnp.where(first, row_sum, sums[:, 1:2] + row_sum)
    v_grad[...] = v_total[...].astype(LOW)


def attend_back(
    queries, keys, values, mixed_grad, raw, inverse, q_gain, k_gain, cosine, sine, waits
):
    length, width = queries.shape
    head_dim = cosine.shape[1]
    heads = width // head_dim
    column = lambda shift: pl.BlockSpec((length, head_dim), lambda i: (0, i + shift * heads))
    whole = lambda v: pl.BlockSpec(v.shape, lambda i: (0, 0))
    gain = pl.BlockSpec((1, head_dim), lambda i: (0, i))
    wide = jax.ShapeDtypeStruct((length, width), FULL)
    vector = jax.ShapeDtypeStruct((1, width), FULL)
    def body(*refs):
        attend_back_kernel(*refs[:11], *refs[11 + len(waits) :])

    return pl.pallas_call(
        body,
        grid=(heads,),
        in_specs=[column(0)] * 4 + [column(0), column(1), whole(inverse), gain, gain, whole(cosine), whole(sine)]
        + [pl.BlockSpec(memory_space=pl.ANY)] * len(waits),
        out_specs=[column(0)] * 3 + [pl.BlockSpec((length, 2), lambda i: (0, 0)), gain, gain],
        out_shape=[wide, wide, jax.ShapeDtypeStruct((length, width), LOW), jax.ShapeDtypeStruct((length, 2), FULL), vector, vector],
        scratch_shapes=[pltpu.VMEM((length, head_dim), FULL)] * 2,
        compiler_params=pltpu.CompilerParams(vmem_limit_bytes=VMEM_LIMIT),
        cost_estimate=pl.CostEstimate(flops=0, bytes_accessed=0, transcendentals=0),
    )(queries, keys, values, mixed_grad, raw, raw, inverse, q_gain, k_gain, cosine, sine, *waits)

def call(kernel, grid, inputs, outputs, waits=(), scalars=(), work=2**33):
    count = len(scalars) + len(inputs)

    def body(*refs):
        kernel(*refs[:count], *refs[count + len(waits) :])

    out = pl.pallas_call(
        body,
        grid=grid,
        in_specs=[spec for _, spec in scalars]
        + [pl.BlockSpec(block, index) for _, block, index in inputs]
        + [pl.BlockSpec(memory_space=pl.ANY)] * len(waits),
        out_specs=[pl.BlockSpec(block, index) for _, _, block, index in outputs],
        out_shape=[jax.ShapeDtypeStruct(shape, kind) for shape, kind, _, _ in outputs],
        compiler_params=pltpu.CompilerParams(vmem_limit_bytes=VMEM_LIMIT),
        cost_estimate=pl.CostEstimate(flops=work, bytes_accessed=0, transcendentals=0),
    )(*(v for v, _ in scalars), *(v for v, _, _ in inputs), *waits)
    return out[0] if len(outputs) == 1 else out


def stay(array):
    return array, array.shape, lambda *i: (0,) * array.ndim


def chip_product(places, lefts, weights, product, width, tile):
    length = lefts[0][0].shape[-2]
    count = length // 16
    inputs = lefts + weights

    def rows_of(ref, chip):
        parts = []
        for z in range(4):
            start = pl.multiple_of((z * 4 + chip) * count, count)
            parts.append(ref[pl.ds(start, count), :])
        return jnp.concatenate(parts, axis=0)

    def part(place, refs, flip_e, flip_x):
        e = 1 - place[0] if flip_e else place[0]
        x = 1 - place[1] if flip_x else place[1]
        rows = [rows_of(ref, e * 2 + x) for ref in refs[: len(lefts)]]
        out = product(rows, *refs[len(lefts) : len(inputs)])
        return out.astype(LOW).reshape(4, count, tile)

    def kernel(place, *refs):
        far = part(place, refs, True, True)
        refs[-5][...] = far[:2]
        refs[-4][...] = far[2:]
        refs[-3][...] = part(place, refs, True, False)
        refs[-2][...] = part(place, refs, False, True)
        refs[-1][...] = part(place, refs, False, False)

    out = lambda parts: (
        (parts, count, width), LOW, (parts, count, tile), lambda j: (0, 0, j),
    )
    outs = [out(2), out(2), out(4), out(4), out(4)]
    smem = pl.BlockSpec(memory_space=pltpu.SMEM)
    return call(kernel, (width // tile,), inputs, outs, (), [(places, smem)])


ATTN_TILE = 512


def feature_blocks(groups, rows):
    size = 8 * rows
    for g in range(groups):
        for k in range(4):
            start = (g * 4 + k) * size
            yield slice(start, start + size), slice(g * 8, g * 8 + 8), k


def project(all_in, weights):
    length = all_in.shape[0]
    eight, four, rows, _ = weights.shape
    tile = ATTN_TILE

    def kernel(a, w, out):
        total = jnp.zeros(out.shape, FULL)
        for columns, pieces, k in feature_blocks(eight // 8, rows):
            total += dot_nn(a[:, columns], w[pieces, k].reshape(8 * rows, tile))
        out[...] = total

    return call(
        kernel,
        (3,),
        [stay(all_in), (weights, (eight, four, rows, tile), lambda j: (0, 0, 0, j + 1))],
        [((length, 3 * tile), FULL, (length, tile), lambda j: (0, j))],
    )


def project_back(places, raw_grad, weights):
    eight, four, rows, columns = weights.shape
    tile = ATTN_TILE
    size = 8 * rows

    def product(lefts, w):
        return dot_nt(lefts[0], w[:, 0, :, tile : 4 * tile].reshape(size, 3 * tile))

    weight = (weights, (8, 1, rows, columns), lambda j: (j // 4, j % 4, 0, 0))
    width = eight // 8 * 4 * size
    return chip_product(places, [stay(raw_grad)], [weight], product, width, size)


def mix_out(places, mixed, weights):
    eight, four, rows, _ = weights.shape
    features = mixed.shape[1]
    tile = ATTN_TILE

    def product(lefts, w):
        return dot_nn(lefts[0], w[:, 0].reshape(features, tile))

    weight = (weights, (eight, 1, rows, tile), lambda j: (0, j, 0, 0))
    return chip_product(places, [stay(mixed)], [weight], product, four * tile, tile)


def mix_out_back(attn_grad, weights):
    length, width = attn_grad.shape
    eight, four, rows, _ = weights.shape
    tile = ATTN_TILE
    features = eight * rows
    part = min(length, 256)

    def kernel(a, w, out):
        total = jnp.zeros(out.shape, FULL)
        for k in range(four):
            right = w[:, k].reshape(features, tile)
            total += dot_nt(a[:, k * tile : (k + 1) * tile], right)
        out[...] = total.astype(LOW)

    return call(
        kernel,
        (length // part,),
        [
            (attn_grad, (part, width), lambda j: (j, 0)),
            (weights, (eight, four, rows, tile), lambda j: (0, 0, 0, 0)),
        ],
        [((length, features), LOW, (part, features), lambda j: (j, 0))],
    )


def gated(mlp_in, weights, waits):
    length = mlp_in.shape[0]
    eight, _, four, rows, count = weights.shape
    tile = min(count, 512)

    def kernel(a, gate_w, up_w, hidden, gate, up):
        both = []
        for w in (gate_w, up_w):
            total = jnp.zeros(gate.shape, FULL)
            for columns, pieces, k in feature_blocks(eight // 8, rows):
                total += dot_nn(a[:, columns], w[pieces, 0, k].reshape(8 * rows, tile))
            both.append(total)
        gate[...], up[...] = both
        hidden[...] = (both[0] * jax.nn.sigmoid(both[0]) * both[1]).astype(LOW)

    weight = lambda i: (
        weights, (eight, 1, four, rows, tile), lambda j: (0, i, 0, 0, j),
    )
    cut = ((length, tile), lambda j: (0, j))
    shape = (length, count)
    return call(
        kernel,
        (count // tile,),
        [stay(mlp_in), weight(0), weight(1)],
        [(shape, LOW) + cut, (shape, FULL) + cut, (shape, FULL) + cut],
        waits,
    )


def branch_out(places, hidden, weights):
    units = hidden.shape[1]
    eight, _, four, rows, width = weights.shape
    tile = min(width, 512)

    def product(lefts, w):
        return dot_nn(lefts[0], w[:, 0].reshape(units, tile))

    weight = (weights, (eight, 1, four, rows, tile), lambda j: (0, 2, 0, 0, j))
    return chip_product(places, [stay(hidden)], [weight], product, width, tile)


def gated_back(branch_rows, weights, gate_raw, up_raw):
    length, units = gate_raw.shape
    eight, _, four, rows, width = weights.shape
    tile = min(units, 512)
    pieces = tile // (four * rows)

    def kernel(a, w, gate, up, out):
        hidden_grad = dot_nt(a[...], w[:, 0].reshape(tile, width))
        raw = gate[...]
        sigmoid = jax.nn.sigmoid(raw)
        slope = sigmoid * (1.0 + raw * (1.0 - sigmoid))
        out[0] = (hidden_grad * up[...] * slope).astype(LOW)
        out[1] = (hidden_grad * raw * sigmoid).astype(LOW)

    cut = ((length, tile), lambda j: (0, j))
    return call(
        kernel,
        (units // tile,),
        [
            stay(branch_rows),
            (weights, (pieces, 1, four, rows, width), lambda j: (j, 2, 0, 0, 0)),
            (gate_raw,) + cut,
            (up_raw,) + cut,
        ],
        [((2, length, units), LOW, (2, length, tile), lambda j: (0, 0, j))],
    )


def input_back(places, grads, weights):
    _, length, units = grads.shape
    eight, _, four, rows, _ = weights.shape
    size = 8 * rows

    def product(lefts, gate_w, up_w):
        gate = dot_nt(lefts[0], gate_w[:, 0, 0].reshape(size, units))
        return gate + dot_nt(lefts[1], up_w[:, 0, 0].reshape(size, units))

    left = lambda i: (grads, (None, length, units), lambda j: (i, 0, 0))
    weight = lambda i: (
        weights, (8, 1, 1, rows, units), lambda j: (j // 4, i, j % 4, 0, 0),
    )
    width = eight // 8 * four * size
    return chip_product(
        places, [left(0), left(1)], [weight(0), weight(1)], product, width, size
    )


def down_grad(hidden, branch_rows, groups, rows):
    length, units = hidden[0].shape
    width = branch_rows[0].shape[1]
    run = 4 * rows
    many = 1 if run % 128 == 0 else 4
    shape = (4, groups, run, width)

    def kernel(a, b, c, d, out):
        total = dot_tn(a[...], b[...]) + dot_tn(c[...], d[...])
        out[...] = total.astype(LOW).reshape(out.shape)

    cut = ((length, many * run), lambda g, j: (0, g * (4 // many) + j))
    return call(
        kernel,
        (groups, 4 // many),
        [
            (hidden[0],) + cut,
            stay(branch_rows[0]),
            (hidden[1],) + cut,
            stay(branch_rows[1]),
        ],
        [(shape, LOW, (many, 1, run, width), lambda g, j: (j, g, 0, 0))],
    )


def lay_features(total, out, many, rows):
    for i in range(many):
        for j in range(4):
            start = (i * 4 + j) * rows
            yield (j, i), total[start : start + rows]


def units_grad(mlp_in, grads, groups, rows):
    length = mlp_in[0].shape[0]
    units = grads[0].shape[2]
    run = 4 * rows
    many = 1 if run % 128 == 0 else 4
    shape = (4, 2, groups, 4, rows, units)

    def kernel(a, b, c, d, out):
        total = (dot_tn(a[...], b[0]) + dot_tn(c[...], d[0])).astype(LOW)
        for (j, i), part in lay_features(total, out, many, rows):
            out[j, 0, 0, i] = part

    cut = ((length, many * run), lambda i, g, j: (0, g * (4 // many) + j))
    right = ((1, length, units), lambda i, g, j: (i, 0, 0))
    return call(
        kernel,
        (2, groups, 4 // many),
        [
            (mlp_in[0],) + cut,
            (grads[0],) + right,
            (mlp_in[1],) + cut,
            (grads[1],) + right,
        ],
        [
            (
                shape,
                LOW,
                (4, 1, 1, many, rows, units),
                lambda i, g, j: (0, i, g, j, 0, 0),
            )
        ],
    )


def attention_grad(all_in, raw_grad, mixed, attn_grad, groups, rows, waits):
    length = all_in[0].shape[0]
    tile = ATTN_TILE
    run = 4 * rows
    many = 1 if run % 128 == 0 else 4
    shape = (4, groups, 4, rows, 4 * tile)

    def kernel(a, b, c, d, e, f, p, q, out):
        total = (dot_tn(a[...], b[...]) + dot_tn(c[...], d[...])).astype(LOW)
        for (j, i), part in lay_features(total, out, many, rows):
            out[j, 0, i, :, tile:] = part
        total = (dot_tn(e[0], f[...]) + dot_tn(p[0], q[...])).astype(LOW)
        for i in range(many):
            for j in range(4):
                part = total[j * rows : (j + 1) * rows, i * tile : (i + 1) * tile]
                out[j, 0, i, :, :tile] = part

    cut = ((length, many * run), lambda g, j: (0, g * (4 // many) + j))
    left = ((1, length, run), lambda g, j: (g, 0, 0))
    right = ((length, many * tile), lambda g, j: (0, j))
    return call(
        kernel,
        (groups, 4 // many),
        [
            (all_in[0],) + cut,
            stay(raw_grad[0]),
            (all_in[1],) + cut,
            stay(raw_grad[1]),
            (mixed[0],) + left,
            (attn_grad[0],) + right,
            (mixed[1],) + left,
            (attn_grad[1],) + right,
        ],
        [(shape, LOW, (4, 1, many, rows, 4 * tile), lambda g, j: (0, g, j, 0, 0))],
        waits,
    )


def wide(value):
    return value.astype(FULL)


def tie(values, others):
    if not others:
        return tuple(values)
    return lax.optimization_barrier(tuple(values) + tuple(others))[: len(values)]


def two_halves(first, second, waits):
    half = (first.shape[0] // 2,) + first.shape[1:]

    def kernel(a, b, a_out, b_out):
        a_out[...] = a[...]
        b_out[...] = b[...]

    out = (half, first.dtype, half, lambda i: (0, 0, 0))
    return call(
        kernel,
        (1,),
        [(first, half, lambda i: (0, 0, 0)), (second, half, lambda i: (1, 0, 0))],
        [out, out],
        waits,
        work=0,
    )


def hold(value, *others):
    def kernel(a, out):
        out[...] = a[...]

    shape = value.shape
    whole = (shape, lambda i: (0,) * len(shape))
    return call(kernel, (1,), [(value,) + whole], [(shape, value.dtype) + whole], others, work=0)


class Steps:
    def __init__(self):
        self.last = ()

    def wait(self, *values):
        self.last += tuple(jax.tree.leaves(values))

    def __call__(self, step, *inputs):
        flat, tree = jax.tree.flatten(inputs)
        out = step(*tree.unflatten(tie(flat, self.last)))
        self.last = tuple(jax.tree.leaves(out))
        return out


class Links:
    def __init__(self, steps):
        self.steps = steps

    def send(self, value, axes, pairs):
        (value,) = tie((value,), self.steps.last)
        return lax.ppermute(value, axes, pairs)

    def swap(self, value, axis):
        return self.send(value, axis, SWAP)

    def swap_both(self, value, first, second):
        return self.send(value, (first, second), BOTH)


def swap(value, axis):
    return lax.ppermute(value, axis, SWAP)


def pick(value, places):
    starts = [0] * value.ndim
    sizes = list(value.shape)
    for dim, place in places.items():
        starts[dim] = place
        sizes[dim] = 1
    taken = lax.dynamic_slice(value, starts, sizes)
    return taken.reshape([s for d, s in enumerate(value.shape) if d not in places])


def put(out, parts):
    for value, starts in parts:
        out = lax.dynamic_update_slice(out, value, starts)
    return out


class Place:
    def __init__(self):
        self.g, self.e, self.x, self.c, self.h, self.l = (lax.axis_index(a) for a in AXES)
        self.groups = lax.axis_size("g")
        self.steps = Steps()
        self.links = Links(self.steps)


class Spread:
    def __init__(self, at, part, inputs, first="e", second="x"):
        self.at, self.places = at, (getattr(at, first), getattr(at, second))
        a, b = self.places

        def start(*inputs):
            return tuple(part(i, j, *inputs) for i in (a, 1 - a) for j in (b, 1 - b))

        self.mine, for_b, for_a, far = at.steps(start, *inputs)
        self.from_a = at.links.swap(for_a, first)
        self.from_b = at.links.swap(for_b, second)
        self.far = at.links.swap_both(far, first, second)
        self.sent = (self.mine, for_b, for_a, far)
        self.came = (self.from_a, self.from_b, self.far)

    def second(self, lay):
        a, b = self.places

        def join(mine, from_a, from_b, far):
            return lay(
                [(mine, a, b), (from_a, 1 - a, b), (from_b, a, 1 - b), (far, 1 - a, 1 - b)]
            )

        return self.at.steps(join, self.mine, self.from_a, self.from_b, self.far)


def one_of(i, j, parts):
    return pick(parts, {0: i, 1: j})


def lay_all(parts):
    shape = parts[0][0].shape
    out = jnp.zeros((2, 2) + shape, parts[0][0].dtype)
    tail = (0,) * len(shape)
    return put(out, [(v.reshape((1, 1) + shape), (i, j) + tail) for v, i, j in parts])


class TokensIn:
    def __init__(self, at, rows):
        self.at = at
        self.spread = Spread(at, one_of, [rows.reshape(2, 2, -1, rows.shape[1])])

    def second(self):
        self.spread = Spread(self.at, one_of, [self.spread.second(lay_all)], "h", "l")

    def third(self):
        def lay(parts):
            out = lay_all(parts)
            return out.reshape((4,) + out.shape[2:])

        return self.spread.second(lay)


class TokensOut:
    def __init__(self, at, blocks):
        self.at = at
        blocks = blocks.reshape((2, 2) + blocks.shape[1:])
        self.spread = Spread(at, one_of, [blocks], "h", "l")

    def second(self):
        self.spread = Spread(self.at, one_of, [self.spread.second(lay_all)])

    def third(self):
        def lay(parts):
            out = lay_all(parts)
            return out.reshape(-1, out.shape[-1])

        return self.spread.second(lay)


class GatherTokens:
    def __init__(self, at, blocks):
        self.at, self.blocks = at, blocks
        self.from_e = at.links.swap(blocks, "e")
        self.from_x = at.links.swap(blocks, "x")

    def second(self, waits=()):
        at = self.at
        half_e, half_x = at.steps(two_halves, self.from_e, self.from_x, waits)
        self.far_0 = at.links.swap(half_e, "x")
        self.far_1 = at.links.swap(half_x, "e")
        four, count, width = self.blocks.shape
        cut = (four, 1, 1, count, width)

        def near(blocks, from_x, from_e):
            out = jnp.zeros((four, 2, 2, count, width), blocks.dtype)
            parts = [
                (blocks.reshape(cut), (0, at.e, at.x, 0, 0)),
                (from_x.reshape(cut), (0, at.e, 1 - at.x, 0, 0)),
                (from_e.reshape(cut), (0, 1 - at.e, at.x, 0, 0)),
            ]
            return put(out, parts)

        self.out = at.steps(near, self.blocks, self.from_x, self.from_e)

    def third(self):
        at = self.at
        four, count, width = self.blocks.shape
        cut = (2, 1, 1, count, width)

        def far(out, far_0, far_1):
            parts = [
                (far_0.reshape(cut), (0, 1 - at.e, 1 - at.x, 0, 0)),
                (far_1.reshape(cut), (2, 1 - at.e, 1 - at.x, 0, 0)),
            ]
            return put(out, parts).reshape(-1, width)

        return at.steps(far, self.out, self.far_0, self.far_1)


class ScatterTokens:
    def __init__(self, at, product, *inputs):
        self.at = at
        far_0, far_1, self.for_e, self.for_x, self.mine = at.steps(product, *inputs)
        self.for_e_0 = at.links.swap(far_0, "x")
        self.for_x_1 = at.links.swap(far_1, "e")

    def second(self):
        at = self.at

        def add(for_e, for_x, for_e_0, for_x_1):
            for_e_0 = (wide(for_e[:2]) + wide(for_e_0)).astype(LOW)
            for_x_1 = (wide(for_x[2:]) + wide(for_x_1)).astype(LOW)
            return jnp.concatenate([for_e_0, for_e[2:]]), jnp.concatenate([for_x[:2], for_x_1])

        for_e, for_x = at.steps(add, self.for_e, self.for_x, self.for_e_0, self.for_x_1)
        self.from_e = at.links.swap(for_e, "e")
        self.from_x = at.links.swap(for_x, "x")

    def third(self, step, *inputs):
        def add(mine, from_e, from_x, *inputs):
            return step(wide(mine) + wide(from_e) + wide(from_x), *inputs)

        return self.at.steps(add, self.mine, self.from_e, self.from_x, *inputs)


def sum_chips(value):
    far = lax.ppermute(value, ("e", "x"), BOTH)
    return value + swap(value, "x") + swap(value, "e") + far


def gather(at, piece, *others):
    (piece,) = tie((piece,), at.steps.last + others)
    return lax.all_gather(piece, ("g", "c", "h", "l"), axis=0)


def scatter(at, value, *others):
    (value,) = tie((value,), at.steps.last + others)
    value = lax.psum_scatter(value, ("h", "l"), scatter_dimension=0)
    return value


def scatter_groups(at, value, dim):
    if at.groups == 1:
        return value.reshape([n for d, n in enumerate(value.shape) if d != dim])
    return lax.psum_scatter(value, "g", scatter_dimension=dim)


def halves(value, core, runs):
    rows, count = value.shape
    each = count // (2 * runs)

    def of(place):
        parts = [
            lax.dynamic_slice(value, (0, (2 * k + place) * each), (rows, each))
            for k in range(runs)
        ]
        return jnp.concatenate(parts, axis=1)

    return of(core), of(1 - core)


class ScatterGains:
    def __init__(self, at, grads):
        self.at = at
        value = grads.reshape(grads.shape[0], at.groups, 2, 2, 2, 2, 2, -1)
        if at.groups > 1:
            value = lax.psum_scatter(value, "g", scatter_dimension=1, tiled=True)
        self.value = value.reshape(value.shape[:1] + value.shape[2:])
        self.axes = ["e", "x", "c", "h", "l"]
        self.start()

    def start(self):
        place = getattr(self.at, self.axes[0])
        self.kept, send = self.at.steps(
            lambda v: (pick(v, {1: place}), pick(v, {1: 1 - place})), self.value
        )
        self.got = self.at.links.swap(send, self.axes.pop(0))

    def more(self, waits=()):
        self.value = self.at.steps(lambda a, b: a + b, self.kept, self.got)
        if waits:
            self.value = hold(self.value, *waits)
        if self.axes:
            self.start()
        return self.value


def rope_tables(places, head_dim):
    half_dim = head_dim // 2
    inverse = jnp.power(
        jnp.float32(ROPE_THETA), -(jnp.arange(half_dim, dtype=FULL) * 2.0 / head_dim)
    )
    angles = places.astype(FULL)[:, None] * inverse[None, :]
    sine = jnp.sin(angles)
    cosine = jnp.cos(angles)
    return (
        jnp.concatenate([cosine, cosine], axis=-1),
        jnp.concatenate([-sine, sine], axis=-1),
    )


def norm_forward(tensor, gain_vec):
    inverse = lax.rsqrt(jnp.mean(tensor * tensor, axis=-1, keepdims=True) + EPSILON)
    unit = tensor * inverse
    return unit * gain_vec, unit, inverse


def norm_backward(grad_in, unit, inverse, gain_vec):
    axes = tuple(range(grad_in.ndim - 1))
    gain_grad = jnp.sum(grad_in * unit, axis=axes)
    unit_grad = grad_in * gain_vec
    inner = jnp.mean(unit_grad * unit, axis=-1, keepdims=True)
    return inverse * (unit_grad - unit * inner), gain_grad


def on_device(
    hidden_in,
    q_weight,
    k_weight,
    v_weight,
    o_weight,
    q_gain,
    k_gain,
    attn_gain,
    gate_weight,
    up_weight,
    down_weight,
    mlp_gain,
    out_grad,
):
    at = Place()
    steps = at.steps
    batch, rows_here, width = hidden_in.shape
    head_dim = width // HEADS
    length = batch * rows_here * 4
    rows_owned = q_weight.shape[0]
    groups = at.groups
    ff_block = down_weight.shape[0]

    assert head_dim % (8 * rows_owned) == 0 or (8 * rows_owned) % head_dim == 0
    assert ff_block == 4 * rows_owned

    def columns_of(e, x, weight):
        rows, count = weight.shape
        part = count // (4 * groups)
        each = [
            lax.dynamic_slice(weight, (0, ((g * 2 + e) * 2 + x) * part), (rows, part))
            for g in range(groups)
        ]
        return jnp.concatenate(each, axis=1)

    def lay_columns(parts):
        rows, count = parts[0][0].shape
        part = count // groups
        out = jnp.zeros((rows, 4 * count), FULL)
        for value, e, x in parts:
            for g in range(groups):
                piece = wide(value[:, g * part : (g + 1) * part])
                out = lax.dynamic_update_slice(out, piece, (0, ((g * 2 + e) * 2 + x) * part))
        return out

    quarter = width // 4

    def columns_of_attention(e, x, q, k, v, o, gains):
        three = [columns_of(e, x, w) for w in (q, k, v)]
        return jnp.concatenate(three + [gains], axis=1)

    def lay_attention(parts):
        tail = lay_all(parts)
        tail = tail.reshape((4,) + tail.shape[2:])
        runs = jnp.stack([o_weight[:, k * quarter : (k + 1) * quarter] for k in range(4)])
        return jnp.concatenate([runs, tail], axis=2)

    def lay_four(parts):
        out = lay_all(parts)
        return out.reshape((4,) + out.shape[2:])

    def lay_three(parts):
        return tuple(
            lay_columns([(v[:, i * quarter : (i + 1) * quarter], e, x) for v, e, x in parts])
            for i in range(3)
        )

    places = jnp.stack([at.e, at.x]).astype(jnp.int32)

    def here(vector):
        return pick(vector.reshape(groups, 2, 2, -1), {1: at.e, 2: at.x}).reshape(1, -1)

    def whole(vector):
        out = jnp.zeros((groups, 2, 2, vector.size // groups), FULL)
        part = vector.reshape(groups, 1, 1, -1)
        return lax.dynamic_update_slice(out, part, (0, at.e, at.x, 0)).reshape(-1)

    def pair(halved, core_sent):
        return halved, at.links.swap(core_sent, "c")

    gains = jnp.stack([q_gain, k_gain, attn_gain, mlp_gain], axis=1)
    gains = jnp.pad(gains, ((0, 0), (0, 124)))
    attn_spread = Spread(
        at, columns_of_attention, [q_weight, k_weight, v_weight, o_weight, gains]
    )
    own = TokensIn(at, hidden_in.reshape(-1, width))
    gate_spread = Spread(at, columns_of, [gate_weight])
    up_spread = Spread(at, columns_of, [up_weight])
    attn_all = gather(at, attn_spread.second(lay_attention))
    own.second()
    cosine, sine = steps(lambda n: rope_tables(n, head_dim), jnp.arange(length))
    gate_mine = gate_spread.second(lay_four)
    up_mine = up_spread.second(lay_four)
    mlp_mine = steps(
        lambda *v: jnp.stack(v), gate_mine, up_mine, down_weight.reshape((4, -1, width))
    )
    mlp_all = gather(at, mlp_mine)
    own_in = own.third()
    all_in = GatherTokens(at, own_in)
    all_in.second()
    all_in = all_in.third()
    all_in_half = pair(*steps(lambda v: halves(v, at.c, 4 * groups), all_in))
    top = TokensIn(at, out_grad.reshape(-1, width))
    steps.wait(all_in_half)

    def gains_of(weights):
        value = wide(weights[..., -128:-124]).reshape(groups, 8, 4, rows_owned, 4)
        return value.transpose(4, 0, 2, 1, 3).reshape(4, -1)

    gains = steps(gains_of, attn_all)
    q_gain_here, k_gain_here = here(gains[0]), here(gains[1])
    attn_gain_all, mlp_gain_all = gains[2], gains[3]

    def squares_of(raw):
        q_raw, k_raw = jnp.split(raw[:, : 2 * quarter], 2, axis=1)
        return jnp.stack([jnp.sum(q_raw * q_raw, -1), jnp.sum(k_raw * k_raw, -1)])

    raw = steps(project, all_in, attn_all)
    squares = sum_chips(steps(squares_of, raw))
    inverse = steps(lambda s: lax.rsqrt(s / width + EPSILON).T, squares)
    queries, keys, values, mixed = steps(
        attend, raw, inverse, q_gain_here, k_gain_here, cosine, sine
    )
    attn_out = ScatterTokens(at, mix_out, places, mixed, attn_all)

    def halve_mixed(mixed):
        return [
            v.reshape(length, groups, -1).swapaxes(0, 1) for v in halves(mixed, at.c, groups)
        ]

    mixed_half = pair(*steps(halve_mixed, mixed))
    steps.wait(mixed_half)
    attn_out.second()

    def after_attention(attn_out, own_in, gain):
        normed, unit, inverse = norm_forward(attn_out, gain)
        residual = wide(own_in) + normed
        return residual.astype(LOW), residual, unit, inverse

    residual_low, residual, attn_unit, attn_inverse = attn_out.third(
        after_attention, own_in, attn_gain_all
    )

    mlp_in = GatherTokens(at, residual_low)
    mlp_in.second()
    mlp_in = mlp_in.third()
    mlp_in_half = pair(*steps(lambda v: halves(v, at.c, 4 * groups), mlp_in))
    steps.wait(mlp_in_half)
    hidden, gate_raw, up_raw = steps(gated, mlp_in, mlp_all, top.spread.came)
    top.second()
    branch = ScatterTokens(at, branch_out, places, hidden, mlp_all)
    hidden_half = pair(*steps(lambda v: halves(v, at.c, groups), hidden))
    steps.wait(hidden_half)
    branch.second()
    own_top = top.third()

    def after_mlp(branch, residual, own_top, gain):
        normed, unit, inverse = norm_forward(branch, gain)
        grad, gain_grad = norm_backward(wide(own_top), unit, inverse, gain)
        return grad.astype(LOW), (residual + normed).astype(LOW), gain_grad

    branch_low, own_out, mlp_gain_grad = branch.third(
        after_mlp, residual, own_top, mlp_gain_all
    )

    branch_rows = GatherTokens(at, branch_low)
    layer_out = TokensOut(at, own_out)
    branch_rows.second(layer_out.spread.came)
    branch_rows = branch_rows.third()
    branch_rows = (branch_rows, at.links.swap(branch_rows, "c"))
    unit_grads = steps(gated_back, branch_rows[0], mlp_all, gate_raw, up_raw)
    unit_grads = (unit_grads, at.links.swap(unit_grads, "c"))
    grad = steps(lambda a, b: down_grad(a, b, groups, rows_owned), hidden_half, branch_rows)
    down_own = scatter(at, grad)
    input_part = ScatterTokens(at, input_back, places, unit_grads[0], mlp_all)
    grad = steps(lambda a, b: units_grad(a, b, groups, rows_owned), mlp_in_half, unit_grads)
    units_own = scatter(at, grad)
    input_part.second()
    layer_out.second()
    layer_out_came = layer_out.spread.came

    def before_attention(input_grad, own_top, unit, inverse, gain):
        residual_grad = wide(own_top) + input_grad
        grad, gain_grad = norm_backward(residual_grad, unit, inverse, gain)
        return grad.astype(LOW), residual_grad, gain_grad

    attn_grad, residual_grad, attn_gain_grad = input_part.third(
        before_attention, own_top, attn_unit, attn_inverse, attn_gain_all
    )

    attn_low = GatherTokens(at, attn_grad)
    layer_out = layer_out.third()
    attn_low.second()
    attn_low = attn_low.third()
    attn_low = (attn_low, swap(attn_low, "c"))
    mixed_grad = steps(mix_out_back, attn_low[0], attn_all)
    q_scaled, k_scaled, v_low, inner, q_gain_grad, k_gain_grad = steps(
        attend_back, queries, keys, values, mixed_grad, raw, inverse,
        q_gain_here, k_gain_here, cosine, sine, (down_own,) + layer_out_came,
    )
    inner = sum_chips(steps(lambda v: v.T / width, inner))

    def before_project(raw, inverse, q_scaled, k_scaled, v_low, inner):
        q_raw, k_raw = jnp.split(raw[:, : 2 * quarter], 2, axis=1)
        inner = inner.T
        grads = []
        for i, (part, scaled) in enumerate([(q_raw, q_scaled), (k_raw, k_scaled)]):
            each = inverse[:, i : i + 1]
            grads.append((each * (scaled - part * each * inner[:, i : i + 1])).astype(LOW))
        return jnp.concatenate(grads + [v_low], axis=1)

    raw_grad = steps(before_project, raw, inverse, q_scaled, k_scaled, v_low, inner)
    raw_grad = (raw_grad, swap(raw_grad, "c"))
    in_part = ScatterTokens(at, project_back, places, raw_grad[0], attn_all)
    attn_grad_part = steps(
        lambda *v: attention_grad(*v[:-1], groups, rows_owned, v[-1:]),
        all_in_half, raw_grad, mixed_half, attn_low, units_own,
    )
    attn_own = scatter(at, attn_grad_part)
    in_part.second()
    gains = jnp.stack([whole(q_gain_grad), whole(k_gain_grad), attn_gain_grad, mlp_gain_grad])
    gains = ScatterGains(at, gains)
    in_grad = in_part.third(lambda a, b: (a + b).astype(LOW), residual_grad)
    in_grad = TokensOut(at, in_grad)
    gains.more()
    gains.more()
    units_own = scatter_groups(at, units_own, 1)
    gate_spread = Spread(at, one_of, [units_own[0].reshape(2, 2, rows_owned, -1)])
    up_spread = Spread(at, one_of, [units_own[1].reshape(2, 2, rows_owned, -1)])
    gate_own = gate_spread.second(lay_columns)
    up_own = up_spread.second(lay_columns)
    in_grad.second()
    attn_own = scatter_groups(at, attn_own, 0)
    attn_spread = Spread(
        at, one_of, [attn_own[..., quarter:].reshape(2, 2, rows_owned, -1)]
    )
    gains.more(attn_spread.sent)
    in_grad = in_grad.third()
    o_own = wide(jnp.concatenate([attn_own[k, :, :quarter] for k in range(4)], axis=1))
    gains.more()
    own_three = list(attn_spread.second(lay_three))
    down_own = wide(scatter_groups(at, down_own, 0))
    gains = gains.more()
    shape = hidden_in.shape
    grads = own_three + [o_own, gate_own, up_own, down_own]
    return (layer_out.reshape(shape), in_grad.reshape(shape)) + tuple(grads) + tuple(gains)


def solution(mesh):
    dp, seq = mesh.shape["dp"], mesh.shape["seq"]
    split = Mesh(mesh.devices.reshape(dp // 8, 2, 2, 2, seq // 2, 2), AXES)
    dp_axes, seq_axes = AXES[:4], AXES[4:]
    tokens = P(dp_axes, seq_axes, None)
    matrix, vector = P(AXES, None), P(AXES)
    return jax.shard_map(
        on_device,
        mesh=split,
        in_specs=(tokens,)
        + (matrix,) * 4
        + (vector,) * 3
        + (matrix,) * 3
        + (vector, tokens),
        out_specs=(tokens,) * 2 + (matrix,) * 7 + (vector,) * 4,
        check_vma=False,
    )
```

```python
import math

import jax
import jax.numpy as jnp
from jax import lax
from jax.experimental import pallas as pl
from jax.experimental.pallas import tpu as pltpu
from jax.sharding import Mesh
from jax.sharding import PartitionSpec as P

HEADS = 16
EPSILON = 1e-06
ROPE_THETA = 500000.0
LOW = jnp.bfloat16
FULL = jnp.float32

AXES = ("g", "e", "x", "c", "h", "l")
SWAP = [(0, 1), (1, 0)]
BOTH = [(i, 3 - i) for i in range(4)]
VMEM_LIMIT = 56 * 1024 * 1024


BLOCK = 256

def dot_nt(a, b):
    return lax.dot_general(a, b, (((1,), (1,)), ((), ())), preferred_element_type=FULL)

def dot_nn(a, b):
    return lax.dot_general(a, b, (((1,), (0,)), ((), ())), preferred_element_type=FULL)

def dot_tn(a, b):
    return lax.dot_general(a, b, (((0,), (0,)), ((), ())), preferred_element_type=FULL)

def turn(tensor):
    return pltpu.roll(tensor, tensor.shape[1] // 2, 1)


def attend_kernel(q_raw, k_raw, v_raw, inverse, q_gain, k_gain, cosine, sine,
                  q_out, k_out, v_out, mixed):
    length, head_dim = q_raw.shape
    factor = 1.0 / math.sqrt(head_dim)
    block = min(BLOCK, length)

    def rope(raw, column, gain):
        normed = raw[...] * inverse[:, column : column + 1] * gain[...]
        return (normed * cosine[...] + turn(normed) * sine[...]).astype(LOW)

    q_out[...] = rope(q_raw, 0, q_gain)
    k_out[...] = rope(k_raw, 1, k_gain)
    v_out[...] = v_raw[...].astype(LOW)
    shape = (block, block)
    allowed = lax.broadcasted_iota(jnp.int32, shape, 1) <= lax.broadcasted_iota(jnp.int32, shape, 0)
    for start in range(0, length, block):
        here = slice(start, start + block)
        queries = q_out[here, :]
        near = jnp.where(allowed, dot_nt(queries, k_out[here, :]) * factor, -1e30)
        top = jnp.max(near, axis=1, keepdims=True)
        if start:
            far = dot_nt(queries, k_out[:start, :]) * factor
            top = jnp.maximum(top, jnp.max(far, axis=1, keepdims=True))
            far = jnp.exp(far - top)
        near = jnp.exp(near - top)
        total = jnp.sum(near, axis=1, keepdims=True)
        if start:
            total += jnp.sum(far, axis=1, keepdims=True)
        scale = 1.0 / total
        out = dot_nn((near * scale).astype(LOW), v_out[here, :])
        if start:
            out += dot_nn((far * scale).astype(LOW), v_out[:start, :])
        mixed[here, :] = out.astype(LOW)


def attend(raw, inverse, q_gain, k_gain, cosine, sine):
    length = raw.shape[0]
    head_dim = cosine.shape[1]
    width = q_gain.shape[1]
    heads = width // head_dim
    column = lambda shift: pl.BlockSpec((length, head_dim), lambda i: (0, i + shift * heads))
    whole = lambda v: pl.BlockSpec(v.shape, lambda i: (0, 0))
    gain = pl.BlockSpec((1, head_dim), lambda i: (0, i))
    out = jax.ShapeDtypeStruct((length, width), LOW)
    return pl.pallas_call(
        attend_kernel,
        grid=(heads,),
        in_specs=[column(0), column(1), column(2), whole(inverse), gain, gain, whole(cosine), whole(sine)],
        out_specs=[column(0)] * 4,
        out_shape=[out] * 4,
        compiler_params=pltpu.CompilerParams(vmem_limit_bytes=VMEM_LIMIT),
        cost_estimate=pl.CostEstimate(flops=0, bytes_accessed=0, transcendentals=0),
    )(raw, raw, raw, inverse, q_gain, k_gain, cosine, sine)


def attend_back_kernel(queries, keys, values, mixed_grad, q_raw, k_raw, inverse, q_gain, k_gain, cosine, sine,
                       q_grad, k_grad, v_grad, sums, q_gain_grad, k_gain_grad, k_total, v_total):
    length, head_dim = queries.shape
    factor = 1.0 / math.sqrt(head_dim)
    block = min(BLOCK, length)
    shape = (block, block)
    allowed = lax.broadcasted_iota(jnp.int32, shape, 0) <= lax.broadcasted_iota(jnp.int32, shape, 1)
    first = pl.program_id(0) == 0

    def unrope(grad, raw, column, gain, rows):
        pre = grad * cosine[rows, :] - turn(grad) * sine[rows, :]
        unit = raw[rows, :] * inverse[rows, column : column + 1]
        scaled = pre * gain[...]
        return scaled, jnp.sum(scaled * unit, axis=1, keepdims=True), jnp.sum(pre * unit, axis=0, keepdims=True)

    q_gain_total = jnp.zeros((1, head_dim), FULL)
    for start in range(0, length, block):
        here = slice(start, start + block)
        query, out_grad = queries[here, :], mixed_grad[here, :]
        near = jnp.where(allowed, dot_nt(keys[here, :], query) * factor, -1e30)
        top = jnp.max(near, axis=0, keepdims=True)
        if start:
            far = dot_nt(keys[:start, :], query) * factor
            top = jnp.maximum(top, jnp.max(far, axis=0, keepdims=True))
            far = jnp.exp(far - top)
        near = jnp.exp(near - top)
        total = jnp.sum(near, axis=0, keepdims=True)
        if start:
            total += jnp.sum(far, axis=0, keepdims=True)
        scale = 1.0 / total
        near = near * scale
        near_grad = dot_nt(values[here, :], out_grad)
        inner = jnp.sum(near * near_grad, axis=0, keepdims=True)
        if start:
            far = far * scale
            far_grad = dot_nt(values[:start, :], out_grad)
            inner += jnp.sum(far * far_grad, axis=0, keepdims=True)
        near_score = (near * (near_grad - inner) * factor).astype(LOW)
        grad = dot_tn(near_score, keys[here, :])
        k_total[here, :] = dot_nn(near_score, query)
        v_total[here, :] = dot_nn(near.astype(LOW), out_grad)
        if start:
            far_score = (far * (far_grad - inner) * factor).astype(LOW)
            grad += dot_tn(far_score, keys[:start, :])
            k_total[:start, :] += dot_nn(far_score, query)
            v_total[:start, :] += dot_nn(far.astype(LOW), out_grad)
        scaled, row_sum, gain_part = unrope(grad, q_raw, 0, q_gain, here)
        q_grad[here, :] = scaled
        q_gain_total += gain_part
        sums[here, 0:1] = jnp.where(first, row_sum, sums[here, 0:1] + row_sum)
    q_gain_grad[...] = q_gain_total
    scaled, row_sum, gain_part = unrope(k_total[...], k_raw, 1, k_gain, slice(None))
    k_grad[...] = scaled
    k_gain_grad[...] = gain_part
    sums[:, 1:2] = jnp.where(first, row_sum, sums[:, 1:2] + row_sum)
    v_grad[...] = v_total[...].astype(LOW)


def attend_back(
    queries, keys, values, mixed_grad, raw, inverse, q_gain, k_gain, cosine, sine, waits
):
    length, width = queries.shape
    head_dim = cosine.shape[1]
    heads = width // head_dim
    column = lambda shift: pl.BlockSpec((length, head_dim), lambda i: (0, i + shift * heads))
    whole = lambda v: pl.BlockSpec(v.shape, lambda i: (0, 0))
    gain = pl.BlockSpec((1, head_dim), lambda i: (0, i))
    wide = jax.ShapeDtypeStruct((length, width), FULL)
    vector = jax.ShapeDtypeStruct((1, width), FULL)
    def body(*refs):
        attend_back_kernel(*refs[:11], *refs[11 + len(waits) :])

    return pl.pallas_call(
        body,
        grid=(heads,),
        in_specs=[column(0)] * 4 + [column(0), column(1), whole(inverse), gain, gain, whole(cosine), whole(sine)]
        + [pl.BlockSpec(memory_space=pl.ANY)] * len(waits),
        out_specs=[column(0)] * 3 + [pl.BlockSpec((length, 2), lambda i: (0, 0)), gain, gain],
        out_shape=[wide, wide, jax.ShapeDtypeStruct((length, width), LOW), jax.ShapeDtypeStruct((length, 2), FULL), vector, vector],
        scratch_shapes=[pltpu.VMEM((length, head_dim), FULL)] * 2,
        compiler_params=pltpu.CompilerParams(vmem_limit_bytes=VMEM_LIMIT),
        cost_estimate=pl.CostEstimate(flops=0, bytes_accessed=0, transcendentals=0),
    )(queries, keys, values, mixed_grad, raw, raw, inverse, q_gain, k_gain, cosine, sine, *waits)

def call(kernel, grid, inputs, outputs, waits=(), scalars=(), work=2**33):
    count = len(scalars) + len(inputs)

    def body(*refs):
        kernel(*refs[:count], *refs[count + len(waits) :])

    out = pl.pallas_call(
        body,
        grid=grid,
        in_specs=[spec for _, spec in scalars]
        + [pl.BlockSpec(block, index) for _, block, index in inputs]
        + [pl.BlockSpec(memory_space=pl.ANY)] * len(waits),
        out_specs=[pl.BlockSpec(block, index) for _, _, block, index in outputs],
        out_shape=[jax.ShapeDtypeStruct(shape, kind) for shape, kind, _, _ in outputs],
        compiler_params=pltpu.CompilerParams(vmem_limit_bytes=VMEM_LIMIT),
        cost_estimate=pl.CostEstimate(flops=work, bytes_accessed=0, transcendentals=0),
    )(*(v for v, _ in scalars), *(v for v, _, _ in inputs), *waits)
    return out[0] if len(outputs) == 1 else out


def stay(array):
    return array, array.shape, lambda *i: (0,) * array.ndim


def chip_product(places, lefts, weights, product, width, tile):
    length = lefts[0][0].shape[-2]
    count = length // 16
    inputs = lefts + weights

    def rows_of(ref, chip):
        parts = []
        for z in range(4):
            start = pl.multiple_of((z * 4 + chip) * count, count)
            parts.append(ref[pl.ds(start, count), :])
        return jnp.concatenate(parts, axis=0)

    def part(place, refs, flip_e, flip_x):
        e = 1 - place[0] if flip_e else place[0]
        x = 1 - place[1] if flip_x else place[1]
        rows = [rows_of(ref, e * 2 + x) for ref in refs[: len(lefts)]]
        out = product(rows, *refs[len(lefts) : len(inputs)])
        return out.astype(LOW).reshape(4, count, tile)

    def kernel(place, *refs):
        far = part(place, refs, True, True)
        refs[-5][...] = far[:2]
        refs[-4][...] = far[2:]
        refs[-3][...] = part(place, refs, True, False)
        refs[-2][...] = part(place, refs, False, True)
        refs[-1][...] = part(place, refs, False, False)

    out = lambda parts: (
        (parts, count, width), LOW, (parts, count, tile), lambda j: (0, 0, j),
    )
    outs = [out(2), out(2), out(4), out(4), out(4)]
    smem = pl.BlockSpec(memory_space=pltpu.SMEM)
    return call(kernel, (width // tile,), inputs, outs, (), [(places, smem)])


ATTN_TILE = 512


def feature_blocks(groups, rows):
    size = 8 * rows
    for g in range(groups):
        for k in range(4):
            start = (g * 4 + k) * size
            yield slice(start, start + size), slice(g * 8, g * 8 + 8), k


def project(all_in, weights):
    length = all_in.shape[0]
    eight, four, rows, _ = weights.shape
    tile = ATTN_TILE

    def kernel(a, w, out):
        total = jnp.zeros(out.shape, FULL)
        for columns, pieces, k in feature_blocks(eight // 8, rows):
            total += dot_nn(a[:, columns], w[pieces, k].reshape(8 * rows, tile))
        out[...] = total

    return call(
        kernel,
        (3,),
        [stay(all_in), (weights, (eight, four, rows, tile), lambda j: (0, 0, 0, j + 1))],
        [((length, 3 * tile), FULL, (length, tile), lambda j: (0, j))],
    )


def project_back(places, raw_grad, weights):
    eight, four, rows, columns = weights.shape
    tile = ATTN_TILE
    size = 8 * rows

    def product(lefts, w):
        return dot_nt(lefts[0], w[:, 0, :, tile : 4 * tile].reshape(size, 3 * tile))

    weight = (weights, (8, 1, rows, columns), lambda j: (j // 4, j % 4, 0, 0))
    width = eight // 8 * 4 * size
    return chip_product(places, [stay(raw_grad)], [weight], product, width, size)


def mix_out(places, mixed, weights):
    eight, four, rows, _ = weights.shape
    features = mixed.shape[1]
    tile = ATTN_TILE

    def product(lefts, w):
        return dot_nn(lefts[0], w[:, 0].reshape(features, tile))

    weight = (weights, (eight, 1, rows, tile), lambda j: (0, j, 0, 0))
    return chip_product(places, [stay(mixed)], [weight], product, four * tile, tile)


def mix_out_back(attn_grad, weights):
    length, width = attn_grad.shape
    eight, four, rows, _ = weights.shape
    tile = ATTN_TILE
    features = eight * rows
    part = min(length, 256)

    def kernel(a, w, out):
        total = jnp.zeros(out.shape, FULL)
        for k in range(four):
            right = w[:, k].reshape(features, tile)
            total += dot_nt(a[:, k * tile : (k + 1) * tile], right)
        out[...] = total.astype(LOW)

    return call(
        kernel,
        (length // part,),
        [
            (attn_grad, (part, width), lambda j: (j, 0)),
            (weights, (eight, four, rows, tile), lambda j: (0, 0, 0, 0)),
        ],
        [((length, features), LOW, (part, features), lambda j: (j, 0))],
    )


def gated(mlp_in, weights, waits):
    length = mlp_in.shape[0]
    eight, _, four, rows, count = weights.shape
    tile = min(count, 512)

    def kernel(a, gate_w, up_w, hidden, gate, up):
        both = []
        for w in (gate_w, up_w):
            total = jnp.zeros(gate.shape, FULL)
            for columns, pieces, k in feature_blocks(eight // 8, rows):
                total += dot_nn(a[:, columns], w[pieces, 0, k].reshape(8 * rows, tile))
            both.append(total)
        gate[...], up[...] = both
        hidden[...] = (both[0] * jax.nn.sigmoid(both[0]) * both[1]).astype(LOW)

    weight = lambda i: (
        weights, (eight, 1, four, rows, tile), lambda j: (0, i, 0, 0, j),
    )
    cut = ((length, tile), lambda j: (0, j))
    shape = (length, count)
    return call(
        kernel,
        (count // tile,),
        [stay(mlp_in), weight(0), weight(1)],
        [(shape, LOW) + cut, (shape, FULL) + cut, (shape, FULL) + cut],
        waits,
    )


def branch_out(places, hidden, weights):
    units = hidden.shape[1]
    eight, _, four, rows, width = weights.shape
    tile = min(width, 512)

    def product(lefts, w):
        return dot_nn(lefts[0], w[:, 0].reshape(units, tile))

    weight = (weights, (eight, 1, four, rows, tile), lambda j: (0, 2, 0, 0, j))
    return chip_product(places, [stay(hidden)], [weight], product, width, tile)


def gated_back(branch_rows, weights, gate_raw, up_raw):
    length, units = gate_raw.shape
    eight, _, four, rows, width = weights.shape
    tile = min(units, 512)
    pieces = tile // (four * rows)

    def kernel(a, w, gate, up, out):
        hidden_grad = dot_nt(a[...], w[:, 0].reshape(tile, width))
        raw = gate[...]
        sigmoid = jax.nn.sigmoid(raw)
        slope = sigmoid * (1.0 + raw * (1.0 - sigmoid))
        out[0] = (hidden_grad * up[...] * slope).astype(LOW)
        out[1] = (hidden_grad * raw * sigmoid).astype(LOW)

    cut = ((length, tile), lambda j: (0, j))
    return call(
        kernel,
        (units // tile,),
        [
            stay(branch_rows),
            (weights, (pieces, 1, four, rows, width), lambda j: (j, 2, 0, 0, 0)),
            (gate_raw,) + cut,
            (up_raw,) + cut,
        ],
        [((2, length, units), LOW, (2, length, tile), lambda j: (0, 0, j))],
    )


def input_back(places, grads, weights):
    _, length, units = grads.shape
    eight, _, four, rows, _ = weights.shape
    size = 8 * rows

    def product(lefts, gate_w, up_w):
        gate = dot_nt(lefts[0], gate_w[:, 0, 0].reshape(size, units))
        return gate + dot_nt(lefts[1], up_w[:, 0, 0].reshape(size, units))

    left = lambda i: (grads, (None, length, units), lambda j: (i, 0, 0))
    weight = lambda i: (
        weights, (8, 1, 1, rows, units), lambda j: (j // 4, i, j % 4, 0, 0),
    )
    width = eight // 8 * four * size
    return chip_product(
        places, [left(0), left(1)], [weight(0), weight(1)], product, width, size
    )


def down_grad(core, hidden, branch_rows, groups, rows):
    length, units = hidden[0].shape
    width = branch_rows[0].shape[1]
    run = 4 * rows
    many = 1 if run % 128 == 0 else 4
    shape = (4, groups, run, width)

    def kernel(core, a, b, c, d, out):
        total = dot_tn(a[...], b[...]) + dot_tn(c[...], d[...])
        out[...] = total.astype(LOW).reshape(out.shape)

    cut = pl.BlockSpec(
        (length, many * run), lambda g, j, core: (0, (g * 2 + core[0]) * (4 // many) + j)
    )
    whole = pl.BlockSpec((length, width), lambda g, j, core: (0, 0))
    return pl.pallas_call(
        kernel,
        grid_spec=pltpu.PrefetchScalarGridSpec(
            num_scalar_prefetch=1,
            grid=(groups, 4 // many),
            in_specs=[cut, whole, cut, whole],
            out_specs=pl.BlockSpec((many, 1, run, width), lambda g, j, core: (j, g, 0, 0)),
        ),
        out_shape=jax.ShapeDtypeStruct(shape, LOW),
        compiler_params=pltpu.CompilerParams(vmem_limit_bytes=VMEM_LIMIT),
        cost_estimate=pl.CostEstimate(flops=2**33, bytes_accessed=0, transcendentals=0),
    )(core, hidden[0], branch_rows[0], hidden[1], branch_rows[1])


def lay_features(total, out, many, rows):
    for i in range(many):
        for j in range(4):
            start = (i * 4 + j) * rows
            yield (j, i), total[start : start + rows]


def units_grad(mlp_in, grads, groups, rows):
    length = mlp_in[0].shape[0]
    units = grads[0].shape[2]
    run = 4 * rows
    many = 1 if run % 128 == 0 else 4
    shape = (4, 2, groups, 4, rows, units)

    def kernel(a, b, c, d, out):
        total = (dot_tn(a[...], b[0]) + dot_tn(c[...], d[0])).astype(LOW)
        for (j, i), part in lay_features(total, out, many, rows):
            out[j, 0, 0, i] = part

    cut = ((length, many * run), lambda i, g, j: (0, g * (4 // many) + j))
    right = ((1, length, units), lambda i, g, j: (i, 0, 0))
    return call(
        kernel,
        (2, groups, 4 // many),
        [
            (mlp_in[0],) + cut,
            (grads[0],) + right,
            (mlp_in[1],) + cut,
            (grads[1],) + right,
        ],
        [
            (
                shape,
                LOW,
                (4, 1, 1, many, rows, units),
                lambda i, g, j: (0, i, g, j, 0, 0),
            )
        ],
    )


def attention_grad(all_in, raw_grad, mixed, attn_grad, groups, rows, waits):
    length = all_in[0].shape[0]
    tile = ATTN_TILE
    run = 4 * rows
    many = 1 if run % 128 == 0 else 4
    shape = (4, groups, 4, rows, 4 * tile)

    def kernel(a, b, c, d, e, f, p, q, out):
        total = (dot_tn(a[...], b[...]) + dot_tn(c[...], d[...])).astype(LOW)
        for (j, i), part in lay_features(total, out, many, rows):
            out[j, 0, i, :, tile:] = part
        total = (dot_tn(e[0], f[...]) + dot_tn(p[0], q[...])).astype(LOW)
        for i in range(many):
            for j in range(4):
                part = total[j * rows : (j + 1) * rows, i * tile : (i + 1) * tile]
                out[j, 0, i, :, :tile] = part

    cut = ((length, many * run), lambda g, j: (0, g * (4 // many) + j))
    left = ((1, length, run), lambda g, j: (g, 0, 0))
    right = ((length, many * tile), lambda g, j: (0, j))
    return call(
        kernel,
        (groups, 4 // many),
        [
            (all_in[0],) + cut,
            stay(raw_grad[0]),
            (all_in[1],) + cut,
            stay(raw_grad[1]),
            (mixed[0],) + left,
            (attn_grad[0],) + right,
            (mixed[1],) + left,
            (attn_grad[1],) + right,
        ],
        [(shape, LOW, (4, 1, many, rows, 4 * tile), lambda g, j: (0, g, j, 0, 0))],
        waits,
    )


def wide(value):
    return value.astype(FULL)


def tie(values, others):
    if not others:
        return tuple(values)
    return lax.optimization_barrier(tuple(values) + tuple(others))[: len(values)]


def two_halves(first, second, waits):
    half = (first.shape[0] // 2,) + first.shape[1:]

    def kernel(a, b, a_out, b_out):
        a_out[...] = a[...]
        b_out[...] = b[...]

    out = (half, first.dtype, half, lambda i: (0, 0, 0))
    return call(
        kernel,
        (1,),
        [(first, half, lambda i: (0, 0, 0)), (second, half, lambda i: (1, 0, 0))],
        [out, out],
        waits,
        work=0,
    )


def hold(value, *others):
    def kernel(a, out):
        out[...] = a[...]

    shape = value.shape
    whole = (shape, lambda i: (0,) * len(shape))
    return call(kernel, (1,), [(value,) + whole], [(shape, value.dtype) + whole], others, work=0)


class Steps:
    def __init__(self):
        self.last = ()

    def wait(self, *values):
        self.last += tuple(jax.tree.leaves(values))

    def __call__(self, step, *inputs):
        flat, tree = jax.tree.flatten(inputs)
        out = step(*tree.unflatten(tie(flat, self.last)))
        self.last = tuple(jax.tree.leaves(out))
        return out


class Links:
    def __init__(self, steps):
        self.steps = steps

    def send(self, value, axes, pairs):
        (value,) = tie((value,), self.steps.last)
        return lax.ppermute(value, axes, pairs)

    def swap(self, value, axis):
        return self.send(value, axis, SWAP)

    def swap_both(self, value, first, second):
        return self.send(value, (first, second), BOTH)


def swap(value, axis):
    return lax.ppermute(value, axis, SWAP)


def pick(value, places):
    starts = [0] * value.ndim
    sizes = list(value.shape)
    for dim, place in places.items():
        starts[dim] = place
        sizes[dim] = 1
    taken = lax.dynamic_slice(value, starts, sizes)
    return taken.reshape([s for d, s in enumerate(value.shape) if d not in places])


def put(out, parts):
    for value, starts in parts:
        out = lax.dynamic_update_slice(out, value, starts)
    return out


class Place:
    def __init__(self):
        self.g, self.e, self.x, self.c, self.h, self.l = (lax.axis_index(a) for a in AXES)
        self.groups = lax.axis_size("g")
        self.steps = Steps()
        self.links = Links(self.steps)


class Spread:
    def __init__(self, at, part, inputs, first="e", second="x"):
        self.at, self.places = at, (getattr(at, first), getattr(at, second))
        a, b = self.places

        def start(*inputs):
            return tuple(part(i, j, *inputs) for i in (a, 1 - a) for j in (b, 1 - b))

        self.mine, for_b, for_a, far = at.steps(start, *inputs)
        self.from_a = at.links.swap(for_a, first)
        self.from_b = at.links.swap(for_b, second)
        self.far = at.links.swap_both(far, first, second)
        self.sent = (self.mine, for_b, for_a, far)
        self.came = (self.from_a, self.from_b, self.far)

    def second(self, lay):
        a, b = self.places

        def join(mine, from_a, from_b, far):
            return lay(
                [(mine, a, b), (from_a, 1 - a, b), (from_b, a, 1 - b), (far, 1 - a, 1 - b)]
            )

        return self.at.steps(join, self.mine, self.from_a, self.from_b, self.far)


def one_of(i, j, parts):
    return pick(parts, {0: i, 1: j})


def lay_all(parts):
    shape = parts[0][0].shape
    out = jnp.zeros((2, 2) + shape, parts[0][0].dtype)
    tail = (0,) * len(shape)
    return put(out, [(v.reshape((1, 1) + shape), (i, j) + tail) for v, i, j in parts])


class TokensIn:
    def __init__(self, at, rows):
        self.at = at
        self.spread = Spread(at, one_of, [rows.reshape(2, 2, -1, rows.shape[1])])

    def second(self):
        self.spread = Spread(self.at, one_of, [self.spread.second(lay_all)], "h", "l")

    def third(self):
        def lay(parts):
            out = lay_all(parts)
            return out.reshape((4,) + out.shape[2:])

        return self.spread.second(lay)


class TokensOut:
    def __init__(self, at, blocks):
        self.at = at
        blocks = blocks.reshape((2, 2) + blocks.shape[1:])
        self.spread = Spread(at, one_of, [blocks], "h", "l")

    def second(self):
        self.spread = Spread(self.at, one_of, [self.spread.second(lay_all)])

    def third(self):
        def lay(parts):
            out = lay_all(parts)
            return out.reshape(-1, out.shape[-1])

        return self.spread.second(lay)


class GatherTokens:
    def __init__(self, at, blocks):
        self.at, self.blocks = at, blocks
        self.from_e = at.links.swap(blocks, "e")
        self.from_x = at.links.swap(blocks, "x")

    def second(self, waits=()):
        at = self.at
        half_e, half_x = at.steps(two_halves, self.from_e, self.from_x, waits)
        self.far_0 = at.links.swap(half_e, "x")
        self.far_1 = at.links.swap(half_x, "e")
        four, count, width = self.blocks.shape
        cut = (four, 1, 1, count, width)

        def near(blocks, from_x, from_e):
            out = jnp.zeros((four, 2, 2, count, width), blocks.dtype)
            parts = [
                (blocks.reshape(cut), (0, at.e, at.x, 0, 0)),
                (from_x.reshape(cut), (0, at.e, 1 - at.x, 0, 0)),
                (from_e.reshape(cut), (0, 1 - at.e, at.x, 0, 0)),
            ]
            return put(out, parts)

        self.out = at.steps(near, self.blocks, self.from_x, self.from_e)

    def third(self):
        at = self.at
        four, count, width = self.blocks.shape
        cut = (2, 1, 1, count, width)

        def far(out, far_0, far_1):
            parts = [
                (far_0.reshape(cut), (0, 1 - at.e, 1 - at.x, 0, 0)),
                (far_1.reshape(cut), (2, 1 - at.e, 1 - at.x, 0, 0)),
            ]
            return put(out, parts).reshape(-1, width)

        return at.steps(far, self.out, self.far_0, self.far_1)


class ScatterTokens:
    def __init__(self, at, product, *inputs):
        self.at = at
        far_0, far_1, self.for_e, self.for_x, self.mine = at.steps(product, *inputs)
        self.for_e_0 = at.links.swap(far_0, "x")
        self.for_x_1 = at.links.swap(far_1, "e")

    def second(self):
        at = self.at

        def add(for_e, for_x, for_e_0, for_x_1):
            for_e_0 = (wide(for_e[:2]) + wide(for_e_0)).astype(LOW)
            for_x_1 = (wide(for_x[2:]) + wide(for_x_1)).astype(LOW)
            return jnp.concatenate([for_e_0, for_e[2:]]), jnp.concatenate([for_x[:2], for_x_1])

        for_e, for_x = at.steps(add, self.for_e, self.for_x, self.for_e_0, self.for_x_1)
        self.from_e = at.links.swap(for_e, "e")
        self.from_x = at.links.swap(for_x, "x")

    def third(self, step, *inputs):
        def add(mine, from_e, from_x, *inputs):
            return step(wide(mine) + wide(from_e) + wide(from_x), *inputs)

        return self.at.steps(add, self.mine, self.from_e, self.from_x, *inputs)


def sum_chips(value):
    far = lax.ppermute(value, ("e", "x"), BOTH)
    return value + swap(value, "x") + swap(value, "e") + far


def gather(at, piece, *others):
    (piece,) = tie((piece,), at.steps.last + others)
    return lax.all_gather(piece, ("g", "c", "h", "l"), axis=0)


def scatter(at, value, *others):
    (value,) = tie((value,), at.steps.last + others)
    value = lax.psum_scatter(value, ("h", "l"), scatter_dimension=0)
    return value


def scatter_groups(at, value, dim):
    if at.groups == 1:
        return value.reshape([n for d, n in enumerate(value.shape) if d != dim])
    return lax.psum_scatter(value, "g", scatter_dimension=dim)


def halves(value, core, runs):
    rows, count = value.shape
    each = count // (2 * runs)

    def of(place):
        parts = [
            lax.dynamic_slice(value, (0, (2 * k + place) * each), (rows, each))
            for k in range(runs)
        ]
        return jnp.concatenate(parts, axis=1)

    return of(core), of(1 - core)


class ScatterGains:
    def __init__(self, at, grads):
        self.at = at
        value = grads.reshape(grads.shape[0], at.groups, 2, 2, 2, 2, 2, -1)
        if at.groups > 1:
            value = lax.psum_scatter(value, "g", scatter_dimension=1, tiled=True)
        self.value = value.reshape(value.shape[:1] + value.shape[2:])
        self.axes = ["e", "x", "c", "h", "l"]
        self.start()

    def start(self):
        place = getattr(self.at, self.axes[0])
        self.kept, send = self.at.steps(
            lambda v: (pick(v, {1: place}), pick(v, {1: 1 - place})), self.value
        )
        self.got = self.at.links.swap(send, self.axes.pop(0))

    def more(self, waits=()):
        self.value = self.at.steps(lambda a, b: a + b, self.kept, self.got)
        if waits:
            self.value = hold(self.value, *waits)
        if self.axes:
            self.start()
        return self.value


def rope_tables(places, head_dim):
    half_dim = head_dim // 2
    inverse = jnp.power(
        jnp.float32(ROPE_THETA), -(jnp.arange(half_dim, dtype=FULL) * 2.0 / head_dim)
    )
    angles = places.astype(FULL)[:, None] * inverse[None, :]
    sine = jnp.sin(angles)
    cosine = jnp.cos(angles)
    return (
        jnp.concatenate([cosine, cosine], axis=-1),
        jnp.concatenate([-sine, sine], axis=-1),
    )


def norm_forward(tensor, gain_vec):
    inverse = lax.rsqrt(jnp.mean(tensor * tensor, axis=-1, keepdims=True) + EPSILON)
    unit = tensor * inverse
    return unit * gain_vec, unit, inverse


def norm_backward(grad_in, unit, inverse, gain_vec):
    axes = tuple(range(grad_in.ndim - 1))
    gain_grad = jnp.sum(grad_in * unit, axis=axes)
    unit_grad = grad_in * gain_vec
    inner = jnp.mean(unit_grad * unit, axis=-1, keepdims=True)
    return inverse * (unit_grad - unit * inner), gain_grad


def on_device(
    hidden_in,
    q_weight,
    k_weight,
    v_weight,
    o_weight,
    q_gain,
    k_gain,
    attn_gain,
    gate_weight,
    up_weight,
    down_weight,
    mlp_gain,
    out_grad,
):
    at = Place()
    steps = at.steps
    batch, rows_here, width = hidden_in.shape
    head_dim = width // HEADS
    length = batch * rows_here * 4
    rows_owned = q_weight.shape[0]
    groups = at.groups
    ff_block = down_weight.shape[0]

    assert head_dim % (8 * rows_owned) == 0 or (8 * rows_owned) % head_dim == 0
    assert ff_block == 4 * rows_owned

    def columns_of(e, x, weight):
        rows, count = weight.shape
        part = count // (4 * groups)
        each = [
            lax.dynamic_slice(weight, (0, ((g * 2 + e) * 2 + x) * part), (rows, part))
            for g in range(groups)
        ]
        return jnp.concatenate(each, axis=1)

    def lay_columns(parts):
        rows, count = parts[0][0].shape
        part = count // groups
        out = jnp.zeros((rows, 4 * count), FULL)
        for value, e, x in parts:
            for g in range(groups):
                piece = wide(value[:, g * part : (g + 1) * part])
                out = lax.dynamic_update_slice(out, piece, (0, ((g * 2 + e) * 2 + x) * part))
        return out

    quarter = width // 4

    def columns_of_attention(e, x, q, k, v, o, gains):
        three = [columns_of(e, x, w) for w in (q, k, v)]
        return jnp.concatenate(three + [gains], axis=1)

    def lay_attention(parts):
        tail = lay_all(parts)
        tail = tail.reshape((4,) + tail.shape[2:])
        runs = jnp.stack([o_weight[:, k * quarter : (k + 1) * quarter] for k in range(4)])
        return jnp.concatenate([runs, tail], axis=2)

    def lay_four(parts):
        out = lay_all(parts)
        return out.reshape((4,) + out.shape[2:])

    def lay_three(parts):
        return tuple(
            lay_columns([(v[:, i * quarter : (i + 1) * quarter], e, x) for v, e, x in parts])
            for i in range(3)
        )

    places = jnp.stack([at.e, at.x]).astype(jnp.int32)

    def here(vector):
        return pick(vector.reshape(groups, 2, 2, -1), {1: at.e, 2: at.x}).reshape(1, -1)

    def whole(vector):
        out = jnp.zeros((groups, 2, 2, vector.size // groups), FULL)
        part = vector.reshape(groups, 1, 1, -1)
        return lax.dynamic_update_slice(out, part, (0, at.e, at.x, 0)).reshape(-1)

    def pair(halved, core_sent):
        return halved, at.links.swap(core_sent, "c")

    gains = jnp.stack([q_gain, k_gain, attn_gain, mlp_gain], axis=1)
    gains = jnp.pad(gains, ((0, 0), (0, 124)))
    attn_spread = Spread(
        at, columns_of_attention, [q_weight, k_weight, v_weight, o_weight, gains]
    )
    own = TokensIn(at, hidden_in.reshape(-1, width))
    gate_spread = Spread(at, columns_of, [gate_weight])
    up_spread = Spread(at, columns_of, [up_weight])
    attn_all = gather(at, attn_spread.second(lay_attention))
    own.second()
    cosine, sine = steps(lambda n: rope_tables(n, head_dim), jnp.arange(length))
    gate_mine = gate_spread.second(lay_four)
    up_mine = up_spread.second(lay_four)
    mlp_mine = steps(
        lambda *v: jnp.stack(v), gate_mine, up_mine, down_weight.reshape((4, -1, width))
    )
    mlp_all = gather(at, mlp_mine)
    own_in = own.third()
    all_in = GatherTokens(at, own_in)
    all_in.second()
    all_in = all_in.third()
    all_in_half = pair(*steps(lambda v: halves(v, at.c, 4 * groups), all_in))
    top = TokensIn(at, out_grad.reshape(-1, width))
    steps.wait(all_in_half)

    def gains_of(weights):
        value = wide(weights[..., -128:-124]).reshape(groups, 8, 4, rows_owned, 4)
        return value.transpose(4, 0, 2, 1, 3).reshape(4, -1)

    gains = steps(gains_of, attn_all)
    q_gain_here, k_gain_here = here(gains[0]), here(gains[1])
    attn_gain_all, mlp_gain_all = gains[2], gains[3]

    def squares_of(raw):
        q_raw, k_raw = jnp.split(raw[:, : 2 * quarter], 2, axis=1)
        return jnp.stack([jnp.sum(q_raw * q_raw, -1), jnp.sum(k_raw * k_raw, -1)])

    raw = steps(project, all_in, attn_all)
    squares = sum_chips(steps(squares_of, raw))
    inverse = steps(lambda s: lax.rsqrt(s / width + EPSILON).T, squares)
    queries, keys, values, mixed = steps(
        attend, raw, inverse, q_gain_here, k_gain_here, cosine, sine
    )
    attn_out = ScatterTokens(at, mix_out, places, mixed, attn_all)

    def halve_mixed(mixed):
        return [
            v.reshape(length, groups, -1).swapaxes(0, 1) for v in halves(mixed, at.c, groups)
        ]

    mixed_half = pair(*steps(halve_mixed, mixed))
    steps.wait(mixed_half)
    attn_out.second()

    def after_attention(attn_out, own_in, gain):
        normed, unit, inverse = norm_forward(attn_out, gain)
        residual = wide(own_in) + normed
        return residual.astype(LOW), residual, unit, inverse

    residual_low, residual, attn_unit, attn_inverse = attn_out.third(
        after_attention, own_in, attn_gain_all
    )

    mlp_in = GatherTokens(at, residual_low)
    mlp_in.second()
    mlp_in = mlp_in.third()
    mlp_in_half = pair(*steps(lambda v: halves(v, at.c, 4 * groups), mlp_in))
    steps.wait(mlp_in_half)
    hidden, gate_raw, up_raw = steps(gated, mlp_in, mlp_all, top.spread.came)
    top.second()
    branch = ScatterTokens(at, branch_out, places, hidden, mlp_all)
    hidden = (hidden, at.links.swap(hidden, "c"))
    branch.second()
    own_top = top.third()

    def after_mlp(branch, residual, own_top, gain):
        normed, unit, inverse = norm_forward(branch, gain)
        grad, gain_grad = norm_backward(wide(own_top), unit, inverse, gain)
        return grad.astype(LOW), (residual + normed).astype(LOW), gain_grad

    branch_low, own_out, mlp_gain_grad = branch.third(
        after_mlp, residual, own_top, mlp_gain_all
    )

    branch_rows = GatherTokens(at, branch_low)
    layer_out = TokensOut(at, own_out)
    branch_rows.second(layer_out.spread.came)
    branch_rows = branch_rows.third()
    branch_rows = (branch_rows, at.links.swap(branch_rows, "c"))
    unit_grads = steps(gated_back, branch_rows[0], mlp_all, gate_raw, up_raw)
    unit_grads = (unit_grads, at.links.swap(unit_grads, "c"))
    core = at.c.astype(jnp.int32).reshape(1)
    grad = steps(
        lambda *v: down_grad(*v, groups, rows_owned), core, hidden, branch_rows
    )
    down_own = scatter(at, grad)
    grad = steps(lambda a, b: units_grad(a, b, groups, rows_owned), mlp_in_half, unit_grads)
    units_own = scatter(at, grad)
    input_part = ScatterTokens(at, input_back, places, unit_grads[0], mlp_all)
    input_part.second()
    layer_out.second()
    layer_out_came = layer_out.spread.came

    def before_attention(input_grad, own_top, unit, inverse, gain):
        residual_grad = wide(own_top) + input_grad
        grad, gain_grad = norm_backward(residual_grad, unit, inverse, gain)
        return grad.astype(LOW), residual_grad, gain_grad

    attn_grad, residual_grad, attn_gain_grad = input_part.third(
        before_attention, own_top, attn_unit, attn_inverse, attn_gain_all
    )

    attn_low = GatherTokens(at, attn_grad)
    layer_out = layer_out.third()
    attn_low.second()
    attn_low = attn_low.third()
    attn_low = (attn_low, swap(attn_low, "c"))
    mixed_grad = steps(mix_out_back, attn_low[0], attn_all)
    q_scaled, k_scaled, v_low, inner, q_gain_grad, k_gain_grad = steps(
        attend_back, queries, keys, values, mixed_grad, raw, inverse,
        q_gain_here, k_gain_here, cosine, sine, (down_own,) + layer_out_came,
    )
    inner = sum_chips(steps(lambda v: v.T / width, inner))

    def before_project(raw, inverse, q_scaled, k_scaled, v_low, inner):
        q_raw, k_raw = jnp.split(raw[:, : 2 * quarter], 2, axis=1)
        inner = inner.T
        grads = []
        for i, (part, scaled) in enumerate([(q_raw, q_scaled), (k_raw, k_scaled)]):
            each = inverse[:, i : i + 1]
            grads.append((each * (scaled - part * each * inner[:, i : i + 1])).astype(LOW))
        return jnp.concatenate(grads + [v_low], axis=1)

    raw_grad = steps(before_project, raw, inverse, q_scaled, k_scaled, v_low, inner)
    raw_grad = (raw_grad, swap(raw_grad, "c"))
    in_part = ScatterTokens(at, project_back, places, raw_grad[0], attn_all)
    attn_grad_part = steps(
        lambda *v: attention_grad(*v[:-1], groups, rows_owned, v[-1:]),
        all_in_half, raw_grad, mixed_half, attn_low, units_own,
    )
    attn_own = scatter(at, attn_grad_part)
    in_part.second()
    gains = jnp.stack([whole(q_gain_grad), whole(k_gain_grad), attn_gain_grad, mlp_gain_grad])
    gains = ScatterGains(at, gains)
    in_grad = in_part.third(lambda a, b: (a + b).astype(LOW), residual_grad)
    in_grad = TokensOut(at, in_grad)
    gains.more()
    gains.more()
    units_own = scatter_groups(at, units_own, 1)
    gate_spread = Spread(at, one_of, [units_own[0].reshape(2, 2, rows_owned, -1)])
    up_spread = Spread(at, one_of, [units_own[1].reshape(2, 2, rows_owned, -1)])
    gate_own = gate_spread.second(lay_columns)
    up_own = up_spread.second(lay_columns)
    in_grad.second()
    attn_own = scatter_groups(at, attn_own, 0)
    attn_spread = Spread(
        at, one_of, [attn_own[..., quarter:].reshape(2, 2, rows_owned, -1)]
    )
    gains.more(attn_spread.sent)
    in_grad = in_grad.third()
    o_own = wide(jnp.concatenate([attn_own[k, :, :quarter] for k in range(4)], axis=1))
    gains.more()
    own_three = list(attn_spread.second(lay_three))
    down_own = wide(scatter_groups(at, down_own, 0))
    gains = gains.more()
    shape = hidden_in.shape
    grads = own_three + [o_own, gate_own, up_own, down_own]
    return (layer_out.reshape(shape), in_grad.reshape(shape)) + tuple(grads) + tuple(gains)


def solution(mesh):
    dp, seq = mesh.shape["dp"], mesh.shape["seq"]
    split = Mesh(mesh.devices.reshape(dp // 8, 2, 2, 2, seq // 2, 2), AXES)
    dp_axes, seq_axes = AXES[:4], AXES[4:]
    tokens = P(dp_axes, seq_axes, None)
    matrix, vector = P(AXES, None), P(AXES)
    return jax.shard_map(
        on_device,
        mesh=split,
        in_specs=(tokens,)
        + (matrix,) * 4
        + (vector,) * 3
        + (matrix,) * 3
        + (vector, tokens),
        out_specs=(tokens,) * 2 + (matrix,) * 7 + (vector,) * 4,
        check_vma=False,
    )
```
